32 devices in a mesh: groups: 2 (over y), ep: 4 (over z), hd: 4 (over x, core).
Axes of the slice: x: 2, y: 2, z: 4, core: 2. Of those that a mesh axis runs over, the one named last changes fastest.
Arguments:
- residual: bfloat16 [64, 4096], P(('groups', 'ep'), 'hd'), parts along dimension 0, may hold values from -13 to 13
- queries: bfloat16 [64, 8192], P(('groups', 'ep'), 'hd'), parts along dimension 0, may hold values from -90 to 90
- key_value_cache: bfloat16 [64, 256, 2, 512], P(('groups', 'ep'), None, None, 'hd'), parts along dimension 0, may hold values from -4.5 to 4.5
- lengths: int32 [64], P(('groups', 'ep')), parts along dimension 0, may hold values from 2 to 256, as said below
- slot_of: int32 [64], P('groups'), parts along dimension 0, may hold values from 0 to 31, each once
- out_weight: bfloat16 [8192, 4096], P('hd', 'ep'), may hold values from -0.5 to 0.5
- expert_ids: int32 [64, 8], P(('groups', 'ep')), parts along dimension 0, may hold values from 0 to 63, all different within a row; in each aligned block of 8 rows (0 to 7, 8 to 15, ...) at most 2 rows name the same one
- route_weight: float32 [64, 8], P(('groups', 'ep')), parts along dimension 0, may hold values from 0.05 to 0.3
- in_weight: bfloat16 [64, 4096, 768], P('ep', None, 'hd'), may hold values from -0.09375 to 0.09375
- down_weight: bfloat16 [64, 768, 4096], P('ep', 'hd'), may hold values from -0.21875 to 0.21875
Outputs:
- layer_out: bfloat16 [64, 4096], P(('groups', 'ep'), 'hd'), parts along dimension 0
The draws below stay inside these ranges and needn't reach their ends.
There are 2 independent parts, one for each index of `groups`. The reference program is written for one: setup_inputs(seed, part) draws one part's arguments, and reference() takes and returns one part's arrays. A program takes and returns all parts, laid end to end along the dimension named above; an argument that names none is the same for every part. Nothing has to cross between parts.
Inputs may be any that keep to these rules, and one draw needn't show every extreme that they name: `expert_ids`: among the rows of one device, at most 2 name the same expert; some expert is named by exactly 2 of them. A permutation: request r's cache sits in slot slot_of[r]. Slot s's cache is filled in its first lengths[s] positions; some slot is full.
All inputs are finite; a program needn't handle non-finite values.
Results may differ from the reference program's by a relative error of at most 0.0043.
The reference program's roundings to bfloat16 on the way count: a program that leaves them out, or rounds other values in their place, can miss the bound.
Values may be sent and summed in bfloat16 or wider, within the bound.
No kernel may reach another device: no remote copies, remote signals or barrier semaphores. Data moves between devices by JAX's collectives and lax.ppermute only.
A program may use at most 128 MiB of HBM per device.

```python
import math
import jax
import jax.numpy as jnp
import numpy as np
from jax import lax

D = 4096
QUERY_HEADS = 64
KEY_VALUE_HEADS = 4
HEAD_SIZE = 128
FF = 768
EXPERTS = 64
TOPK = 8
CAP = 2
CACHE_LENGTH = 256
ROWS_DEV = 8
REQUEST_COUNT = 32


def draw_queries(key, part):
    key = jax.random.fold_in(key, 11)
    first_result = jax.random.fold_in(key, 0)
    heads_per_group = QUERY_HEADS // KEY_VALUE_HEADS
    start_offset = jnp.clip(jax.random.normal(first_result, (REQUEST_COUNT, KEY_VALUE_HEADS, heads_per_group, HEAD_SIZE), jnp.float32), -4.5, 4.5)
    return start_offset.reshape(REQUEST_COUNT, QUERY_HEADS * HEAD_SIZE).astype(jnp.bfloat16)


def draw_key_value_cache(key, part):
    key = jax.random.fold_in(key, 7)
    start_offset = jnp.clip(jax.random.normal(key, (REQUEST_COUNT, CACHE_LENGTH, 2, KEY_VALUE_HEADS, HEAD_SIZE), jnp.float32), -4.5, 4.5)
    return start_offset.reshape(REQUEST_COUNT, CACHE_LENGTH, 2, KEY_VALUE_HEADS * HEAD_SIZE).astype(jnp.bfloat16)


def draw_lengths(key, part):
    key = jax.random.fold_in(key, 5)
    first_result, second_result, third_result = jax.random.split(key, 3)
    left = jax.random.randint(first_result, (REQUEST_COUNT,), 0, CACHE_LENGTH - 1)
    right = jax.random.randint(second_result, (REQUEST_COUNT,), 0, CACHE_LENGTH - 1)
    values = 2 + left * right // (CACHE_LENGTH - 2)
    picked = jax.random.randint(third_result, (), 0, REQUEST_COUNT)
    values = values.at[picked].set(CACHE_LENGTH)
    return values.astype(jnp.int32)


def draw_residual(key, part):
    key = jax.random.fold_in(key, 3)
    first_result, second_result, third_result = jax.random.split(key, 3)
    start_offset = 0.5 * jnp.clip(jax.random.normal(first_result, (REQUEST_COUNT, D), jnp.float32), -4.0, 4.0)
    lower = 0.4
    upper = 2.5
    row_scale = jnp.exp(jax.random.uniform(second_result, (REQUEST_COUNT, 1), jnp.float32, math.log(lower), math.log(upper)))
    column_scale = jnp.exp(jax.random.uniform(third_result, (1, D), jnp.float32, math.log(lower), math.log(upper)))
    return (start_offset * row_scale * column_scale).astype(jnp.bfloat16)


def block_levels(own_key, dims, pieces, least, high):
    def one(position, parts):
        heights = jax.random.uniform(jax.random.fold_in(jax.random.fold_in(own_key, 6), position), (parts,), jnp.float32, least / len(pieces), high / len(pieces))
        return jnp.repeat(jnp.exp(heights), dims[position] // parts).reshape((-1,) + (1,) * (len(dims) - position - 1))

    factor_of = one(*pieces[0])
    for cut in pieces[1:]:
        factor_of = factor_of * one(*cut)
    return factor_of


def routed_block(own_key, own, number, rows, number_of, top, reach, lean):
    ranking = jax.random.permutation(own_key, number_of)
    crowded, ordinary = portions_of(number_of, rows * top, reach, lean, True), portions_of(number_of, rows * top, reach, lean, False)
    places = jnp.arange(number_of)

    def named(sizes, rotation):
        used = int((sizes > 0).sum())
        fixed = max(1, used // 4)
        moved = fixed + (places - fixed + rotation * (used - fixed)) % max(1, number_of - fixed)
        return jnp.zeros((number_of,), jnp.int32).at[ranking[jnp.where(places < fixed, places, moved)]].set(jnp.asarray(sizes, jnp.int32))

    sizes = jnp.where(number % 4 == 0, named(crowded, number // 4), named(ordinary, number - number // 4 - 1))
    mixed = jax.random.permutation(jax.random.fold_in(own, 3), number_of)
    giver, taker = mixed[0:number_of // 2 * 2:2], mixed[1:number_of // 2 * 2:2]
    room = jnp.minimum(sizes[giver] - 1, reach - sizes[taker]) // 2
    room = jnp.where((giver == ranking[0]) | (taker == ranking[0]) | (sizes[taker] == 0), 0, jnp.maximum(room, 0))
    moved = jax.random.randint(jax.random.fold_in(own, 4), (number_of // 2,), 0, 1 << 20) % (room + 1)
    sizes = sizes.at[giver].add(-moved).at[taker].add(moved)
    items = jnp.searchsorted(jnp.cumsum(sizes), jnp.arange(rows * top), side="right").astype(jnp.int32)
    table = items.reshape(top, rows).T
    table = table[jax.random.permutation(jax.random.fold_in(own, 1), rows)]
    rotation = jax.random.randint(jax.random.fold_in(own, 2), (rows, 1), 0, top)
    return jnp.take_along_axis(table, (jnp.arange(top)[None, :] + rotation) % top, axis=1)


def portions_of(amount, total, reach, slope, full):
    portions = [(1 << 20) // math.isqrt(grade ** slope) + 1 for grade in range(1, amount + 1)]
    largest = reach if full else min(reach, max(-(-total // amount), total * portions[0] // sum(portions)))
    least = 1 if total - largest >= amount - 1 else 0
    holding, spare = [largest] + [least] * (amount - 1), total - largest - least * (amount - 1)
    while spare > 0:
        movable = [i for i in range(1, amount) if holding[i] < largest] or [i for i in range(1, amount) if holding[i] < reach]
        mass, remaining = sum([portions[i] for i in movable]), spare
        for i in movable:
            addition = min(reach - holding[i], max(1, remaining * portions[i] // mass), spare)
            holding[i] = holding[i] + addition
            spare = spare - addition
    return np.array(holding)


def gaussian(stream_key, extent, width, most, shards=(), held_as=jnp.bfloat16):
    result = width * jax.random.normal(stream_key, extent, jnp.float32)
    if shards:
        result = result * block_levels(stream_key, extent, shards, -0.22, 0.18)
    return jnp.clip(result, -most, most).astype(held_as)


def setup_inputs(seed: int = 0, part: int = 0) -> dict:
    arg_keys = jax.random.split(jax.random.key(seed), 11)
    part_splits = jax.random.split(jax.random.fold_in(arg_keys[10], part), 11)
    residual = draw_residual(jax.random.fold_in(jax.random.fold_in(arg_keys[10], part), 71), part)
    queries = draw_queries(jax.random.fold_in(jax.random.fold_in(arg_keys[10], part), 71), part)
    key_value_cache = draw_key_value_cache(jax.random.fold_in(jax.random.fold_in(arg_keys[10], part), 71), part)
    lengths = draw_lengths(jax.random.fold_in(jax.random.fold_in(arg_keys[10], part), 71), part)
    slot_of = jax.random.permutation(part_splits[4], REQUEST_COUNT).astype(jnp.int32)
    out_weight = gaussian(arg_keys[5], (QUERY_HEADS * HEAD_SIZE, D), (max(QUERY_HEADS * HEAD_SIZE // 64, 16)) ** -0.5, 0.5, ((0, 4), (1, 4)))
    expert_ids_keys = jax.random.split(jax.random.fold_in(part_splits[6], 1), REQUEST_COUNT // ROWS_DEV)
    expert_ids_turns = jax.random.permutation(jax.random.fold_in(part_splits[6], 3), REQUEST_COUNT // ROWS_DEV)
    expert_ids = jax.vmap(lambda own, number: routed_block(jax.random.fold_in(part_splits[6], 2), own, number, ROWS_DEV, EXPERTS, TOPK, CAP, 2))(expert_ids_keys, expert_ids_turns).reshape((REQUEST_COUNT, TOPK))
    route_weight = jnp.clip(0.05 + 0.25 * jax.random.uniform(part_splits[7], (REQUEST_COUNT, TOPK), jnp.float32) ** block_levels(part_splits[7], (REQUEST_COUNT, TOPK), ((0, 4),), -0.2, 0.2), 0.05, 0.3)
    in_weight = gaussian(arg_keys[8], (EXPERTS, D, FF), D ** -0.5, 0.09375, ((0, 4), (2, 4)))
    down_weight = gaussian(arg_keys[9], (EXPERTS, FF, D), FF ** -0.5, 0.21875, ((0, 4), (1, 4)))
    return {"residual": residual, "queries": queries, "key_value_cache": key_value_cache, "lengths": lengths, "slot_of": slot_of, "out_weight": out_weight, "expert_ids": expert_ids, "route_weight": route_weight, "in_weight": in_weight, "down_weight": down_weight}


def reference(residual, queries, key_value_cache, lengths, slot_of, out_weight, expert_ids, route_weight, in_weight, down_weight):
    heads_per_group = QUERY_HEADS // KEY_VALUE_HEADS
    query_head_rows = queries.astype(jnp.float32).reshape(REQUEST_COUNT, KEY_VALUE_HEADS, heads_per_group, HEAD_SIZE)
    cached_key_rows = key_value_cache[:, :, 0].astype(jnp.float32).reshape(REQUEST_COUNT, CACHE_LENGTH, KEY_VALUE_HEADS, HEAD_SIZE)
    cached_value_rows = key_value_cache[:, :, 1].astype(jnp.float32).reshape(REQUEST_COUNT, CACHE_LENGTH, KEY_VALUE_HEADS, HEAD_SIZE)
    scores = jnp.einsum('sagd,slad->sagl', query_head_rows, cached_key_rows) * (1.0 / math.sqrt(HEAD_SIZE))
    visible = (jnp.arange(CACHE_LENGTH)[None, :] < lengths[:, None])[:, None, None, :]
    scores = jnp.where(visible, scores, -1e+30)
    highest = lax.optimization_barrier(jnp.max(scores, axis=3, keepdims=True))
    raised = jnp.where(visible, jnp.exp(scores - highest), 0.0)
    weights = (raised / lax.optimization_barrier(jnp.sum(raised, axis=3, keepdims=True))).astype(jnp.bfloat16)
    attended = jnp.einsum('sagl,slad->sagd', weights.astype(jnp.float32), cached_value_rows)
    attended = attended.astype(jnp.bfloat16).reshape(REQUEST_COUNT, QUERY_HEADS * HEAD_SIZE)
    projected = jnp.dot(attended, out_weight, preferred_element_type=jnp.float32)
    stream = residual.astype(jnp.float32) + jnp.take(projected, slot_of, axis=0)
    normed = (stream * lax.rsqrt(lax.optimization_barrier(jnp.mean(stream * stream, axis=1)) + 1e-06)[:, None]).astype(jnp.bfloat16)
    member = expert_ids[:, :, None] == jnp.arange(EXPERTS)[None, None, :]
    mixing = lax.optimization_barrier(jnp.sum(jnp.where(member, route_weight[:, :, None], 0.0), axis=1))

    def one_expert(carry, inputs):
        entry, exit_weight, column = inputs
        hidden = jax.nn.silu(jnp.dot(normed, entry, preferred_element_type=jnp.float32)).astype(jnp.bfloat16)
        output = jnp.dot(hidden, exit_weight, preferred_element_type=jnp.float32).astype(jnp.bfloat16)
        return (carry + column[:, None] * output.astype(jnp.float32), None)
    mixture, unused = lax.scan(one_expert, jnp.zeros((REQUEST_COUNT, D), jnp.float32), (in_weight, down_weight, mixing.T))
    return (stream + mixture).astype(jnp.bfloat16)
```

```python
import functools
import math

import jax
import jax.numpy as jnp
from jax import lax
from jax.experimental import pallas as pl
from jax.experimental.pallas import tpu as pltpu
from jax.sharding import PartitionSpec as P

D = 4096
QUERY_HEADS = 64
KEY_VALUE_HEADS = 4
HEAD_SIZE = 128
EXPERTS = 64
TOPK = 8
CAP = 2
CACHE_LENGTH = 256
BF16 = jnp.bfloat16
F32 = jnp.float32
MIB = 1 << 20
VMEM_SPEC = pl.BlockSpec(memory_space=pltpu.VMEM)
SMEM_SPEC = pl.BlockSpec(memory_space=pltpu.SMEM)


def swap(block, axis, k, n):
    return lax.ppermute(block, axis, [(i, i ^ k) for i in range(n)])


def attention_kernel(lengths, queries, cache, ids, route, out, staged, gathered):
    rows = queries.shape[0]
    heads = queries.shape[1] // HEAD_SIZE
    for h in range(heads):
        lanes = slice(h * HEAD_SIZE, (h + 1) * HEAD_SIZE)
        staged[h * rows : (h + 1) * rows, :] = queries[:, lanes].astype(F32)
    place = lax.broadcasted_iota(jnp.int32, (heads, 2 * CACHE_LENGTH), 1)
    for s in range(rows):
        mine = staged[pl.ds(s, heads, stride=rows), :].astype(BF16)
        both = cache[s]
        scores = lax.dot_general(
            mine, both, (((1,), (1,)), ((), ())), preferred_element_type=F32
        ) * (1.0 / math.sqrt(HEAD_SIZE))
        visible = jnp.logical_and(place % 2 == 0, place < 2 * lengths[s])
        scores = jnp.where(visible, scores, -1e30)
        raised = jnp.where(visible, jnp.exp(scores - jnp.max(scores, axis=1, keepdims=True)), 0.0)
        weights = raised / jnp.sum(raised, axis=1, keepdims=True)
        moved = pltpu.roll(weights, 1, 1).astype(BF16)
        gathered[pl.ds(s, heads, stride=rows), :] = jnp.dot(
            moved, both, preferred_element_type=F32
        )
    for h in range(heads):
        lanes = slice(h * HEAD_SIZE, (h + 1) * HEAD_SIZE)
        out[:, lanes] = gathered[h * rows : (h + 1) * rows, :].astype(BF16)
    weight = route[...]
    high = weight.astype(BF16)
    rest = weight - high.astype(F32)
    middle = rest.astype(BF16)
    low = (rest - middle.astype(F32)).astype(BF16)
    row = lax.broadcasted_iota(jnp.int32, (TOPK, 128), 0)
    lane = lax.broadcasted_iota(jnp.int32, (TOPK, 128), 1)
    total = jnp.zeros((rows, 128), F32)
    for j, part in enumerate((ids[...].astype(F32).astype(BF16), high, middle, low)):
        spread = (lane == row + j * TOPK).astype(F32).astype(BF16)
        total = total + jnp.dot(part, spread, preferred_element_type=F32)
    out[:, heads * HEAD_SIZE :] = total.astype(BF16)


def attention(lengths, queries, cache, ids, route):
    rows, width = queries.shape
    return pl.pallas_call(
        attention_kernel,
        out_shape=jax.ShapeDtypeStruct((rows, width + 128), BF16),
        in_specs=[SMEM_SPEC] + [VMEM_SPEC] * 4,
        out_specs=VMEM_SPEC,
        scratch_shapes=[
            pltpu.VMEM((rows * width // HEAD_SIZE, HEAD_SIZE), F32),
            pltpu.VMEM((rows * width // HEAD_SIZE, HEAD_SIZE), F32),
        ],
        compiler_params=pltpu.CompilerParams(vmem_limit_bytes=6 * MIB),
        cost_estimate=pl.CostEstimate(
            flops=10_000_000, bytes_accessed=1_200_000, transcendentals=65536
        ),
        name="attention",
    )(lengths, queries, cache, ids, route)


def projection_kernel(n, slot_of, b0, b1, b2, b3, weight, out, routing):
    blocks = (b0, b1, b2, b3)
    rows = b0.shape[0]
    width = b0.shape[1] - 128
    everyone = n * rows
    me = lax.axis_index("ep")
    held = jnp.concatenate([b[:, :width].astype(F32) for b in blocks], axis=0).astype(BF16)
    row = lax.broadcasted_iota(jnp.int32, (everyone, everyone), 0)
    column = lax.broadcasted_iota(jnp.int32, (everyone, everyone), 1)
    wanted = jnp.zeros((everyone, everyone), jnp.int32)
    for r in range(everyone):
        slot = slot_of[r]
        wanted = jnp.where(row == r, ((slot // rows) ^ me) * rows + slot % rows, wanted)
    order = (wanted == column).astype(F32).astype(BF16)
    ordered = jnp.dot(order, held, preferred_element_type=F32).astype(BF16)
    answer = jnp.dot(ordered, weight[...], preferred_element_type=F32)
    for i in range(n):
        out[i] = answer[i * rows : (i + 1) * rows, :]
    for k, block in enumerate(blocks):
        routing[pl.ds((me ^ k) * rows, rows), :] = block[:, width:].astype(F32)


def projection(slot_of, blocks, weight):
    n = len(blocks)
    rows = blocks[0].shape[0]
    return pl.pallas_call(
        functools.partial(projection_kernel, n),
        out_shape=(
            jax.ShapeDtypeStruct((n, rows, weight.shape[1]), F32),
            jax.ShapeDtypeStruct((n * rows, 128), F32),
        ),
        in_specs=[SMEM_SPEC] + [VMEM_SPEC] * 5,
        out_specs=(VMEM_SPEC, VMEM_SPEC),
        compiler_params=pltpu.CompilerParams(vmem_limit_bytes=8 * MIB),
        cost_estimate=pl.CostEstimate(
            flops=140_000_000, bytes_accessed=4_500_000, transcendentals=0
        ),
        name="projection",
    )(slot_of, *blocks, weight)


def norm_kernel(b0, b1, b2, b3, out):
    blocks = (b0, b1, b2, b3)
    me = lax.axis_index("ep")
    width = b0.shape[1]
    squares = 0.0
    for block in blocks:
        squares = squares + jnp.sum(block[...] * block[...], axis=1, keepdims=True)
    scale = lax.rsqrt(squares / (width * len(blocks)) + 1e-06)
    for k, block in enumerate(blocks):
        start = pl.multiple_of((me ^ k) * width, width)
        out[:, pl.ds(start, width)] = (block[...] * scale).astype(BF16)


def norm(blocks):
    rows, width = blocks[0].shape
    return pl.pallas_call(
        norm_kernel,
        out_shape=jax.ShapeDtypeStruct((rows, width * len(blocks)), BF16),
        in_specs=[VMEM_SPEC] * 4,
        out_specs=VMEM_SPEC,
        compiler_params=pltpu.CompilerParams(vmem_limit_bytes=4 * MIB),
        cost_estimate=pl.CostEstimate(flops=100_000, bytes_accessed=200_000, transcendentals=8),
        name="norm",
    )(*blocks)


def experts_kernel(rows_in, routing, entry, leave, o0, o1, o2, o3, total):
    step = pl.program_id(0)
    number = lax.axis_index("ep") * pl.num_programs(0) + step
    table = routing[...]
    lane = lax.broadcasted_iota(jnp.int32, table.shape, 1)
    weight = pltpu.roll(table, 128 - TOPK, 1) + pltpu.roll(table, 128 - 2 * TOPK, 1)
    weight = weight + pltpu.roll(table, 128 - 3 * TOPK, 1)
    chosen = jnp.logical_and(lane < TOPK, table == number.astype(F32))
    share = jnp.sum(jnp.where(chosen, weight, 0.0), axis=1, keepdims=True)
    before = lax.dot_general(
        rows_in[...], entry[0], (((1,), (1,)), ((), ())), preferred_element_type=F32
    )
    hidden = (before / (1.0 + jnp.exp(-before))).astype(BF16)
    result = jnp.dot(hidden, leave[0], preferred_element_type=F32) * share

    @pl.when(step == 0)
    def _():
        total[...] = result

    @pl.when(step > 0)
    def _():
        total[...] += result

    @pl.when(step == pl.num_programs(0) - 1)
    def _():
        me = lax.axis_index("hd")
        for k, out in enumerate((o0, o1, o2, o3)):
            width = out.shape[1]
            start = pl.multiple_of((me ^ k) * width, width)
            out[...] = total[:, pl.ds(start, width)].astype(out.dtype)


def experts(rows_in, routing, entry, leave):
    count, hidden, width = leave.shape
    rows = rows_in.shape[0]
    part = (rows, width // 4)
    whole = lambda shape: pl.BlockSpec(shape, lambda i: (0, 0))
    return pl.pallas_call(
        experts_kernel,
        grid=(count,),
        out_shape=[jax.ShapeDtypeStruct(part, F32)] + [jax.ShapeDtypeStruct(part, BF16)] * 3,
        in_specs=[
            whole((rows, width)),
            whole((rows, 128)),
            pl.BlockSpec((1, hidden, width), lambda i: (i, 0, 0)),
            pl.BlockSpec((1, hidden, width), lambda i: (i, 0, 0)),
        ],
        out_specs=[whole(part)] * 4,
        scratch_shapes=[pltpu.VMEM((rows, width), F32)],
        compiler_params=pltpu.CompilerParams(vmem_limit_bytes=24 * MIB),
        cost_estimate=pl.CostEstimate(
            flops=4 * rows * count * hidden * width,
            bytes_accessed=4 * count * hidden * width,
            transcendentals=rows * count * hidden,
        ),
        name="experts",
    )(rows_in, routing, entry, leave)


def gather_kernel(own, r1, r2, r3, o0, o1, o2, o3):
    total = own[...] + r1[...].astype(F32) + r2[...].astype(F32) + r3[...].astype(F32)
    rows = o0.shape[0]
    me = lax.axis_index("ep")
    scratch = total.reshape(4, rows, total.shape[1])
    for k, out in enumerate((o0, o1, o2, o3)):
        picked = jnp.zeros(out.shape, F32)
        for i in range(4):
            picked = jnp.where((me ^ k) == i, scratch[i], picked)
        out[...] = picked.astype(out.dtype)


def combine(own, received):
    rows, width = own.shape
    part = (rows // 4, width)
    return pl.pallas_call(
        gather_kernel,
        out_shape=[jax.ShapeDtypeStruct(part, F32)] * 4,
        in_specs=[VMEM_SPEC] * 4,
        out_specs=[VMEM_SPEC] * 4,
        compiler_params=pltpu.CompilerParams(vmem_limit_bytes=4 * MIB),
        cost_estimate=pl.CostEstimate(flops=200_000, bytes_accessed=500_000, transcendentals=0),
        name="combine",
    )(own, *received)


def square_body(
    n,
    residual,
    queries,
    key_value_cache,
    lengths,
    slot_of,
    out_weight,
    expert_ids,
    route_weight,
    in_weight,
    down_weight,
):
    rows = queries.shape[0]
    mirror = [(e * n + h, h * n + e) for e in range(n) for h in range(n)]
    crossed = lax.ppermute(residual, ("ep", "hd"), mirror)
    cache = key_value_cache.reshape(rows, 2 * CACHE_LENGTH, HEAD_SIZE)
    attended = attention(lengths, queries, cache, expert_ids, route_weight)
    blocks = [attended] + [swap(attended, "ep", k, n) for k in range(1, n)]
    projected, routing = projection(slot_of, blocks, out_weight)
    mine = lax.axis_index("hd")
    pieces = [lax.dynamic_index_in_dim(projected, mine ^ k, 0, keepdims=False) for k in range(n)]
    summed = pieces[0]
    for k in range(1, n):
        summed = summed + swap(pieces[k], "hd", k, n)
    stream = crossed.astype(F32) + summed
    returned = lax.ppermute(stream, ("ep", "hd"), mirror)
    normed = norm([stream] + [swap(stream, "ep", k, n) for k in range(1, n)])
    full_rows = lax.all_gather(normed, "hd", axis=0, tiled=True)
    own, *others = experts(full_rows, routing, jnp.swapaxes(in_weight, 1, 2), down_weight)
    received = [swap(block, "hd", k + 1, n) for k, block in enumerate(others)]
    own, *others = combine(own, received)
    total = returned + own
    for k, block in enumerate(others):
        total = total + swap(block, "ep", k + 1, n)
    return total.astype(BF16)


def expert_pass(block, in_weight, down_weight):
    local_count = in_weight.shape[0]
    senders = block.shape[0] // local_count
    slots = block.shape[1]
    width = block.shape[2]
    grouped = block.reshape(senders, local_count, slots, width)
    hidden = jnp.einsum("secd,edf->secf", grouped, in_weight, preferred_element_type=jnp.float32)
    hidden = jax.nn.silu(hidden).astype(jnp.bfloat16)
    output = jnp.einsum("secf,efd->secd", hidden, down_weight, preferred_element_type=jnp.float32)
    return output.reshape(senders * local_count, slots, width)


def body(
    residual,
    queries,
    key_value_cache,
    lengths,
    slot_of,
    out_weight,
    expert_ids,
    route_weight,
    in_weight,
    down_weight,
):
    rows_here = queries.shape[0]
    local_groups = key_value_cache.shape[3] // HEAD_SIZE
    heads_per_group = QUERY_HEADS // KEY_VALUE_HEADS
    query_head_rows = queries.reshape(rows_here, local_groups, heads_per_group, HEAD_SIZE)
    cached_key_rows = key_value_cache[:, :, 0].reshape(
        rows_here, CACHE_LENGTH, local_groups, HEAD_SIZE
    )
    cached_value_rows = key_value_cache[:, :, 1].reshape(
        rows_here, CACHE_LENGTH, local_groups, HEAD_SIZE
    )
    scores = jnp.einsum(
        "sagd,slad->sagl", query_head_rows, cached_key_rows, preferred_element_type=jnp.float32
    )
    scores = scores * (1.0 / math.sqrt(HEAD_SIZE))
    visible = (jnp.arange(CACHE_LENGTH)[None, :] < lengths[:, None])[:, None, None, :]
    scores = jnp.where(visible, scores, -1e30)
    highest = jnp.max(scores, axis=3, keepdims=True)
    raised = jnp.where(visible, jnp.exp(scores - highest), 0.0)
    weights = (raised / jnp.sum(raised, axis=3, keepdims=True)).astype(jnp.bfloat16)
    attended = jnp.einsum(
        "sagl,slad->sagd", weights, cached_value_rows, preferred_element_type=jnp.float32
    )
    attended = attended.astype(jnp.bfloat16).reshape(
        rows_here, local_groups * heads_per_group * HEAD_SIZE
    )
    partial_value = jnp.dot(
        lax.all_gather(attended, "ep", axis=0, tiled=True),
        out_weight,
        preferred_element_type=jnp.float32,
    )
    ordered = jnp.take(partial_value, slot_of, axis=0)
    moved = lax.all_to_all(ordered, "ep", split_axis=0, concat_axis=1, tiled=True)
    summed = lax.psum_scatter(moved, "hd", scatter_dimension=1, tiled=True)
    stream = residual.astype(jnp.float32) + summed
    squares = lax.psum(jnp.sum(stream * stream, axis=1), "hd")
    normed = (stream * lax.rsqrt(squares / D + 1e-06)[:, None]).astype(jnp.bfloat16)
    picked = expert_ids.reshape(-1)
    member = (picked[:, None] == jnp.arange(EXPERTS)[None, :]).astype(jnp.int32)
    earlier = jnp.cumsum(member, axis=0) - member
    position = jnp.sum(earlier * member, axis=1)
    target = picked * CAP + position
    placed = (target[:, None] == jnp.arange(EXPERTS * CAP)[None, :]).astype(jnp.float32)
    owner = (jnp.arange(picked.shape[0])[:, None] // TOPK == jnp.arange(rows_here)[None, :]).astype(
        jnp.float32
    )
    select_matrix = jnp.dot(placed.T, owner, precision=lax.Precision.HIGHEST).astype(jnp.bfloat16)
    mixing = jnp.dot(
        owner.T, placed * route_weight.reshape(-1)[:, None], precision=lax.Precision.HIGHEST
    )
    full_rows = lax.all_gather(normed, "hd", axis=1, tiled=True)
    outgoing = jnp.dot(select_matrix, full_rows, preferred_element_type=jnp.float32).astype(
        jnp.bfloat16
    )
    outgoing = outgoing.reshape(EXPERTS, CAP, full_rows.shape[1])
    results = expert_pass(
        lax.all_to_all(outgoing, "ep", split_axis=0, concat_axis=0, tiled=True),
        in_weight,
        down_weight,
    )
    share_width = residual.shape[1]
    shares = lax.psum_scatter(results.astype(jnp.bfloat16), "hd", scatter_dimension=2, tiled=True)
    returned = lax.all_to_all(shares, "ep", split_axis=0, concat_axis=0, tiled=True)
    flat_back = returned.reshape(EXPERTS * CAP, share_width).astype(jnp.float32)
    mixture = jnp.dot(mixing, flat_back, precision=lax.Precision.HIGHEST)
    return (stream + mixture).astype(jnp.bfloat16)


def solution(mesh):
    in_specs = (
        P(("groups", "ep"), "hd"),
        P(("groups", "ep"), "hd"),
        P(("groups", "ep"), None, None, "hd"),
        P(("groups", "ep")),
        P("groups"),
        P("hd", "ep"),
        P(("groups", "ep"), None),
        P(("groups", "ep"), None),
        P("ep", None, "hd"),
        P("ep", "hd", None),
    )
    out_specs = P(("groups", "ep"), "hd")
    chosen = functools.partial(square_body, 4) if mesh.shape["ep"] == mesh.shape["hd"] == 4 else body
    return jax.shard_map(chosen, mesh=mesh, in_specs=in_specs, out_specs=out_specs, check_vma=False)
```

```python
import functools
import math

import jax
import jax.numpy as jnp
from jax import lax
from jax.experimental import pallas as pl
from jax.experimental.pallas import tpu as pltpu
from jax.sharding import PartitionSpec as P

D = 4096
QUERY_HEADS = 64
KEY_VALUE_HEADS = 4
HEAD_SIZE = 128
EXPERTS = 64
TOPK = 8
CAP = 2
CACHE_LENGTH = 256
SIDE = 4
BF16 = jnp.bfloat16
F32 = jnp.float32
MIB = 1 << 20
HERE = pl.BlockSpec(memory_space=pltpu.VMEM)
SCALARS = pl.BlockSpec(memory_space=pltpu.SMEM)
ANYWHERE = pl.BlockSpec(memory_space=pl.ANY)
DMA = pltpu.SemaphoreType.DMA


def swap(block, axis, k):
    return lax.ppermute(block, axis, [(i, i ^ k) for i in range(SIDE)])


def far(array):
    return pltpu.with_memory_space_constraint(array, pltpu.HBM)


def split3(value):
    high = value.astype(BF16)
    rest = value - high.astype(F32)
    middle = rest.astype(BF16)
    low = (rest - middle.astype(F32)).astype(BF16)
    return high, middle, low


def kernel_call(body, name, out_shape, in_specs, scratch=(), limit=4, cost=(0, 0, 0), aliases=None):
    many = isinstance(out_shape, (tuple, list))
    return pl.pallas_call(
        body,
        out_shape=out_shape,
        in_specs=in_specs,
        out_specs=(HERE,) * len(out_shape) if many else HERE,
        scratch_shapes=list(scratch),
        input_output_aliases=aliases or {},
        compiler_params=pltpu.CompilerParams(vmem_limit_bytes=limit * MIB),
        cost_estimate=pl.CostEstimate(
            flops=cost[0], bytes_accessed=cost[1], transcendentals=cost[2]
        ),
        name=name,
    )


def attention_kernel(
    lengths_far,
    queries_far,
    cache_far,
    ids_far,
    route_far,
    residual_far,
    weight_far,
    entry_far,
    out,
    weight,
    entry,
    lengths,
    queries,
    cache,
    ids,
    route,
    residual,
    staged,
    gathered,
    sems,
):
    width = entry.shape[2]
    own = pl.ds(pl.multiple_of(lax.axis_index("ep") * width, width), width)
    copies = [
        pltpu.make_async_copy(source, target, sems.at[i])
        for i, (source, target) in enumerate(
            (
                (lengths_far, lengths),
                (queries_far, queries),
                (cache_far, cache),
                (ids_far, ids),
                (route_far, route),
                (residual_far, residual),
                (weight_far, weight),
                (entry_far.at[:, :, own], entry),
            )
        )
    ]
    for copy in copies:
        copy.start()
    copies[0].wait()
    copies[1].wait()
    rows = queries.shape[0]
    heads = queries.shape[1] // HEAD_SIZE
    for h in range(heads):
        lanes = slice(h * HEAD_SIZE, (h + 1) * HEAD_SIZE)
        staged[h * rows : (h + 1) * rows, :] = queries[:, lanes].astype(F32)
    copies[2].wait()
    place = lax.broadcasted_iota(jnp.int32, (heads, 2 * CACHE_LENGTH), 1)
    for s in range(rows):
        mine = staged[pl.ds(s, heads, stride=rows), :].astype(BF16)
        both = cache[s]
        scores = lax.dot_general(
            mine, both, (((1,), (1,)), ((), ())), preferred_element_type=F32
        ) * (1.0 / math.sqrt(HEAD_SIZE))
        visible = jnp.logical_and(place % 2 == 0, place < 2 * lengths[s])
        scores = jnp.where(visible, scores, -1e30)
        raised = jnp.where(visible, jnp.exp(scores - jnp.max(scores, axis=1, keepdims=True)), 0.0)
        weights = raised / jnp.sum(raised, axis=1, keepdims=True)
        moved = pltpu.roll(weights, 1, 1).astype(BF16)
        gathered[pl.ds(s, heads, stride=rows), :] = jnp.dot(
            moved, both, preferred_element_type=F32
        )
    width = heads * HEAD_SIZE
    for h in range(heads):
        lanes = slice(h * HEAD_SIZE, (h + 1) * HEAD_SIZE)
        out[:, lanes] = gathered[h * rows : (h + 1) * rows, :].astype(BF16)
    copies[3].wait()
    copies[4].wait()
    row = lax.broadcasted_iota(jnp.int32, (TOPK, 128), 0)
    lane = lax.broadcasted_iota(jnp.int32, (TOPK, 128), 1)
    total = jnp.zeros((rows, 128), F32)
    for j, part in enumerate((ids[...].astype(F32).astype(BF16), *split3(route[...]))):
        spread = (lane == row + j * TOPK).astype(F32).astype(BF16)
        total = total + jnp.dot(part, spread, preferred_element_type=F32)
    out[:, width : width + 128] = total.astype(BF16)
    copies[5].wait()
    out[:, width + 128 :] = residual[...]
    copies[6].wait()
    copies[7].wait()


def attention(lengths, queries, cache, ids, route, residual, weight, entry):
    rows, width = queries.shape
    staged = pltpu.VMEM((rows * width // HEAD_SIZE, HEAD_SIZE), F32)
    return kernel_call(
        attention_kernel,
        "attention",
        (
            jax.ShapeDtypeStruct((rows, width + 128 + residual.shape[1]), BF16),
            pltpu.VMEM(weight.shape, BF16),
            pltpu.VMEM((*entry.shape[:2], entry.shape[2] // SIDE), BF16),
        ),
        [ANYWHERE] * 8,
        [
            pltpu.SMEM(lengths.shape, jnp.int32),
            pltpu.VMEM(queries.shape, BF16),
            pltpu.VMEM(cache.shape, BF16),
            pltpu.VMEM(ids.shape, jnp.int32),
            pltpu.VMEM(route.shape, F32),
            pltpu.VMEM(residual.shape, BF16),
            staged,
            staged,
            DMA((8,)),
        ],
        cost=(10_000_000, 12_000_000, 65536),
    )(*map(far, (lengths, queries, cache, ids, route, residual, weight, entry)))


def fetch_entry_kernel(after, source, t1, t2, t3, sems):
    del after
    width = t1.shape[2]
    copies = []
    for k, target in enumerate((t1, t2, t3), 1):
        start = pl.multiple_of((lax.axis_index("ep") ^ k) * width, width)
        copies.append(
            pltpu.make_async_copy(source.at[:, :, pl.ds(start, width)], target, sems.at[k - 1])
        )
    for copy in copies:
        copy.start()
    for copy in copies:
        copy.wait()


def fetch_entry(source, after):
    shape = (*source.shape[:2], source.shape[2] // SIDE)
    return kernel_call(
        fetch_entry_kernel,
        "fetch_entry",
        (pltpu.VMEM(shape, BF16),) * 3,
        [ANYWHERE, ANYWHERE],
        [DMA((3,))],
        limit=1,
        cost=(0, 6 * math.prod(shape), 0),
    )(after, far(source))


def fetch_kernel(start, after, source, target, sem):
    del after
    copy = pltpu.make_async_copy(source.at[pl.ds(start, target.shape[0])], target, sem)
    copy.start()
    copy.wait()


def fetch(name, source, start, count, after):
    shape = (count, *source.shape[1:])
    return kernel_call(
        functools.partial(fetch_kernel, start),
        name,
        pltpu.VMEM(shape, BF16),
        [ANYWHERE, ANYWHERE],
        [DMA],
        limit=1,
        cost=(0, 2 * math.prod(shape), 0),
    )(after, far(source))


def projection_kernel(slot_far, b0, b1, b2, b3, weight, unused, out, routing, slot_of, kept, sem):
    del unused
    copy = pltpu.make_async_copy(slot_far, slot_of, sem)
    copy.start()
    blocks = (b0, b1, b2, b3)
    rows = b0.shape[0]
    width = weight.shape[0]
    everyone = SIDE * rows
    me = lax.axis_index("ep")
    held = jnp.concatenate([b[:, :width].astype(F32) for b in blocks], axis=0).astype(BF16)
    row = lax.broadcasted_iota(jnp.int32, (everyone, everyone), 0)
    column = lax.broadcasted_iota(jnp.int32, (everyone, everyone), 1)
    wanted = jnp.zeros((everyone, everyone), jnp.int32)
    for k, block in enumerate(blocks):
        span = pl.ds(pl.multiple_of((me ^ k) * rows, rows), rows)
        routing[span, :] = block[:, width : width + 128].astype(F32)
        kept[span, :] = block[:, width + 128 :].astype(F32)
    copy.wait()
    for r in range(everyone):
        slot = slot_of[r]
        wanted = jnp.where(row == r, ((slot // rows) ^ me) * rows + slot % rows, wanted)
    order = (wanted == column).astype(F32).astype(BF16)
    ordered = jnp.dot(order, held, preferred_element_type=F32).astype(BF16)
    own = (me == lax.axis_index("hd")).astype(F32)
    out[...] = jnp.dot(ordered, weight[...], preferred_element_type=F32) + own * kept[...]


def projection(slot_of, blocks, weight, unused):
    everyone = SIDE * blocks[0].shape[0]
    wide = (everyone, weight.shape[1])
    return kernel_call(
        projection_kernel,
        "projection",
        (jax.ShapeDtypeStruct(wide, F32), jax.ShapeDtypeStruct((everyone, 128), F32)),
        [ANYWHERE] + [HERE] * 5 + [ANYWHERE],
        [pltpu.SMEM(slot_of.shape, jnp.int32), pltpu.VMEM(wide, F32), DMA],
        limit=6,
        cost=(140_000_000, 4_500_000, 0),
    )(far(slot_of), *blocks, weight, unused)


def add_kernel(a, b, out):
    out[...] = a[...] + b[...]


def add(a, b):
    return kernel_call(
        add_kernel, "add", jax.ShapeDtypeStruct(a.shape, F32), [HERE] * 2, cost=(a.size, a.size, 0)
    )(a, b)


def stream_kernel(a, b, unused, stream, packed):
    del unused
    total = a[...] + b[...]
    stream[...] = total
    width = total.shape[1]
    packed[:, :width] = total.astype(BF16)
    squares = jnp.sum(total * total, axis=1, keepdims=True)
    lane = lax.broadcasted_iota(jnp.int32, (total.shape[0], 128), 1)
    parts = [part.astype(F32) for part in split3(jnp.broadcast_to(squares, lane.shape))]
    spread = jnp.where(lane == 0, parts[0], jnp.where(lane == 1, parts[1], parts[2]))
    packed[:, width:] = jnp.where(lane < 3, spread, 0.0).astype(BF16)


def streams(a, b, unused):
    rows, width = a.shape
    return kernel_call(
        stream_kernel,
        "stream",
        (jax.ShapeDtypeStruct(a.shape, F32), jax.ShapeDtypeStruct((rows, width + 128), BF16)),
        [HERE, HERE, ANYWHERE],
        cost=(a.size * 4, a.size * 4, 0),
    )(a, b, unused)


def entry_product(packed, near, put):
    count, hidden, width = near.shape
    turned = packed[:, :width].astype(F32).T.astype(BF16)
    for e in range(count):
        part = jnp.dot(near[e], turned, preferred_element_type=F32)
        put(e * hidden, hidden, part)


def entry_first_kernel(start, packed, near, source, out, target, sem):
    copy = pltpu.make_async_copy(source.at[pl.ds(start, target.shape[0])], target, sem)
    copy.start()

    def put(at, hidden, part):
        out[at : at + hidden, :] = part

    entry_product(packed, near, put)
    copy.wait()


def entry_next_kernel(start, packed, near, before, source, out, target, sem):
    copy = pltpu.make_async_copy(source.at[pl.ds(start, target.shape[0])], target, sem)
    copy.start()

    def put(at, hidden, part):
        out[at : at + hidden, :] = before[at : at + hidden, :] + part

    entry_product(packed, near, put)
    copy.wait()


def entry_more_kernel(packed, near, before, out):
    def put(at, hidden, part):
        out[at : at + hidden, :] = before[at : at + hidden, :] + part

    entry_product(packed, near, put)


def entry_last_kernel(packed, near, before, routing, p0, p1, p2, out):
    count, _, width = near.shape
    rows = packed.shape[0]
    squares = jnp.zeros((rows, 128), F32)
    for block in (p0, p1, p2, packed):
        squares = squares + block[:, width:].astype(F32)
    mean = jnp.sum(squares.T, axis=0, keepdims=True) / (SIDE * width)
    scale = lax.rsqrt(mean + 1e-06)
    table = routing[...].T
    ids = table[0:TOPK, :]
    weight = table[TOPK : 2 * TOPK, :] + table[2 * TOPK : 3 * TOPK, :]
    weight = weight + table[3 * TOPK : 4 * TOPK, :]
    base = lax.axis_index("ep") * count

    def put(at, hidden, part):
        number = (base + at // hidden).astype(F32)
        share = jnp.sum(jnp.where(ids == number, weight, 0.0), axis=0, keepdims=True)
        total = (before[at : at + hidden, :] + part) * scale
        active = (total / (1.0 + jnp.exp(-total))).astype(BF16).astype(F32) * share
        high = active.astype(BF16).astype(F32)
        out[at : at + hidden, :] = jnp.concatenate([high, active - high], axis=1).astype(BF16)

    entry_product(packed, near, put)


def entries(packs, near, routing, source, starts):
    count, hidden, width = source.shape
    rows = packs[0].shape[0]
    part = jax.ShapeDtypeStruct((count * hidden, rows), F32)
    cost = (2 * rows * count * hidden * width // SIDE, 2 * count * hidden * width // SIDE, 0)
    bring = lambda start, end: pltpu.VMEM((end - start, hidden, width), BF16)
    total, more = kernel_call(
        functools.partial(entry_first_kernel, starts[0]),
        "entry0",
        (part, bring(*starts[:2])),
        [HERE] * 2 + [ANYWHERE],
        [DMA],
        cost=cost,
    )(packs[0], near[0], far(source))
    total, rest = kernel_call(
        functools.partial(entry_next_kernel, starts[1]),
        "entry1",
        (part, bring(starts[1], count)),
        [HERE] * 3 + [ANYWHERE],
        [DMA],
        cost=cost,
        aliases={2: 0},
    )(packs[1], near[1], total, far(source))
    total = kernel_call(
        entry_more_kernel, "entry2", part, [HERE] * 3, cost=cost, aliases={2: 0}
    )(packs[2], near[2], total)
    scaled = kernel_call(
        entry_last_kernel,
        "entry3",
        jax.ShapeDtypeStruct((count * hidden, 2 * rows), BF16),
        [HERE] * 7,
        cost=cost,
    )(packs[3], near[3], total, routing, *packs[:3])
    return scaled, more, rest


def leave_product(start, count, step, scaled, near, out):
    rows = out.shape[0]
    left = scaled[...].astype(F32).T.astype(BF16)
    for c in range(0, count, step):
        columns = pl.ds(pl.multiple_of(start + c, step), step)
        total = jnp.zeros((2 * rows, step), F32)
        at = 0
        for array in near:
            depth = array.shape[0] * array.shape[1]
            flat = array.reshape(depth, array.shape[2])
            total = total + jnp.dot(
                left[:, at : at + depth], flat[:, columns], preferred_element_type=F32
            )
            at += depth
        out[:, c : c + step] = (total[:rows] + total[rows:]).astype(out.dtype)


def leave_kernel(other, step, scaled, a, b, c, unused, out):
    del unused
    half = out.shape[1]
    chip = (lax.axis_index("hd") // 2) ^ other
    leave_product(pl.multiple_of(chip * half, half), half, step, scaled, (a, b, c), out)


def leaves(name, other, dtype, scaled, near, unused):
    count = sum(array.shape[0] for array in near)
    _, hidden, width = near[0].shape
    rows = scaled.shape[1] // 2
    return kernel_call(
        functools.partial(leave_kernel, other, 1024),
        name,
        jax.ShapeDtypeStruct((rows, width // 2), dtype),
        [HERE] * 4 + [ANYWHERE],
        cost=(2 * rows * count * hidden * width, count * hidden * width, 0),
        limit=6,
    )(scaled, *near, unused)


def halve_kernel(mine, received, keep, send):
    width = keep.shape[1]
    core = lax.axis_index("hd") % 2
    for out, which in ((send, 1 - core), (keep, core)):
        columns = pl.ds(pl.multiple_of(which * width, width), width)
        out[...] = mine[:, columns] + received[:, columns].astype(F32)


def halve(mine, received):
    rows, width = mine.shape
    return kernel_call(
        halve_kernel,
        "halve",
        (jax.ShapeDtypeStruct((rows, width // 2), F32),) * 2,
        [HERE] * 2,
        cost=(mine.size, mine.size * 6, 0),
    )(mine, received)


def share_kernel(own, received, stream, o0, o1, o2, o3):
    rows = o0.shape[0]
    me = lax.axis_index("ep")
    here = (me == lax.axis_index("hd")).astype(F32)
    for k, out in enumerate((o0, o1, o2, o3)):
        span = pl.ds(pl.multiple_of((me ^ k) * rows, rows), rows)
        out[...] = own[span, :] + received[span, :] + here * stream[span, :]


def share(own, received, stream):
    rows, width = own.shape
    return kernel_call(
        share_kernel,
        "share",
        (jax.ShapeDtypeStruct((rows // SIDE, width), F32),) * SIDE,
        [HERE] * 3,
        cost=(own.size * 3, own.size * 16, 0),
    )(own, received, stream)


def square_body(
    residual,
    queries,
    key_value_cache,
    lengths,
    slot_of,
    out_weight,
    expert_ids,
    route_weight,
    in_weight,
    down_weight,
):
    rows = queries.shape[0]
    cache = key_value_cache.reshape(rows, 2 * CACHE_LENGTH, HEAD_SIZE)
    entry = jnp.swapaxes(in_weight, 1, 2)
    count = entry.shape[0]
    starts = (count // 2, count * 3 // 4)
    attended, weight, near0 = attention(
        lengths, queries, cache, expert_ids, route_weight, residual, out_weight, entry
    )
    blocks = [attended] + [swap(attended, "ep", k) for k in (1, 2, 3)]
    near = (near0, *fetch_entry(entry, attended))
    partial_value, routing = projection(slot_of, blocks, weight, near[3])
    pair = add(partial_value, swap(partial_value, "hd", 1))
    far_pair = swap(pair, "hd", 2)
    leave_a = fetch("fetch_leave", down_weight, 0, starts[0], pair)
    stream, packed = streams(pair, far_pair, leave_a)
    packs = [packed] + [swap(packed, "ep", k) for k in (1, 2, 3)]
    scaled, *rest = entries(packs, near, routing, down_weight, starts)
    theirs = leaves("leave_away", 1, BF16, scaled, (leave_a, *rest), scaled)
    mine = leaves("leave_here", 0, F32, scaled, (leave_a, *rest), theirs)
    keep, send = halve(mine, swap(theirs, "hd", 2))
    total, *others = share(keep, swap(send, "hd", 1), stream)
    for k, block in enumerate(others):
        total = total + swap(block, "ep", k + 1)
    return total.astype(BF16)


def expert_pass(block, in_weight, down_weight):
    local_count = in_weight.shape[0]
    senders = block.shape[0] // local_count
    slots = block.shape[1]
    width = block.shape[2]
    grouped = block.reshape(senders, local_count, slots, width)
    hidden = jnp.einsum("secd,edf->secf", grouped, in_weight, preferred_element_type=jnp.float32)
    hidden = jax.nn.silu(hidden).astype(jnp.bfloat16)
    output = jnp.einsum("secf,efd->secd", hidden, down_weight, preferred_element_type=jnp.float32)
    return output.reshape(senders * local_count, slots, width)


def body(
    residual,
    queries,
    key_value_cache,
    lengths,
    slot_of,
    out_weight,
    expert_ids,
    route_weight,
    in_weight,
    down_weight,
):
    rows_here = queries.shape[0]
    local_groups = key_value_cache.shape[3] // HEAD_SIZE
    heads_per_group = QUERY_HEADS // KEY_VALUE_HEADS
    query_head_rows = queries.reshape(rows_here, local_groups, heads_per_group, HEAD_SIZE)
    cached_key_rows = key_value_cache[:, :, 0].reshape(
        rows_here, CACHE_LENGTH, local_groups, HEAD_SIZE
    )
    cached_value_rows = key_value_cache[:, :, 1].reshape(
        rows_here, CACHE_LENGTH, local_groups, HEAD_SIZE
    )
    scores = jnp.einsum(
        "sagd,slad->sagl", query_head_rows, cached_key_rows, preferred_element_type=jnp.float32
    )
    scores = scores * (1.0 / math.sqrt(HEAD_SIZE))
    visible = (jnp.arange(CACHE_LENGTH)[None, :] < lengths[:, None])[:, None, None, :]
    scores = jnp.where(visible, scores, -1e30)
    highest = jnp.max(scores, axis=3, keepdims=True)
    raised = jnp.where(visible, jnp.exp(scores - highest), 0.0)
    weights = (raised / jnp.sum(raised, axis=3, keepdims=True)).astype(jnp.bfloat16)
    attended = jnp.einsum(
        "sagl,slad->sagd", weights, cached_value_rows, preferred_element_type=jnp.float32
    )
    attended = attended.astype(jnp.bfloat16).reshape(
        rows_here, local_groups * heads_per_group * HEAD_SIZE
    )
    partial_value = jnp.dot(
        lax.all_gather(attended, "ep", axis=0, tiled=True),
        out_weight,
        preferred_element_type=jnp.float32,
    )
    ordered = jnp.take(partial_value, slot_of, axis=0)
    moved = lax.all_to_all(ordered, "ep", split_axis=0, concat_axis=1, tiled=True)
    summed = lax.psum_scatter(moved, "hd", scatter_dimension=1, tiled=True)
    stream = residual.astype(jnp.float32) + summed
    squares = lax.psum(jnp.sum(stream * stream, axis=1), "hd")
    normed = (stream * lax.rsqrt(squares / D + 1e-06)[:, None]).astype(jnp.bfloat16)
    picked = expert_ids.reshape(-1)
    member = (picked[:, None] == jnp.arange(EXPERTS)[None, :]).astype(jnp.int32)
    earlier = jnp.cumsum(member, axis=0) - member
    position = jnp.sum(earlier * member, axis=1)
    target = picked * CAP + position
    placed = (target[:, None] == jnp.arange(EXPERTS * CAP)[None, :]).astype(jnp.float32)
    owner = (jnp.arange(picked.shape[0])[:, None] // TOPK == jnp.arange(rows_here)[None, :]).astype(
        jnp.float32
    )
    select_matrix = jnp.dot(placed.T, owner, precision=lax.Precision.HIGHEST).astype(jnp.bfloat16)
    mixing = jnp.dot(
        owner.T, placed * route_weight.reshape(-1)[:, None], precision=lax.Precision.HIGHEST
    )
    full_rows = lax.all_gather(normed, "hd", axis=1, tiled=True)
    outgoing = jnp.dot(select_matrix, full_rows, preferred_element_type=jnp.float32).astype(
        jnp.bfloat16
    )
    outgoing = outgoing.reshape(EXPERTS, CAP, full_rows.shape[1])
    results = expert_pass(
        lax.all_to_all(outgoing, "ep", split_axis=0, concat_axis=0, tiled=True),
        in_weight,
        down_weight,
    )
    share_width = residual.shape[1]
    shares = lax.psum_scatter(results.astype(jnp.bfloat16), "hd", scatter_dimension=2, tiled=True)
    returned = lax.all_to_all(shares, "ep", split_axis=0, concat_axis=0, tiled=True)
    flat_back = returned.reshape(EXPERTS * CAP, share_width).astype(jnp.float32)
    mixture = jnp.dot(mixing, flat_back, precision=lax.Precision.HIGHEST)
    return (stream + mixture).astype(jnp.bfloat16)


def solution(mesh):
    in_specs = (
        P(("groups", "ep"), "hd"),
        P(("groups", "ep"), "hd"),
        P(("groups", "ep"), None, None, "hd"),
        P(("groups", "ep")),
        P("groups"),
        P("hd", "ep"),
        P(("groups", "ep"), None),
        P(("groups", "ep"), None),
        P("ep", None, "hd"),
        P("ep", "hd", None),
    )
    out_specs = P(("groups", "ep"), "hd")
    chosen = square_body if mesh.shape["ep"] == mesh.shape["hd"] == SIDE else body
    return jax.shard_map(chosen, mesh=mesh, in_specs=in_specs, out_specs=out_specs, check_vma=False)
```

```python
import functools
import math

import jax
import jax.numpy as jnp
from jax import lax
from jax.experimental import pallas as pl
from jax.experimental.pallas import tpu as pltpu
from jax.sharding import PartitionSpec as P

D = 4096
QUERY_HEADS = 64
KEY_VALUE_HEADS = 4
HEAD_SIZE = 128
EXPERTS = 64
TOPK = 8
CAP = 2
CACHE_LENGTH = 256
SIDE = 4
BF16 = jnp.bfloat16
F32 = jnp.float32
MIB = 1 << 20
HERE = pl.BlockSpec(memory_space=pltpu.VMEM)
SCALARS = pl.BlockSpec(memory_space=pltpu.SMEM)
ANYWHERE = pl.BlockSpec(memory_space=pl.ANY)
DMA = pltpu.SemaphoreType.DMA


def swap(block, axis, k):
    return lax.ppermute(block, axis, [(i, i ^ k) for i in range(SIDE)])


def far(array):
    return pltpu.with_memory_space_constraint(array, pltpu.HBM)


def split3(value):
    high = value.astype(BF16)
    rest = value - high.astype(F32)
    middle = rest.astype(BF16)
    low = (rest - middle.astype(F32)).astype(BF16)
    return high, middle, low


def hosted(body, inputs, outputs, loads):
    n = len(loads)

    def kernel(*refs):
        sources = refs[inputs : inputs + n]
        targets = refs[inputs + n + outputs : inputs + n + outputs + n]
        ins, outs = refs[:inputs], refs[inputs + n : inputs + n + outputs]
        copies = []
        for i, (load, source, target) in enumerate(zip(loads, sources, targets)):
            _, first, count, place = load
            width = target.shape[2]
            columns = pl.ds(pl.multiple_of(place() * width, width), width)
            source = source.at[pl.ds(first, count), :, columns]
            copies.append(pltpu.make_async_copy(source, target, refs[-1].at[i]))
        begin = lambda: [copy.start() for copy in copies]
        rest = refs[inputs + outputs + 2 * n : -1]
        if body is attention_kernel:
            body(*ins, *outs, *rest, begin)
        else:
            begin()
            body(*ins, *outs, *rest)
        for copy in copies:
            copy.wait()

    return kernel


def kernel_call(
    body, name, args, specs, outs, scratch=(), loads=(), parts=1, limit=4, cost=(0, 0, 0), aliases=None
):
    targets = [
        pltpu.VMEM((count, array.shape[1], array.shape[2] // part), BF16)
        for (array, _, count, _), part in zip(loads, parts if loads else ())
    ]
    flops, bytes_accessed, transcendentals = cost
    bytes_accessed += sum(2 * math.prod(target.shape) for target in targets)
    results = pl.pallas_call(
        hosted(body, len(args), len(outs), loads) if loads else body,
        out_shape=(*outs, *targets),
        in_specs=[*specs] + [ANYWHERE] * len(loads),
        out_specs=(HERE,) * (len(outs) + len(targets)),
        scratch_shapes=[*scratch] + ([DMA((len(loads),))] if loads else []),
        input_output_aliases=aliases or {},
        compiler_params=pltpu.CompilerParams(vmem_limit_bytes=limit * MIB),
        cost_estimate=pl.CostEstimate(
            flops=flops, bytes_accessed=bytes_accessed, transcendentals=transcendentals
        ),
        name=name,
    )(*args, *(far(array) for array, *_ in loads))
    return results[: len(outs)], results[len(outs) :]


class Loads:
    def __init__(self, entry, leave):
        self.entry, self.leave = entry, leave
        self.near = {}

    def call(self, body, name, args, specs, outs, pieces=(), **more):
        loads, parts = [], []
        for what, which, first, count in pieces:
            if what == "entry":
                loads.append((self.entry, first, count, functools.partial(self.block, which)))
                parts.append(SIDE)
            else:
                loads.append((self.leave, first, count, functools.partial(self.half, which)))
                parts.append(2)
        results, arrays = kernel_call(
            body, name, args, specs, outs, loads=tuple(loads), parts=parts, **more
        )
        for (what, which, _, _), array in zip(pieces, arrays):
            self.near.setdefault((what, which), []).append(array)
        return results

    @staticmethod
    def block(k):
        return lax.axis_index("ep") ^ k

    @staticmethod
    def half(other):
        return (lax.axis_index("hd") // 2) ^ other


def shaped(shape, dtype=F32):
    return jax.ShapeDtypeStruct(shape, dtype)


def attention_kernel(
    lengths_far,
    queries_far,
    cache_far,
    ids_far,
    route_far,
    residual_far,
    weight_far,
    out,
    weight,
    lengths,
    queries,
    cache,
    ids,
    route,
    residual,
    staged,
    gathered,
    sems,
    begin,
):
    pairs = (
        (lengths_far, lengths),
        (queries_far, queries),
        (cache_far, cache),
        (ids_far, ids),
        (route_far, route),
        (residual_far, residual),
        (weight_far, weight),
    )
    copies = [pltpu.make_async_copy(*pair, sems.at[i]) for i, pair in enumerate(pairs)]
    for copy in copies:
        copy.start()
    begin()
    rows = queries.shape[0]
    heads = queries.shape[1] // HEAD_SIZE
    everyone = rows * heads
    copies[1].wait()
    for h in range(heads):
        lanes = slice(h * HEAD_SIZE, (h + 1) * HEAD_SIZE)
        staged[pl.ds(h, rows, stride=heads), :] = queries[:, lanes].astype(F32)
    turned = staged[...].T.astype(BF16)
    copies[0].wait()
    slot = lax.broadcasted_iota(jnp.int32, (1, everyone), 1) // heads
    limit = jnp.zeros((1, everyone), jnp.int32)
    for s in range(rows):
        limit = jnp.where(slot == s, 2 * lengths[s], limit)
    place = lax.broadcasted_iota(jnp.int32, (2 * CACHE_LENGTH, everyone), 0)
    visible = jnp.logical_and(place % 2 == 0, place < limit)
    copies[2].wait()
    scores = jnp.dot(cache[0], turned, preferred_element_type=F32)
    for s in range(1, rows):
        more = jnp.dot(cache[s], turned, preferred_element_type=F32)
        scores = jnp.where(slot == s, more, scores)
    scores = jnp.where(visible, scores * (1.0 / math.sqrt(HEAD_SIZE)), -1e30)
    raised = jnp.where(visible, jnp.exp(scores - jnp.max(scores, axis=0, keepdims=True)), 0.0)
    weights = raised / jnp.sum(raised, axis=0, keepdims=True)
    moved = pltpu.roll(weights, 1, 0).T.astype(BF16)
    for s in range(rows):
        span = slice(s * heads, (s + 1) * heads)
        gathered[span, :] = jnp.dot(moved[span], cache[s], preferred_element_type=F32)
    width = heads * HEAD_SIZE
    for h in range(heads):
        lanes = slice(h * HEAD_SIZE, (h + 1) * HEAD_SIZE)
        out[:, lanes] = gathered[pl.ds(h, rows, stride=heads), :].astype(BF16)
    copies[3].wait()
    copies[4].wait()
    row = lax.broadcasted_iota(jnp.int32, (TOPK, 128), 0)
    lane = lax.broadcasted_iota(jnp.int32, (TOPK, 128), 1)
    total = jnp.zeros((rows, 128), F32)
    for j, part in enumerate((ids[...].astype(F32).astype(BF16), *split3(route[...]))):
        spread = (lane == row + j * TOPK).astype(F32).astype(BF16)
        total = total + jnp.dot(part, spread, preferred_element_type=F32)
    out[:, width : width + 128] = total.astype(BF16)
    copies[5].wait()
    out[:, width + 128 :] = residual[...]
    copies[6].wait()


def attention(loads, pieces, lengths, queries, cache, ids, route, residual, weight):
    rows, width = queries.shape
    staged = pltpu.VMEM((rows * width // HEAD_SIZE, HEAD_SIZE), F32)
    return loads.call(
        attention_kernel,
        "attention",
        tuple(map(far, (lengths, queries, cache, ids, route, residual, weight))),
        [ANYWHERE] * 7,
        (shaped((rows, width + 128 + residual.shape[1]), BF16), pltpu.VMEM(weight.shape, BF16)),
        pieces,
        scratch=[
            pltpu.SMEM(lengths.shape, jnp.int32),
            pltpu.VMEM(queries.shape, BF16),
            pltpu.VMEM(cache.shape, BF16),
            pltpu.VMEM(ids.shape, jnp.int32),
            pltpu.VMEM(route.shape, F32),
            pltpu.VMEM(residual.shape, BF16),
            staged,
            staged,
            DMA((7,)),
        ],
        cost=(140_000_000, 12_000_000, 65536),
    )


def fetch_kernel(after, mark):
    del after
    mark[...] = jnp.zeros_like(mark)


def fetch(loads, pieces, name, after):
    return loads.call(
        fetch_kernel, name, (after,), [ANYWHERE], (shaped((8, 128)),), pieces, limit=1
    )[0]


def projection_kernel(slot_far, b0, b1, b2, b3, weight, unused, out, routing, slot_of, kept, sem):
    del unused
    copy = pltpu.make_async_copy(slot_far, slot_of, sem)
    copy.start()
    blocks = (b0, b1, b2, b3)
    rows = b0.shape[0]
    width = weight.shape[0]
    everyone = SIDE * rows
    me = lax.axis_index("ep")
    held = jnp.concatenate([b[:, :width].astype(F32) for b in blocks], axis=0).astype(BF16)
    row = lax.broadcasted_iota(jnp.int32, (everyone, everyone), 0)
    column = lax.broadcasted_iota(jnp.int32, (everyone, everyone), 1)
    wanted = jnp.zeros((everyone, everyone), jnp.int32)
    for k, block in enumerate(blocks):
        span = pl.ds(pl.multiple_of((me ^ k) * rows, rows), rows)
        routing[span, :] = block[:, width : width + 128].astype(F32)
        kept[span, :] = block[:, width + 128 :].astype(F32)
    copy.wait()
    for r in range(everyone):
        slot = slot_of[r]
        wanted = jnp.where(row == r, ((slot // rows) ^ me) * rows + slot % rows, wanted)
    order = (wanted == column).astype(F32).astype(BF16)
    ordered = jnp.dot(order, held, preferred_element_type=F32).astype(BF16)
    own = (me == lax.axis_index("hd")).astype(F32)
    out[...] = jnp.dot(ordered, weight[...], preferred_element_type=F32) + own * kept[...]


def projection(loads, pieces, slot_of, blocks, weight, unused):
    everyone = SIDE * blocks[0].shape[0]
    wide = (everyone, weight.shape[1])
    return loads.call(
        projection_kernel,
        "projection",
        (far(slot_of), *blocks, weight, unused),
        [ANYWHERE] + [HERE] * 5 + [ANYWHERE],
        (shaped(wide), shaped((everyone, 128))),
        pieces,
        scratch=[pltpu.SMEM(slot_of.shape, jnp.int32), pltpu.VMEM(wide, F32), DMA],
        limit=6,
        cost=(140_000_000, 4_500_000, 0),
    )


def add_kernel(a, b, out):
    out[...] = a[...] + b[...]


def add(a, b):
    outs = (shaped(a.shape),)
    return kernel_call(add_kernel, "add", (a, b), [HERE] * 2, outs, cost=(a.size, a.size, 0))[0][0]


def stream_kernel(a, b, unused, stream, packed):
    del unused
    total = a[...] + b[...]
    stream[...] = total
    width = total.shape[1]
    packed[:, :width] = total.astype(BF16)
    squares = jnp.sum(total * total, axis=1, keepdims=True)
    lane = lax.broadcasted_iota(jnp.int32, (total.shape[0], 128), 1)
    parts = [part.astype(F32) for part in split3(jnp.broadcast_to(squares, lane.shape))]
    spread = jnp.where(lane == 0, parts[0], jnp.where(lane == 1, parts[1], parts[2]))
    packed[:, width:] = jnp.where(lane < 3, spread, 0.0).astype(BF16)


def streams(a, b, unused):
    rows, width = a.shape
    outs = (shaped(a.shape), shaped((rows, width + 128), BF16))
    return kernel_call(
        stream_kernel,
        "stream",
        (a, b, unused),
        [HERE, HERE, ANYWHERE],
        outs,
        cost=(a.size * 4, a.size * 4, 0),
    )[0]


def entry_kernel(k, n, packed, *refs):
    near, before, out = refs[:n], refs[n] if k else None, refs[-1]
    width = near[0].shape[2]
    turned = packed[:, :width].astype(F32).T.astype(BF16)
    at = 0
    for array in near:
        for e in range(array.shape[0]):
            part = jnp.dot(array[e], turned, preferred_element_type=F32)
            span = slice(at, at + part.shape[0])
            out[span, :] = before[span, :] + part if k else part
            at = span.stop


def entry_last_kernel(n, packed, *refs):
    near, (before, routing, p0, p1, p2, out) = refs[:n], refs[n:]
    hidden, width = near[0].shape[1:]
    rows = packed.shape[0]
    turned = packed[:, :width].astype(F32).T.astype(BF16)
    squares = jnp.zeros((rows, 128), F32)
    for block in (p0, p1, p2, packed):
        squares = squares + block[:, width:].astype(F32)
    mean = jnp.sum(squares.T, axis=0, keepdims=True) / (SIDE * width)
    scale = lax.rsqrt(mean + 1e-06)
    table = routing[...].T
    ids = table[0:TOPK, :]
    weight = table[TOPK : 2 * TOPK, :] + table[2 * TOPK : 3 * TOPK, :]
    weight = weight + table[3 * TOPK : 4 * TOPK, :]
    base = lax.axis_index("ep") * (before.shape[0] // hidden)
    number = 0
    pair = []
    for array in near:
        for e in range(array.shape[0]):
            at = number * hidden
            chosen = ids == (base + number).astype(F32)
            share = jnp.sum(jnp.where(chosen, weight, 0.0), axis=0, keepdims=True)
            part = jnp.dot(array[e], turned, preferred_element_type=F32)
            total = (before[at : at + hidden, :] + part) * scale
            active = (total / (1.0 + jnp.exp(-total))).astype(BF16).astype(F32) * share
            high = active.astype(BF16).astype(F32)
            pair.append(jnp.concatenate([high, active - high], axis=1))
            number += 1
            if len(pair) == 2:
                end = number * hidden
                both = jnp.concatenate(pair, axis=0)
                out[:, end - 2 * hidden : end] = both.T.astype(BF16)
                pair = []


def entries(loads, plan, packs, routing):
    count, hidden, width = loads.leave.shape
    rows = packs[0].shape[0]
    cost = (2 * rows * count * hidden * width // SIDE, 2 * count * hidden * width // SIDE, 0)
    total = None
    for k in range(SIDE):
        near = tuple(loads.near["entry", k])
        args = (packs[k], *near) + ((total,) if k else ())
        n = len(near)
        if k < SIDE - 1:
            body = functools.partial(entry_kernel, k, n)
            outs = (shaped((count * hidden, rows)),)
            aliases = {n + 1: 0} if k else None
        else:
            args += (routing, *packs[:-1])
            body = functools.partial(entry_last_kernel, n)
            outs = (shaped((2 * rows, count * hidden), BF16),)
            aliases = None
        (total,) = loads.call(
            body,
            f"entry{k}",
            args,
            [HERE] * len(args),
            outs,
            plan.get(f"entry{k}", ()),
            cost=cost,
            aliases=aliases,
        )
    return total


def leave_kernel(n, step, scaled, *refs):
    near, out = refs[:n], refs[-1]
    rows, count = out.shape
    for c in range(0, count, step):
        total = jnp.zeros((2 * rows, step), F32)
        at = 0
        for array in near:
            depth = array.shape[0] * array.shape[1]
            flat = array.reshape(depth, array.shape[2])
            total = total + jnp.dot(
                scaled[:, at : at + depth], flat[:, c : c + step], preferred_element_type=F32
            )
            at += depth
        out[:, c : c + step] = (total[:rows] + total[rows:]).astype(out.dtype)


def leaves(loads, pieces, name, other, dtype, scaled, unused):
    near = tuple(loads.near["leave", other])
    count, hidden, width = loads.leave.shape
    rows = scaled.shape[0] // 2
    return loads.call(
        functools.partial(leave_kernel, len(near), 1024),
        name,
        (scaled, *near, unused),
        [HERE] * (1 + len(near)) + [ANYWHERE],
        (shaped((rows, width // 2), dtype),),
        pieces,
        cost=(2 * rows * count * hidden * width, count * hidden * width, 0),
        limit=6,
    )[0]


def halve_kernel(mine, received, keep, send):
    width = keep.shape[1]
    core = lax.axis_index("hd") % 2
    for out, which in ((send, 1 - core), (keep, core)):
        columns = pl.ds(pl.multiple_of(which * width, width), width)
        out[...] = mine[:, columns] + received[:, columns].astype(F32)


def halve(mine, received):
    rows, width = mine.shape
    outs = (shaped((rows, width // 2)),) * 2
    cost = (mine.size, mine.size * 6, 0)
    return kernel_call(halve_kernel, "halve", (mine, received), [HERE] * 2, outs, cost=cost)[0]


def share_kernel(own, received, stream, o0, o1, o2, o3):
    rows = o0.shape[0]
    me = lax.axis_index("ep")
    here = (me == lax.axis_index("hd")).astype(F32)
    for k, out in enumerate((o0, o1, o2, o3)):
        span = pl.ds(pl.multiple_of((me ^ k) * rows, rows), rows)
        out[...] = own[span, :] + received[span, :] + here * stream[span, :]


def share(own, received, stream):
    rows, width = own.shape
    outs = (shaped((rows // SIDE, width)),) * SIDE
    cost = (own.size * 3, own.size * 16, 0)
    args = (own, received, stream)
    return kernel_call(share_kernel, "share", args, [HERE] * 3, outs, cost=cost)[0]


def plan_of(count):
    half, quarter = count // 2, count // 4
    cut = (count // 8, half, count * 3 // 8, count * 3 // 8)
    return {
        "attention": [("entry", 0, 0, half)],
        "fetch0": [("entry", 0, half, half), ("entry", 1, 0, count)],
        "projection": [("entry", 2, 0, half)],
        "fetch1": [("entry", 2, half, half), ("entry", 3, 0, half)],
        "entry0": [("entry", 3, half, half), ("leave", 1, 0, cut[0])],
        "entry1": [("leave", 1, cut[0], cut[2])],
        "entry2": [("leave", 1, cut[0] + cut[2], count - cut[0] - cut[2])],
        "entry3": [("leave", 0, 0, cut[3])],
        "leave1": [("leave", 0, cut[3], count - cut[3])],
    }


def square_body(
    residual,
    queries,
    key_value_cache,
    lengths,
    slot_of,
    out_weight,
    expert_ids,
    route_weight,
    in_weight,
    down_weight,
):
    rows = queries.shape[0]
    cache = key_value_cache.reshape(rows, 2 * CACHE_LENGTH, HEAD_SIZE)
    loads = Loads(jnp.swapaxes(in_weight, 1, 2), down_weight)
    plan = plan_of(down_weight.shape[0])
    attended, weight = attention(
        loads,
        plan["attention"],
        lengths,
        queries,
        cache,
        expert_ids,
        route_weight,
        residual,
        out_weight,
    )
    blocks = [attended] + [swap(attended, "ep", k) for k in (1, 2, 3)]
    mark = fetch(loads, plan["fetch0"], "fetch0", attended)
    partial_value, routing = projection(loads, plan["projection"], slot_of, blocks, weight, mark)
    pair = add(partial_value, swap(partial_value, "hd", 1))
    far_pair = swap(pair, "hd", 2)
    mark = fetch(loads, plan["fetch1"], "fetch1", pair)
    stream, packed = streams(pair, far_pair, mark)
    packs = [packed] + [swap(packed, "ep", k) for k in (1, 2, 3)]
    scaled = entries(loads, plan, packs, routing)
    theirs = leaves(loads, plan["leave1"], "leave1", 1, BF16, scaled, scaled)
    mine = leaves(loads, (), "leave0", 0, F32, scaled, theirs)
    keep, send = halve(mine, swap(theirs, "hd", 2))
    total, *others = share(keep, swap(send, "hd", 1), stream)
    for k, block in enumerate(others):
        total = total + swap(block, "ep", k + 1)
    return total.astype(BF16)


def expert_pass(block, in_weight, down_weight):
    local_count = in_weight.shape[0]
    senders = block.shape[0] // local_count
    slots = block.shape[1]
    width = block.shape[2]
    grouped = block.reshape(senders, local_count, slots, width)
    hidden = jnp.einsum("secd,edf->secf", grouped, in_weight, preferred_element_type=jnp.float32)
    hidden = jax.nn.silu(hidden).astype(jnp.bfloat16)
    output = jnp.einsum("secf,efd->secd", hidden, down_weight, preferred_element_type=jnp.float32)
    return output.reshape(senders * local_count, slots, width)


def body(
    residual,
    queries,
    key_value_cache,
    lengths,
    slot_of,
    out_weight,
    expert_ids,
    route_weight,
    in_weight,
    down_weight,
):
    rows_here = queries.shape[0]
    local_groups = key_value_cache.shape[3] // HEAD_SIZE
    heads_per_group = QUERY_HEADS // KEY_VALUE_HEADS
    query_head_rows = queries.reshape(rows_here, local_groups, heads_per_group, HEAD_SIZE)
    cached_key_rows = key_value_cache[:, :, 0].reshape(
        rows_here, CACHE_LENGTH, local_groups, HEAD_SIZE
    )
    cached_value_rows = key_value_cache[:, :, 1].reshape(
        rows_here, CACHE_LENGTH, local_groups, HEAD_SIZE
    )
    scores = jnp.einsum(
        "sagd,slad->sagl", query_head_rows, cached_key_rows, preferred_element_type=jnp.float32
    )
    scores = scores * (1.0 / math.sqrt(HEAD_SIZE))
    visible = (jnp.arange(CACHE_LENGTH)[None, :] < lengths[:, None])[:, None, None, :]
    scores = jnp.where(visible, scores, -1e30)
    highest = jnp.max(scores, axis=3, keepdims=True)
    raised = jnp.where(visible, jnp.exp(scores - highest), 0.0)
    weights = (raised / jnp.sum(raised, axis=3, keepdims=True)).astype(jnp.bfloat16)
    attended = jnp.einsum(
        "sagl,slad->sagd", weights, cached_value_rows, preferred_element_type=jnp.float32
    )
    attended = attended.astype(jnp.bfloat16).reshape(
        rows_here, local_groups * heads_per_group * HEAD_SIZE
    )
    partial_value = jnp.dot(
        lax.all_gather(attended, "ep", axis=0, tiled=True),
        out_weight,
        preferred_element_type=jnp.float32,
    )
    ordered = jnp.take(partial_value, slot_of, axis=0)
    moved = lax.all_to_all(ordered, "ep", split_axis=0, concat_axis=1, tiled=True)
    summed = lax.psum_scatter(moved, "hd", scatter_dimension=1, tiled=True)
    stream = residual.astype(jnp.float32) + summed
    squares = lax.psum(jnp.sum(stream * stream, axis=1), "hd")
    normed = (stream * lax.rsqrt(squares / D + 1e-06)[:, None]).astype(jnp.bfloat16)
    picked = expert_ids.reshape(-1)
    member = (picked[:, None] == jnp.arange(EXPERTS)[None, :]).astype(jnp.int32)
    earlier = jnp.cumsum(member, axis=0) - member
    position = jnp.sum(earlier * member, axis=1)
    target = picked * CAP + position
    placed = (target[:, None] == jnp.arange(EXPERTS * CAP)[None, :]).astype(jnp.float32)
    owner = (jnp.arange(picked.shape[0])[:, None] // TOPK == jnp.arange(rows_here)[None, :]).astype(
        jnp.float32
    )
    select_matrix = jnp.dot(placed.T, owner, precision=lax.Precision.HIGHEST).astype(jnp.bfloat16)
    mixing = jnp.dot(
        owner.T, placed * route_weight.reshape(-1)[:, None], precision=lax.Precision.HIGHEST
    )
    full_rows = lax.all_gather(normed, "hd", axis=1, tiled=True)
    outgoing = jnp.dot(select_matrix, full_rows, preferred_element_type=jnp.float32).astype(
        jnp.bfloat16
    )
    outgoing = outgoing.reshape(EXPERTS, CAP, full_rows.shape[1])
    results = expert_pass(
        lax.all_to_all(outgoing, "ep", split_axis=0, concat_axis=0, tiled=True),
        in_weight,
        down_weight,
    )
    share_width = residual.shape[1]
    shares = lax.psum_scatter(results.astype(jnp.bfloat16), "hd", scatter_dimension=2, tiled=True)
    returned = lax.all_to_all(shares, "ep", split_axis=0, concat_axis=0, tiled=True)
    flat_back = returned.reshape(EXPERTS * CAP, share_width).astype(jnp.float32)
    mixture = jnp.dot(mixing, flat_back, precision=lax.Precision.HIGHEST)
    return (stream + mixture).astype(jnp.bfloat16)


def solution(mesh):
    in_specs = (
        P(("groups", "ep"), "hd"),
        P(("groups", "ep"), "hd"),
        P(("groups", "ep"), None, None, "hd"),
        P(("groups", "ep")),
        P("groups"),
        P("hd", "ep"),
        P(("groups", "ep"), None),
        P(("groups", "ep"), None),
        P("ep", None, "hd"),
        P("ep", "hd", None),
    )
    out_specs = P(("groups", "ep"), "hd")
    chosen = square_body if mesh.shape["ep"] == mesh.shape["hd"] == SIDE else body
    return jax.shard_map(chosen, mesh=mesh, in_specs=in_specs, out_specs=out_specs, check_vma=False)
```

```python
import functools
import math

import jax
import jax.numpy as jnp
from jax import lax
from jax.experimental import pallas as pl
from jax.experimental.pallas import tpu as pltpu
from jax.sharding import PartitionSpec as P

D = 4096
QUERY_HEADS = 64
KEY_VALUE_HEADS = 4
HEAD_SIZE = 128
EXPERTS = 64
TOPK = 8
CAP = 2
CACHE_LENGTH = 256
SIDE = 4
BF16 = jnp.bfloat16
F32 = jnp.float32
MIB = 1 << 20
HERE = pl.BlockSpec(memory_space=pltpu.VMEM)
SCALARS = pl.BlockSpec(memory_space=pltpu.SMEM)
ANYWHERE = pl.BlockSpec(memory_space=pl.ANY)
DMA = pltpu.SemaphoreType.DMA


def swap(block, axis, k):
    return lax.ppermute(block, axis, [(i, i ^ k) for i in range(SIDE)])


def far(array):
    return pltpu.with_memory_space_constraint(array, pltpu.HBM)


def split3(value):
    high = value.astype(BF16)
    rest = value - high.astype(F32)
    middle = rest.astype(BF16)
    low = (rest - middle.astype(F32)).astype(BF16)
    return high, middle, low


def hosted(body, inputs, outputs, loads):
    n = len(loads)

    def kernel(*refs):
        sources = refs[inputs : inputs + n]
        targets = refs[inputs + n + outputs : inputs + n + outputs + n]
        ins, outs = refs[:inputs], refs[inputs + n : inputs + n + outputs]
        copies = []
        for i, (load, source, target) in enumerate(zip(loads, sources, targets)):
            _, first, count = load
            depth = target.shape[0]
            source = source.at[pl.ds(first * (depth // count), depth)]
            copies.append(pltpu.make_async_copy(source, target, refs[-1].at[i]))
        begin = lambda: [copy.start() for copy in copies]
        rest = refs[inputs + outputs + 2 * n : -1]
        if body is attention_kernel:
            body(*ins, *outs, *rest, begin)
        else:
            begin()

            @pl.when(lax.axis_index("ep") >= 0)
            def _():
                body(*ins, *outs, *rest)

        for copy in copies:
            copy.wait()

    return kernel


def kernel_call(
    body, name, args, specs, outs, scratch=(), loads=(), limit=4, cost=(0, 0, 0), aliases=None
):
    targets = [
        pltpu.VMEM((count * array.shape[1], array.shape[2]), BF16) for array, _, count in loads
    ]
    flops, bytes_accessed, transcendentals = cost
    bytes_accessed += sum(2 * math.prod(target.shape) for target in targets)
    results = pl.pallas_call(
        hosted(body, len(args), len(outs), loads) if loads else body,
        out_shape=(*outs, *targets),
        in_specs=[*specs] + [ANYWHERE] * len(loads),
        out_specs=(HERE,) * (len(outs) + len(targets)),
        scratch_shapes=[*scratch] + ([DMA((len(loads),))] if loads else []),
        input_output_aliases=aliases or {},
        compiler_params=pltpu.CompilerParams(vmem_limit_bytes=limit * MIB),
        cost_estimate=pl.CostEstimate(
            flops=flops, bytes_accessed=bytes_accessed, transcendentals=transcendentals
        ),
        name=name,
    )(*args, *(far(array.reshape(-1, array.shape[2])) for array, *_ in loads))
    return results[: len(outs)], results[len(outs) :]


class Loads:
    def __init__(self, entry, leave):
        self.entry, self.leave = entry, leave
        self.near = {"entry": [], "leave": []}

    def call(self, body, name, args, specs, outs, pieces=(), **more):
        loads = tuple((getattr(self, what), first, count) for what, first, count in pieces)
        results, arrays = kernel_call(body, name, args, specs, outs, loads=loads, **more)
        for (what, first, count), array in zip(pieces, arrays):
            self.near[what].append((first, count, array))
        return results

    def pieces(self, what, first, last):
        chosen = [p for p in self.near[what] if first <= p[0] and p[0] + p[1] <= last]
        assert sum(p[1] for p in chosen) == last - first
        return tuple(p[2] for p in sorted(chosen, key=lambda p: p[0]))


def shaped(shape, dtype=F32):
    return jax.ShapeDtypeStruct(shape, dtype)


def attention_kernel(
    lengths_far,
    queries_far,
    cache_far,
    ids_far,
    route_far,
    residual_far,
    weight_far,
    slot_far,
    out,
    weight,
    order,
    lengths,
    queries,
    cache,
    ids,
    route,
    residual,
    slot_of,
    staged,
    gathered,
    sems,
    begin,
):
    pairs = (
        (lengths_far, lengths),
        (queries_far, queries),
        (cache_far, cache),
        (ids_far, ids),
        (route_far, route),
        (residual_far, residual),
        (slot_far, slot_of),
        (weight_far, weight),
    )
    copies = [pltpu.make_async_copy(*pair, sems.at[i]) for i, pair in enumerate(pairs)]
    for copy in copies:
        copy.start()
    begin()
    rows = queries.shape[0]
    heads = queries.shape[1] // HEAD_SIZE
    everyone = rows * heads
    copies[1].wait()
    for h in range(heads):
        lanes = slice(h * HEAD_SIZE, (h + 1) * HEAD_SIZE)
        staged[pl.ds(h, rows, stride=heads), :] = queries[:, lanes].astype(F32)
    turned = staged[...].T.astype(BF16)
    copies[0].wait()
    slot = lax.broadcasted_iota(jnp.int32, (1, everyone), 1) // heads
    limit = jnp.zeros((1, everyone), jnp.int32)
    for s in range(rows):
        limit = jnp.where(slot == s, 2 * lengths[s], limit)
    place = lax.broadcasted_iota(jnp.int32, (2 * CACHE_LENGTH, everyone), 0)
    visible = jnp.logical_and(place % 2 == 0, place < limit)
    width = heads * HEAD_SIZE
    copies[3].wait()
    copies[4].wait()
    row = lax.broadcasted_iota(jnp.int32, (TOPK, 128), 0)
    lane = lax.broadcasted_iota(jnp.int32, (TOPK, 128), 1)
    total = jnp.zeros((rows, 128), F32)
    for j, part in enumerate((ids[...].astype(F32).astype(BF16), *split3(route[...]))):
        spread = (lane == row + j * TOPK).astype(F32).astype(BF16)
        total = total + jnp.dot(part, spread, preferred_element_type=F32)
    out[:, width : width + 128] = total.astype(BF16)
    copies[5].wait()
    out[:, width + 128 :] = residual[...]
    copies[6].wait()
    me = lax.axis_index("ep")
    row = lax.broadcasted_iota(jnp.int32, order.shape, 0)
    wanted = jnp.zeros(order.shape, jnp.int32)
    for r in range(order.shape[0]):
        held = slot_of[r]
        wanted = jnp.where(row == r, ((held // rows) ^ me) * rows + held % rows, wanted)
    column = lax.broadcasted_iota(jnp.int32, order.shape, 1)
    order[...] = (wanted == column).astype(F32).astype(BF16)
    copies[2].wait()
    scores = jnp.dot(cache[0], turned, preferred_element_type=F32)
    for s in range(1, rows):
        more = jnp.dot(cache[s], turned, preferred_element_type=F32)
        scores = jnp.where(slot == s, more, scores)
    scores = jnp.where(visible, scores * (1.0 / math.sqrt(HEAD_SIZE)), -1e30)
    raised = jnp.where(visible, jnp.exp(scores - jnp.max(scores, axis=0, keepdims=True)), 0.0)
    weights = raised / jnp.sum(raised, axis=0, keepdims=True)
    moved = pltpu.roll(weights, 1, 0).T.astype(BF16)
    for s in range(rows):
        span = slice(s * heads, (s + 1) * heads)
        gathered[span, :] = jnp.dot(moved[span], cache[s], preferred_element_type=F32)
    for h in range(heads):
        lanes = slice(h * HEAD_SIZE, (h + 1) * HEAD_SIZE)
        out[:, lanes] = gathered[pl.ds(h, rows, stride=heads), :].astype(BF16)
    copies[7].wait()


def attention(loads, pieces, lengths, queries, cache, ids, route, residual, weight, slot_of):
    rows, width = queries.shape
    staged = pltpu.VMEM((rows * width // HEAD_SIZE, HEAD_SIZE), F32)
    return loads.call(
        attention_kernel,
        "attention",
        tuple(map(far, (lengths, queries, cache, ids, route, residual, weight, slot_of))),
        [ANYWHERE] * 8,
        (
            shaped((rows, width + 128 + residual.shape[1]), BF16),
            pltpu.VMEM(weight.shape, BF16),
            shaped((slot_of.shape[0], slot_of.shape[0]), BF16),
        ),
        pieces,
        scratch=[
            pltpu.SMEM(lengths.shape, jnp.int32),
            pltpu.VMEM(queries.shape, BF16),
            pltpu.VMEM(cache.shape, BF16),
            pltpu.VMEM(ids.shape, jnp.int32),
            pltpu.VMEM(route.shape, F32),
            pltpu.VMEM(residual.shape, BF16),
            pltpu.SMEM(slot_of.shape, jnp.int32),
            staged,
            staged,
            DMA((8,)),
        ],
        cost=(140_000_000, 12_000_000, 65536),
    )


def fetch_kernel(after, mark):
    del after
    mark[...] = jnp.zeros_like(mark)


def fetch(loads, pieces, name, after):
    return loads.call(
        fetch_kernel, name, (after,), [ANYWHERE], (shaped((8, 128)),), pieces, limit=1
    )[0]


def projection_kernel(order, b0, b1, b2, b3, weight, unused, out, routing, kept):
    del unused
    blocks = (b0, b1, b2, b3)
    rows = b0.shape[0]
    width = weight.shape[0]
    me = lax.axis_index("ep")
    for k, block in enumerate(blocks):
        span = pl.ds(pl.multiple_of((me ^ k) * rows, rows), rows)
        routing[span, :] = block[:, width : width + 128].astype(F32)
        kept[span, :] = block[:, width + 128 :].astype(F32)
    held = jnp.concatenate([b[:, :width].astype(F32) for b in blocks], axis=0).astype(BF16)
    ordered = jnp.dot(order[...], held, preferred_element_type=F32).astype(BF16)
    own = (me == lax.axis_index("hd")).astype(F32)
    out[...] = jnp.dot(ordered, weight[...], preferred_element_type=F32) + own * kept[...]


def projection(loads, pieces, order, blocks, weight, unused):
    everyone = SIDE * blocks[0].shape[0]
    wide = (everyone, weight.shape[1])
    return loads.call(
        projection_kernel,
        "projection",
        (order, *blocks, weight, unused),
        [HERE] * 6 + [ANYWHERE],
        (shaped(wide), shaped((everyone, 128))),
        pieces,
        scratch=[pltpu.VMEM(wide, F32)],
        limit=6,
        cost=(140_000_000, 4_500_000, 0),
    )


def add_kernel(a, b, out):
    out[...] = a[...] + b[...]


def add(a, b):
    outs = (shaped(a.shape),)
    return kernel_call(add_kernel, "add", (a, b), [HERE] * 2, outs, cost=(a.size, a.size, 0))[0][0]


def stream_kernel(a, b, unused, stream, packed):
    del unused
    total = a[...] + b[...]
    stream[...] = total
    width = total.shape[1]
    packed[:, :width] = total.astype(BF16)
    squares = jnp.sum(total * total, axis=1, keepdims=True)
    lane = lax.broadcasted_iota(jnp.int32, (total.shape[0], 128), 1)
    parts = [part.astype(F32) for part in split3(jnp.broadcast_to(squares, lane.shape))]
    spread = jnp.where(lane == 0, parts[0], jnp.where(lane == 1, parts[1], parts[2]))
    packed[:, width:] = jnp.where(lane < 3, spread, 0.0).astype(BF16)


def streams(a, b, unused):
    rows, width = a.shape
    outs = (shaped(a.shape), shaped((rows, width + 128), BF16))
    return kernel_call(
        stream_kernel,
        "stream",
        (a, b, unused),
        [HERE, HERE, ANYWHERE],
        outs,
        cost=(a.size * 4, a.size * 4, 0),
    )[0]


def entry_kernel(base, first, n, hidden, *refs):
    packs, routing, near, rest = refs[:SIDE], refs[SIDE], refs[SIDE + 1 : SIDE + 1 + n], refs[SIDE + 1 + n :]
    rows, width = packs[0].shape
    width = width - 128
    me = lax.axis_index("ep")
    if first:
        _, out, turned = rest
        for k, packed in enumerate(packs):
            span = pl.ds(pl.multiple_of((me ^ k) * width, width), width)
            turned[span, :] = packed[:, :width].astype(F32).T.astype(BF16)
    else:
        turned, out = rest
    squares = jnp.zeros((rows, 128), F32)
    for packed in packs:
        squares = squares + packed[:, width:].astype(F32)
    mean = jnp.sum(squares.T, axis=0, keepdims=True) / (SIDE * width)
    scale = lax.rsqrt(mean + 1e-06)
    table = routing[...].T
    ids = table[0:TOPK, :]
    weight = table[TOPK : 2 * TOPK, :] + table[2 * TOPK : 3 * TOPK, :]
    weight = weight + table[3 * TOPK : 4 * TOPK, :]
    count = EXPERTS // SIDE
    number = 0
    pair = []
    for array in near:
        for start in range(0, array.shape[0], hidden):
            chosen = ids == (me * count + base + number).astype(F32)
            share = jnp.sum(jnp.where(chosen, weight, 0.0), axis=0, keepdims=True)
            total = scale * jnp.dot(
                array[start : start + hidden, :], turned[...], preferred_element_type=F32
            )
            active = (total / (1.0 + jnp.exp(-total))).astype(BF16).astype(F32) * share
            high = active.astype(BF16).astype(F32)
            pair.append(jnp.concatenate([high, active - high], axis=1))
            number += 1
            if len(pair) == 2:
                end = number * hidden
                both = jnp.concatenate(pair, axis=0)
                out[:, end - 2 * hidden : end] = both.T.astype(BF16)
                pair = []


def entries(loads, pieces, base, last, packs, routing, mark=None, turned=None):
    _, hidden, width = loads.leave.shape
    count = last - base
    rows = packs[0].shape[0]
    near = loads.pieces("entry", base, last)
    first = turned is None
    args = (*packs, routing, *near) + ((mark,) if first else (turned,))
    outs = (shaped((2 * rows, count * hidden), BF16),)
    if first:
        outs += (shaped((width, rows), BF16),)
    return loads.call(
        functools.partial(entry_kernel, base, first, len(near), hidden),
        f"entry{base}",
        args,
        [HERE] * len(args),
        outs,
        pieces,
        cost=(2 * rows * count * hidden * width, 2 * count * hidden * width, 0),
    )


def leave_kernel(other, n, m, step, *refs):
    scaled, near, out = refs[:m], refs[m : m + n], refs[-1]
    rows, half = out.shape
    chip = (lax.axis_index("hd") // 2) ^ other
    for c in range(0, half, step):
        columns = pl.ds(pl.multiple_of(chip * half + c, step), step)
        total = jnp.zeros((2 * rows, step), F32)
        which, at = 0, 0
        for array in near:
            done = 0
            while done < array.shape[0]:
                depth = min(array.shape[0] - done, scaled[which].shape[1] - at)
                total = total + jnp.dot(
                    scaled[which][:, at : at + depth],
                    array[done : done + depth, columns],
                    preferred_element_type=F32,
                )
                done, at = done + depth, at + depth
                if at == scaled[which].shape[1]:
                    which, at = which + 1, 0
        out[:, c : c + step] = (total[:rows] + total[rows:]).astype(out.dtype)


def leaves(loads, name, other, dtype, scaled, unused):
    count, hidden, width = loads.leave.shape
    near = loads.pieces("leave", 0, count)
    rows = scaled[0].shape[0] // 2
    return kernel_call(
        functools.partial(leave_kernel, other, len(near), len(scaled), 1024),
        name,
        (*scaled, *near, unused),
        [HERE] * (len(scaled) + len(near)) + [ANYWHERE],
        (shaped((rows, width // 2), dtype),),
        cost=(2 * rows * count * hidden * width, count * hidden * width, 0),
        limit=6,
    )[0][0]


def halve_kernel(mine, received, keep, send):
    width = keep.shape[1]
    core = lax.axis_index("hd") % 2
    for out, which in ((send, 1 - core), (keep, core)):
        columns = pl.ds(pl.multiple_of(which * width, width), width)
        out[...] = mine[:, columns] + received[:, columns].astype(F32)


def halve(mine, received):
    rows, width = mine.shape
    outs = (shaped((rows, width // 2)),) * 2
    cost = (mine.size, mine.size * 6, 0)
    return kernel_call(halve_kernel, "halve", (mine, received), [HERE] * 2, outs, cost=cost)[0]


def share_kernel(own, received, stream, o0, o1, o2, o3):
    rows = o0.shape[0]
    me = lax.axis_index("ep")
    here = (me == lax.axis_index("hd")).astype(F32)
    for k, out in enumerate((o0, o1, o2, o3)):
        span = pl.ds(pl.multiple_of((me ^ k) * rows, rows), rows)
        out[...] = own[span, :] + received[span, :] + here * stream[span, :]


def share(own, received, stream):
    rows, width = own.shape
    outs = (shaped((rows // SIDE, width)),) * SIDE
    cost = (own.size * 3, own.size * 16, 0)
    args = (own, received, stream)
    return kernel_call(share_kernel, "share", args, [HERE] * 3, outs, cost=cost)[0]


PLAN = {
    "attention": [("entry", 0, 2)],
    "fetch0": [("entry", 2, 6), ("entry", 8, 2)],
    "projection": [],
    "fetch1": [("entry", 10, 6)],
    "fetch2": [("leave", 0, 5)],
    "entry0": [("leave", 5, 6)],
    "entry8": [("leave", 11, 5)],
}


def square_body(
    residual,
    queries,
    key_value_cache,
    lengths,
    slot_of,
    out_weight,
    expert_ids,
    route_weight,
    in_weight,
    down_weight,
):
    rows = queries.shape[0]
    cache = key_value_cache.reshape(rows, 2 * CACHE_LENGTH, HEAD_SIZE)
    loads = Loads(jnp.swapaxes(in_weight, 1, 2), down_weight)
    plan = PLAN
    attended, weight, order = attention(
        loads,
        plan["attention"],
        lengths,
        queries,
        cache,
        expert_ids,
        route_weight,
        residual,
        out_weight,
        slot_of,
    )
    blocks = [attended] + [swap(attended, "ep", k) for k in (1, 2, 3)]
    mark = fetch(loads, plan["fetch0"], "fetch0", attended)
    partial_value, routing = projection(loads, plan["projection"], order, blocks, weight, mark)
    pair = add(partial_value, swap(partial_value, "hd", 1))
    far_pair = swap(pair, "hd", 2)
    mark = fetch(loads, plan["fetch1"], "fetch1", pair)
    stream, packed = streams(pair, far_pair, mark)
    packs = [packed] + [swap(packed, "ep", k) for k in (1, 2, 3)]
    mark = fetch(loads, plan["fetch2"], "fetch2", packed)
    scaled, turned = entries(loads, plan["entry0"], 0, 8, packs, routing, mark)
    (more,) = entries(loads, plan["entry8"], 8, 16, packs, routing, turned=turned)
    scaled = (scaled, more)
    theirs = leaves(loads, "leave1", 1, BF16, scaled, more)
    mine = leaves(loads, "leave0", 0, F32, scaled, theirs)
    keep, send = halve(mine, swap(theirs, "hd", 2))
    total, *others = share(keep, swap(send, "hd", 1), stream)
    for k in (3, 2, 1):
        total = total + swap(others[k - 1], "ep", k)
    return total.astype(BF16)


def expert_pass(block, in_weight, down_weight):
    local_count = in_weight.shape[0]
    senders = block.shape[0] // local_count
    slots = block.shape[1]
    width = block.shape[2]
    grouped = block.reshape(senders, local_count, slots, width)
    hidden = jnp.einsum("secd,edf->secf", grouped, in_weight, preferred_element_type=jnp.float32)
    hidden = jax.nn.silu(hidden).astype(jnp.bfloat16)
    output = jnp.einsum("secf,efd->secd", hidden, down_weight, preferred_element_type=jnp.float32)
    return output.reshape(senders * local_count, slots, width)


def body(
    residual,
    queries,
    key_value_cache,
    lengths,
    slot_of,
    out_weight,
    expert_ids,
    route_weight,
    in_weight,
    down_weight,
):
    rows_here = queries.shape[0]
    local_groups = key_value_cache.shape[3] // HEAD_SIZE
    heads_per_group = QUERY_HEADS // KEY_VALUE_HEADS
    query_head_rows = queries.reshape(rows_here, local_groups, heads_per_group, HEAD_SIZE)
    cached_key_rows = key_value_cache[:, :, 0].reshape(
        rows_here, CACHE_LENGTH, local_groups, HEAD_SIZE
    )
    cached_value_rows = key_value_cache[:, :, 1].reshape(
        rows_here, CACHE_LENGTH, local_groups, HEAD_SIZE
    )
    scores = jnp.einsum(
        "sagd,slad->sagl", query_head_rows, cached_key_rows, preferred_element_type=jnp.float32
    )
    scores = scores * (1.0 / math.sqrt(HEAD_SIZE))
    visible = (jnp.arange(CACHE_LENGTH)[None, :] < lengths[:, None])[:, None, None, :]
    scores = jnp.where(visible, scores, -1e30)
    highest = jnp.max(scores, axis=3, keepdims=True)
    raised = jnp.where(visible, jnp.exp(scores - highest), 0.0)
    weights = (raised / jnp.sum(raised, axis=3, keepdims=True)).astype(jnp.bfloat16)
    attended = jnp.einsum(
        "sagl,slad->sagd", weights, cached_value_rows, preferred_element_type=jnp.float32
    )
    attended = attended.astype(jnp.bfloat16).reshape(
        rows_here, local_groups * heads_per_group * HEAD_SIZE
    )
    partial_value = jnp.dot(
        lax.all_gather(attended, "ep", axis=0, tiled=True),
        out_weight,
        preferred_element_type=jnp.float32,
    )
    ordered = jnp.take(partial_value, slot_of, axis=0)
    moved = lax.all_to_all(ordered, "ep", split_axis=0, concat_axis=1, tiled=True)
    summed = lax.psum_scatter(moved, "hd", scatter_dimension=1, tiled=True)
    stream = residual.astype(jnp.float32) + summed
    squares = lax.psum(jnp.sum(stream * stream, axis=1), "hd")
    normed = (stream * lax.rsqrt(squares / D + 1e-06)[:, None]).astype(jnp.bfloat16)
    picked = expert_ids.reshape(-1)
    member = (picked[:, None] == jnp.arange(EXPERTS)[None, :]).astype(jnp.int32)
    earlier = jnp.cumsum(member, axis=0) - member
    position = jnp.sum(earlier * member, axis=1)
    target = picked * CAP + position
    placed = (target[:, None] == jnp.arange(EXPERTS * CAP)[None, :]).astype(jnp.float32)
    owner = (jnp.arange(picked.shape[0])[:, None] // TOPK == jnp.arange(rows_here)[None, :]).astype(
        jnp.float32
    )
    select_matrix = jnp.dot(placed.T, owner, precision=lax.Precision.HIGHEST).astype(jnp.bfloat16)
    mixing = jnp.dot(
        owner.T, placed * route_weight.reshape(-1)[:, None], precision=lax.Precision.HIGHEST
    )
    full_rows = lax.all_gather(normed, "hd", axis=1, tiled=True)
    outgoing = jnp.dot(select_matrix, full_rows, preferred_element_type=jnp.float32).astype(
        jnp.bfloat16
    )
    outgoing = outgoing.reshape(EXPERTS, CAP, full_rows.shape[1])
    results = expert_pass(
        lax.all_to_all(outgoing, "ep", split_axis=0, concat_axis=0, tiled=True),
        in_weight,
        down_weight,
    )
    share_width = residual.shape[1]
    shares = lax.psum_scatter(results.astype(jnp.bfloat16), "hd", scatter_dimension=2, tiled=True)
    returned = lax.all_to_all(shares, "ep", split_axis=0, concat_axis=0, tiled=True)
    flat_back = returned.reshape(EXPERTS * CAP, share_width).astype(jnp.float32)
    mixture = jnp.dot(mixing, flat_back, precision=lax.Precision.HIGHEST)
    return (stream + mixture).astype(jnp.bfloat16)


def solution(mesh):
    in_specs = (
        P(("groups", "ep"), "hd"),
        P(("groups", "ep"), "hd"),
        P(("groups", "ep"), None, None, "hd"),
        P(("groups", "ep")),
        P("groups"),
        P("hd", "ep"),
        P(("groups", "ep"), None),
        P(("groups", "ep"), None),
        P("ep", None, "hd"),
        P("ep", "hd", None),
    )
    out_specs = P(("groups", "ep"), "hd")
    chosen = square_body if mesh.shape["ep"] == mesh.shape["hd"] == SIDE else body
    return jax.shard_map(chosen, mesh=mesh, in_specs=in_specs, out_specs=out_specs, check_vma=False)
```

```python
import functools
import math

import jax
import jax.numpy as jnp
from jax import lax
from jax.experimental import pallas as pl
from jax.experimental.pallas import tpu as pltpu
from jax.sharding import PartitionSpec as P

D = 4096
QUERY_HEADS = 64
KEY_VALUE_HEADS = 4
HEAD_SIZE = 128
EXPERTS = 64
TOPK = 8
CAP = 2
CACHE_LENGTH = 256
SIDE = 4
BF16 = jnp.bfloat16
F32 = jnp.float32
MIB = 1 << 20
HERE = pl.BlockSpec(memory_space=pltpu.VMEM)
SCALARS = pl.BlockSpec(memory_space=pltpu.SMEM)
ANYWHERE = pl.BlockSpec(memory_space=pl.ANY)
DMA = pltpu.SemaphoreType.DMA


def swap(block, axis, k):
    return lax.ppermute(block, axis, [(i, i ^ k) for i in range(SIDE)])


def far(array):
    return pltpu.with_memory_space_constraint(array, pltpu.HBM)


def split3(value):
    high = value.astype(BF16)
    rest = value - high.astype(F32)
    middle = rest.astype(BF16)
    low = (rest - middle.astype(F32)).astype(BF16)
    return high, middle, low


def hosted(body, inputs, outputs, loads):
    n = len(loads)

    def kernel(*refs):
        sources = refs[inputs : inputs + n]
        targets = refs[inputs + n + outputs : inputs + n + outputs + n]
        ins, outs = refs[:inputs], refs[inputs + n : inputs + n + outputs]
        copies = []
        for i, (load, source, target) in enumerate(zip(loads, sources, targets)):
            _, first, count, other = load
            depth, width = target.shape
            rows = pl.ds(first * (depth // count), depth)
            if other is None:
                source = source.at[rows]
            else:
                chip = (lax.axis_index("hd") // 2) ^ other
                source = source.at[rows, pl.ds(pl.multiple_of(chip * width, width), width)]
            copies.append(pltpu.make_async_copy(source, target, refs[-1].at[i]))
        begin = lambda: [copy.start() for copy in copies]
        rest = refs[inputs + outputs + 2 * n : -1]
        if body is attention_kernel:
            body(*ins, *outs, *rest, begin)
        else:
            begin()

            @pl.when(lax.axis_index("ep") >= 0)
            def _():
                body(*ins, *outs, *rest)

        for copy in copies:
            copy.wait()

    return kernel


def kernel_call(
    body, name, args, specs, outs, scratch=(), loads=(), limit=4, cost=(0, 0, 0), aliases=None
):
    targets = [
        pltpu.VMEM((count * array.shape[1], array.shape[2] // (1 if other is None else 2)), BF16)
        for array, _, count, other in loads
    ]
    flops, bytes_accessed, transcendentals = cost
    bytes_accessed += sum(2 * math.prod(target.shape) for target in targets)
    results = pl.pallas_call(
        hosted(body, len(args), len(outs), loads) if loads else body,
        out_shape=(*outs, *targets),
        in_specs=[*specs] + [ANYWHERE] * len(loads),
        out_specs=(HERE,) * (len(outs) + len(targets)),
        scratch_shapes=[*scratch] + ([DMA((len(loads),))] if loads else []),
        input_output_aliases=aliases or {},
        compiler_params=pltpu.CompilerParams(vmem_limit_bytes=limit * MIB),
        cost_estimate=pl.CostEstimate(
            flops=flops, bytes_accessed=bytes_accessed, transcendentals=transcendentals
        ),
        name=name,
    )(*args, *(far(array.reshape(-1, array.shape[2])) for array, *_ in loads))
    return results[: len(outs)], results[len(outs) :]


class Loads:
    def __init__(self, entry, leave):
        self.entry, self.leave = entry, leave
        self.near = {"entry": [], "leave": [], "away": [], "here": []}

    def call(self, body, name, args, specs, outs, pieces=(), **more):
        half = {"away": 1, "here": 0}
        loads = tuple(
            (self.entry if what == "entry" else self.leave, first, count, half.get(what))
            for what, first, count in pieces
        )
        results, arrays = kernel_call(body, name, args, specs, outs, loads=loads, **more)
        for (what, first, count), array in zip(pieces, arrays):
            self.near[what].append((first, count, array))
        return results

    def pieces(self, first, last, *kinds):
        held = sum((self.near[what] for what in kinds), [])
        chosen = [p for p in held if first <= p[0] and p[0] + p[1] <= last]
        assert sum(p[1] for p in chosen) == last - first
        return tuple(p[2] for p in sorted(chosen, key=lambda p: p[0]))


def shaped(shape, dtype=F32):
    return jax.ShapeDtypeStruct(shape, dtype)


def attention_kernel(
    lengths_far,
    queries_far,
    cache_far,
    ids_far,
    route_far,
    residual_far,
    weight_far,
    slot_far,
    out,
    weight,
    order,
    lengths,
    queries,
    cache,
    ids,
    route,
    residual,
    slot_of,
    staged,
    gathered,
    sems,
    begin,
):
    pairs = (
        (lengths_far, lengths),
        (queries_far, queries),
        (cache_far, cache),
        (ids_far, ids),
        (route_far, route),
        (residual_far, residual),
        (slot_far, slot_of),
        (weight_far, weight),
    )
    copies = [pltpu.make_async_copy(*pair, sems.at[i]) for i, pair in enumerate(pairs)]
    for copy in copies:
        copy.start()
    begin()
    rows = queries.shape[0]
    heads = queries.shape[1] // HEAD_SIZE
    everyone = rows * heads
    copies[1].wait()
    for h in range(heads):
        lanes = slice(h * HEAD_SIZE, (h + 1) * HEAD_SIZE)
        staged[pl.ds(h, rows, stride=heads), :] = queries[:, lanes].astype(F32)
    turned = staged[...].T.astype(BF16)
    copies[0].wait()
    slot = lax.broadcasted_iota(jnp.int32, (1, everyone), 1) // heads
    limit = jnp.zeros((1, everyone), jnp.int32)
    for s in range(rows):
        limit = jnp.where(slot == s, 2 * lengths[s], limit)
    place = lax.broadcasted_iota(jnp.int32, (2 * CACHE_LENGTH, everyone), 0)
    visible = jnp.logical_and(place % 2 == 0, place < limit)
    width = heads * HEAD_SIZE
    copies[3].wait()
    copies[4].wait()
    row = lax.broadcasted_iota(jnp.int32, (TOPK, 128), 0)
    lane = lax.broadcasted_iota(jnp.int32, (TOPK, 128), 1)
    total = jnp.zeros((rows, 128), F32)
    for j, part in enumerate((ids[...].astype(F32).astype(BF16), *split3(route[...]))):
        spread = (lane == row + j * TOPK).astype(F32).astype(BF16)
        total = total + jnp.dot(part, spread, preferred_element_type=F32)
    out[:, width : width + 128] = total.astype(BF16)
    copies[5].wait()
    out[:, width + 128 :] = residual[...]
    copies[6].wait()
    me = lax.axis_index("ep")
    row = lax.broadcasted_iota(jnp.int32, order.shape, 0)
    wanted = jnp.zeros(order.shape, jnp.int32)
    for r in range(order.shape[0]):
        held = slot_of[r]
        wanted = jnp.where(row == r, ((held // rows) ^ me) * rows + held % rows, wanted)
    column = lax.broadcasted_iota(jnp.int32, order.shape, 1)
    order[...] = (wanted == column).astype(F32).astype(BF16)
    copies[2].wait()
    scores = jnp.dot(cache[0], turned, preferred_element_type=F32)
    for s in range(1, rows):
        more = jnp.dot(cache[s], turned, preferred_element_type=F32)
        scores = jnp.where(slot == s, more, scores)
    scores = jnp.where(visible, scores * (1.0 / math.sqrt(HEAD_SIZE)), -1e30)
    raised = jnp.where(visible, jnp.exp(scores - jnp.max(scores, axis=0, keepdims=True)), 0.0)
    weights = raised / jnp.sum(raised, axis=0, keepdims=True)
    moved = pltpu.roll(weights, 1, 0).T.astype(BF16)
    for s in range(rows):
        span = slice(s * heads, (s + 1) * heads)
        gathered[span, :] = jnp.dot(moved[span], cache[s], preferred_element_type=F32)
    for h in range(heads):
        lanes = slice(h * HEAD_SIZE, (h + 1) * HEAD_SIZE)
        out[:, lanes] = gathered[pl.ds(h, rows, stride=heads), :].astype(BF16)
    copies[7].wait()


def attention(loads, pieces, lengths, queries, cache, ids, route, residual, weight, slot_of):
    rows, width = queries.shape
    staged = pltpu.VMEM((rows * width // HEAD_SIZE, HEAD_SIZE), F32)
    return loads.call(
        attention_kernel,
        "attention",
        tuple(map(far, (lengths, queries, cache, ids, route, residual, weight, slot_of))),
        [ANYWHERE] * 8,
        (
            shaped((rows, width + 128 + residual.shape[1]), BF16),
            pltpu.VMEM(weight.shape, BF16),
            shaped((slot_of.shape[0], slot_of.shape[0]), BF16),
        ),
        pieces,
        scratch=[
            pltpu.SMEM(lengths.shape, jnp.int32),
            pltpu.VMEM(queries.shape, BF16),
            pltpu.VMEM(cache.shape, BF16),
            pltpu.VMEM(ids.shape, jnp.int32),
            pltpu.VMEM(route.shape, F32),
            pltpu.VMEM(residual.shape, BF16),
            pltpu.SMEM(slot_of.shape, jnp.int32),
            staged,
            staged,
            DMA((8,)),
        ],
        cost=(140_000_000, 12_000_000, 65536),
    )


def fetch_kernel(after, mark):
    del after
    mark[...] = jnp.zeros_like(mark)


def fetch(loads, pieces, name, after):
    return loads.call(
        fetch_kernel, name, (after,), [ANYWHERE], (shaped((8, 128)),), pieces, limit=1
    )[0]


def projection_kernel(order, b0, b1, b2, b3, weight, unused, out, routing, kept):
    del unused
    blocks = (b0, b1, b2, b3)
    rows = b0.shape[0]
    width = weight.shape[0]
    me = lax.axis_index("ep")
    for k, block in enumerate(blocks):
        span = pl.ds(pl.multiple_of((me ^ k) * rows, rows), rows)
        routing[span, :] = block[:, width : width + 128].astype(F32)
        kept[span, :] = block[:, width + 128 :].astype(F32)
    held = jnp.concatenate([b[:, :width].astype(F32) for b in blocks], axis=0).astype(BF16)
    ordered = jnp.dot(order[...], held, preferred_element_type=F32).astype(BF16)
    own = (me == lax.axis_index("hd")).astype(F32)
    out[...] = jnp.dot(ordered, weight[...], preferred_element_type=F32) + own * kept[...]


def projection(loads, pieces, order, blocks, weight, unused):
    everyone = SIDE * blocks[0].shape[0]
    wide = (everyone, weight.shape[1])
    return loads.call(
        projection_kernel,
        "projection",
        (order, *blocks, weight, unused),
        [HERE] * 6 + [ANYWHERE],
        (shaped(wide), shaped((everyone, 128))),
        pieces,
        scratch=[pltpu.VMEM(wide, F32)],
        limit=6,
        cost=(140_000_000, 4_500_000, 0),
    )


def add_kernel(a, b, out):
    out[...] = a[...] + b[...]


def add(a, b):
    outs = (shaped(a.shape),)
    return kernel_call(add_kernel, "add", (a, b), [HERE] * 2, outs, cost=(a.size, a.size, 0))[0][0]


def stream_kernel(a, b, unused, stream, packed):
    del unused
    total = a[...] + b[...]
    stream[...] = total
    width = total.shape[1]
    packed[:, :width] = total.astype(BF16)
    squares = jnp.sum(total * total, axis=1, keepdims=True)
    lane = lax.broadcasted_iota(jnp.int32, (total.shape[0], 128), 1)
    parts = [part.astype(F32) for part in split3(jnp.broadcast_to(squares, lane.shape))]
    spread = jnp.where(lane == 0, parts[0], jnp.where(lane == 1, parts[1], parts[2]))
    packed[:, width:] = jnp.where(lane < 3, spread, 0.0).astype(BF16)


def streams(a, b, unused):
    rows, width = a.shape
    outs = (shaped(a.shape), shaped((rows, width + 128), BF16))
    return kernel_call(
        stream_kernel,
        "stream",
        (a, b, unused),
        [HERE, HERE, ANYWHERE],
        outs,
        cost=(a.size * 4, a.size * 4, 0),
    )[0]


def entry_own_kernel(hidden, packed, *refs):
    near, out = refs[:-1], refs[-1]
    width = packed.shape[1] - 128
    start = pl.multiple_of(lax.axis_index("ep") * width, width)
    turned = packed[:, :width].astype(F32).T.astype(BF16)
    at = 0
    for array in near:
        for first in range(0, array.shape[0], hidden):
            out[at : at + hidden, :] = jnp.dot(
                array[first : first + hidden, pl.ds(start, width)],
                turned,
                preferred_element_type=F32,
            )
            at += hidden


def entry_own(loads, pieces, packed, count):
    _, hidden, width = loads.leave.shape
    rows = packed.shape[0]
    near = loads.pieces(0, count, "entry")
    return loads.call(
        functools.partial(entry_own_kernel, hidden),
        "entry_own",
        (packed, *near),
        [HERE] * (1 + len(near)),
        (shaped((count * hidden, rows)),),
        pieces,
        cost=(2 * rows * count * hidden * width // 4, count * hidden * width // 2, 0),
    )[0]


def entry_kernel(base, first, n, hidden, *refs):
    packs, routing, before = refs[:SIDE], refs[SIDE], refs[SIDE + 1]
    near, rest = refs[SIDE + 2 : SIDE + 2 + n], refs[SIDE + 2 + n :]
    rows, width = packs[0].shape
    width = width - 128
    me = lax.axis_index("ep")
    if first:
        out, turned = rest
        for k, packed in enumerate(packs):
            turned[k * width : (k + 1) * width, :] = packed[:, :width].astype(F32).T.astype(BF16)
    else:
        turned, out = rest
    squares = jnp.zeros((rows, 128), F32)
    for packed in packs:
        squares = squares + packed[:, width:].astype(F32)
    mean = jnp.sum(squares.T, axis=0, keepdims=True) / (SIDE * width)
    scale = lax.rsqrt(mean + 1e-06)
    table = routing[...].T
    ids = table[0:TOPK, :]
    weight = table[TOPK : 2 * TOPK, :] + table[2 * TOPK : 3 * TOPK, :]
    weight = weight + table[3 * TOPK : 4 * TOPK, :]
    count = EXPERTS // SIDE
    number = 0
    pair = []
    for array in near:
        for start in range(0, array.shape[0], hidden):
            chosen = ids == (me * count + base + number).astype(F32)
            share = jnp.sum(jnp.where(chosen, weight, 0.0), axis=0, keepdims=True)
            at = (base + number) * hidden
            begun = at < before.shape[0]
            total = before[at : at + hidden, :] if begun else 0.0
            for k in range(1 if begun else 0, SIDE):
                columns = pl.ds(pl.multiple_of((me ^ k) * width, width), width)
                total = total + jnp.dot(
                    array[start : start + hidden, columns],
                    turned[k * width : (k + 1) * width, :],
                    preferred_element_type=F32,
                )
            total = total * scale
            active = (total / (1.0 + jnp.exp(-total))).astype(BF16).astype(F32) * share
            high = active.astype(BF16).astype(F32)
            pair.append(jnp.concatenate([high, active - high], axis=1))
            number += 1
            if len(pair) == 2:
                end = number * hidden
                both = jnp.concatenate(pair, axis=0)
                out[:, end - 2 * hidden : end] = both.T.astype(BF16)
                pair = []


def entries(loads, pieces, base, last, packs, routing, before, turned=None):
    _, hidden, width = loads.leave.shape
    count = last - base
    rows = packs[0].shape[0]
    near = loads.pieces(base, last, "entry")
    first = turned is None
    args = (*packs, routing, before, *near) + (() if first else (turned,))
    outs = (shaped((2 * rows, count * hidden), BF16),)
    if first:
        outs += (shaped((width, rows), BF16),)
    return loads.call(
        functools.partial(entry_kernel, base, first, len(near), hidden),
        f"entry{base}",
        args,
        [HERE] * len(args),
        outs,
        pieces,
        cost=(2 * rows * count * hidden * width, 2 * count * hidden * width, 0),
    )


def leave_kernel(other, n, m, step, *refs):
    scaled, near, out = refs[:m], refs[m : m + n], refs[m + n + 1]
    rows, half = out.shape
    chip = (lax.axis_index("hd") // 2) ^ other
    for c in range(0, half, step):
        total = jnp.zeros((2 * rows, step), F32)
        which, at = 0, 0
        for array in near:
            start = c if array.shape[1] == half else pl.multiple_of(chip * half + c, step)
            done = 0
            while done < array.shape[0]:
                depth = min(array.shape[0] - done, scaled[which].shape[1] - at)
                total = total + jnp.dot(
                    scaled[which][:, at : at + depth],
                    array[done : done + depth, pl.ds(start, step)],
                    preferred_element_type=F32,
                )
                done, at = done + depth, at + depth
                if at == scaled[which].shape[1]:
                    which, at = which + 1, 0
        out[:, c : c + step] = (total[:rows] + total[rows:]).astype(out.dtype)


def leaves(loads, pieces, name, other, dtype, scaled, unused):
    count, hidden, width = loads.leave.shape
    near = loads.pieces(0, count, "leave", "away" if other else "here")
    rows = scaled[0].shape[0] // 2
    return loads.call(
        functools.partial(leave_kernel, other, len(near), len(scaled), 1024),
        name,
        (*scaled, *near, unused),
        [HERE] * (len(scaled) + len(near)) + [ANYWHERE],
        (shaped((rows, width // 2), dtype),),
        pieces,
        cost=(2 * rows * count * hidden * width, count * hidden * width, 0),
        limit=6,
    )[0]


def halve_kernel(mine, received, keep, send):
    width = keep.shape[1]
    core = lax.axis_index("hd") % 2
    for out, which in ((send, 1 - core), (keep, core)):
        columns = pl.ds(pl.multiple_of(which * width, width), width)
        out[...] = mine[:, columns] + received[:, columns].astype(F32)


def halve(mine, received):
    rows, width = mine.shape
    outs = (shaped((rows, width // 2)),) * 2
    cost = (mine.size, mine.size * 6, 0)
    return kernel_call(halve_kernel, "halve", (mine, received), [HERE] * 2, outs, cost=cost)[0]


def share_kernel(own, received, stream, o0, o1, o2, o3):
    rows = o0.shape[0]
    me = lax.axis_index("ep")
    here = (me == lax.axis_index("hd")).astype(F32)
    for k, out in enumerate((o0, o1, o2, o3)):
        span = pl.ds(pl.multiple_of((me ^ k) * rows, rows), rows)
        out[...] = own[span, :] + received[span, :] + here * stream[span, :]


def share(own, received, stream):
    rows, width = own.shape
    outs = (shaped((rows // SIDE, width)),) * SIDE
    cost = (own.size * 3, own.size * 16, 0)
    args = (own, received, stream)
    return kernel_call(share_kernel, "share", args, [HERE] * 3, outs, cost=cost)[0]


PLAN = {
    "attention": [("entry", 0, 2)],
    "fetch0": [("entry", 2, 6)],
    "projection": [],
    "fetch1": [("entry", 8, 7)],
    "own": [("leave", 0, 7)],
    "entry0": [("entry", 15, 1), ("leave", 7, 2)],
    "entry8": [("away", 9, 7)],
    "leave1": [("here", 9, 7)],
}


def square_body(
    residual,
    queries,
    key_value_cache,
    lengths,
    slot_of,
    out_weight,
    expert_ids,
    route_weight,
    in_weight,
    down_weight,
):
    rows = queries.shape[0]
    cache = key_value_cache.reshape(rows, 2 * CACHE_LENGTH, HEAD_SIZE)
    loads = Loads(jnp.swapaxes(in_weight, 1, 2), down_weight)
    plan = PLAN
    attended, weight, order = attention(
        loads,
        plan["attention"],
        lengths,
        queries,
        cache,
        expert_ids,
        route_weight,
        residual,
        out_weight,
        slot_of,
    )
    blocks = [attended] + [swap(attended, "ep", k) for k in (1, 2, 3)]
    mark = fetch(loads, plan["fetch0"], "fetch0", attended)
    partial_value, routing = projection(loads, plan["projection"], order, blocks, weight, mark)
    pair = add(partial_value, swap(partial_value, "hd", 1))
    far_pair = swap(pair, "hd", 2)
    mark = fetch(loads, plan["fetch1"], "fetch1", pair)
    stream, packed = streams(pair, far_pair, mark)
    packs = [packed] + [swap(packed, "ep", k) for k in (1, 2, 3)]
    before = entry_own(loads, plan["own"], packed, 15)
    scaled, turned = entries(loads, plan["entry0"], 0, 8, packs, routing, before)
    (more,) = entries(loads, plan["entry8"], 8, 16, packs, routing, before, turned)
    scaled = (scaled, more)
    theirs = leaves(loads, plan["leave1"], "leave1", 1, BF16, scaled, more)
    mine = leaves(loads, (), "leave0", 0, F32, scaled, theirs)
    keep, send = halve(mine, swap(theirs, "hd", 2))
    total, *others = share(keep, swap(send, "hd", 1), stream)
    for k in (3, 2, 1):
        total = total + swap(others[k - 1], "ep", k)
    return total.astype(BF16)


def expert_pass(block, in_weight, down_weight):
    local_count = in_weight.shape[0]
    senders = block.shape[0] // local_count
    slots = block.shape[1]
    width = block.shape[2]
    grouped = block.reshape(senders, local_count, slots, width)
    hidden = jnp.einsum("secd,edf->secf", grouped, in_weight, preferred_element_type=jnp.float32)
    hidden = jax.nn.silu(hidden).astype(jnp.bfloat16)
    output = jnp.einsum("secf,efd->secd", hidden, down_weight, preferred_element_type=jnp.float32)
    return output.reshape(senders * local_count, slots, width)


def body(
    residual,
    queries,
    key_value_cache,
    lengths,
    slot_of,
    out_weight,
    expert_ids,
    route_weight,
    in_weight,
    down_weight,
):
    rows_here = queries.shape[0]
    local_groups = key_value_cache.shape[3] // HEAD_SIZE
    heads_per_group = QUERY_HEADS // KEY_VALUE_HEADS
    query_head_rows = queries.reshape(rows_here, local_groups, heads_per_group, HEAD_SIZE)
    cached_key_rows = key_value_cache[:, :, 0].reshape(
        rows_here, CACHE_LENGTH, local_groups, HEAD_SIZE
    )
    cached_value_rows = key_value_cache[:, :, 1].reshape(
        rows_here, CACHE_LENGTH, local_groups, HEAD_SIZE
    )
    scores = jnp.einsum(
        "sagd,slad->sagl", query_head_rows, cached_key_rows, preferred_element_type=jnp.float32
    )
    scores = scores * (1.0 / math.sqrt(HEAD_SIZE))
    visible = (jnp.arange(CACHE_LENGTH)[None, :] < lengths[:, None])[:, None, None, :]
    scores = jnp.where(visible, scores, -1e30)
    highest = jnp.max(scores, axis=3, keepdims=True)
    raised = jnp.where(visible, jnp.exp(scores - highest), 0.0)
    weights = (raised / jnp.sum(raised, axis=3, keepdims=True)).astype(jnp.bfloat16)
    attended = jnp.einsum(
        "sagl,slad->sagd", weights, cached_value_rows, preferred_element_type=jnp.float32
    )
    attended = attended.astype(jnp.bfloat16).reshape(
        rows_here, local_groups * heads_per_group * HEAD_SIZE
    )
    partial_value = jnp.dot(
        lax.all_gather(attended, "ep", axis=0, tiled=True),
        out_weight,
        preferred_element_type=jnp.float32,
    )
    ordered = jnp.take(partial_value, slot_of, axis=0)
    moved = lax.all_to_all(ordered, "ep", split_axis=0, concat_axis=1, tiled=True)
    summed = lax.psum_scatter(moved, "hd", scatter_dimension=1, tiled=True)
    stream = residual.astype(jnp.float32) + summed
    squares = lax.psum(jnp.sum(stream * stream, axis=1), "hd")
    normed = (stream * lax.rsqrt(squares / D + 1e-06)[:, None]).astype(jnp.bfloat16)
    picked = expert_ids.reshape(-1)
    member = (picked[:, None] == jnp.arange(EXPERTS)[None, :]).astype(jnp.int32)
    earlier = jnp.cumsum(member, axis=0) - member
    position = jnp.sum(earlier * member, axis=1)
    target = picked * CAP + position
    placed = (target[:, None] == jnp.arange(EXPERTS * CAP)[None, :]).astype(jnp.float32)
    owner = (jnp.arange(picked.shape[0])[:, None] // TOPK == jnp.arange(rows_here)[None, :]).astype(
        jnp.float32
    )
    select_matrix = jnp.dot(placed.T, owner, precision=lax.Precision.HIGHEST).astype(jnp.bfloat16)
    mixing = jnp.dot(
        owner.T, placed * route_weight.reshape(-1)[:, None], precision=lax.Precision.HIGHEST
    )
    full_rows = lax.all_gather(normed, "hd", axis=1, tiled=True)
    outgoing = jnp.dot(select_matrix, full_rows, preferred_element_type=jnp.float32).astype(
        jnp.bfloat16
    )
    outgoing = outgoing.reshape(EXPERTS, CAP, full_rows.shape[1])
    results = expert_pass(
        lax.all_to_all(outgoing, "ep", split_axis=0, concat_axis=0, tiled=True),
        in_weight,
        down_weight,
    )
    share_width = residual.shape[1]
    shares = lax.psum_scatter(results.astype(jnp.bfloat16), "hd", scatter_dimension=2, tiled=True)
    returned = lax.all_to_all(shares, "ep", split_axis=0, concat_axis=0, tiled=True)
    flat_back = returned.reshape(EXPERTS * CAP, share_width).astype(jnp.float32)
    mixture = jnp.dot(mixing, flat_back, precision=lax.Precision.HIGHEST)
    return (stream + mixture).astype(jnp.bfloat16)


def solution(mesh):
    in_specs = (
        P(("groups", "ep"), "hd"),
        P(("groups", "ep"), "hd"),
        P(("groups", "ep"), None, None, "hd"),
        P(("groups", "ep")),
        P("groups"),
        P("hd", "ep"),
        P(("groups", "ep"), None),
        P(("groups", "ep"), None),
        P("ep", None, "hd"),
        P("ep", "hd", None),
    )
    out_specs = P(("groups", "ep"), "hd")
    chosen = square_body if mesh.shape["ep"] == mesh.shape["hd"] == SIDE else body
    return jax.shard_map(chosen, mesh=mesh, in_specs=in_specs, out_specs=out_specs, check_vma=False)
```

```python
import functools
import math

import jax
import jax.numpy as jnp
from jax import lax
from jax.experimental import pallas as pl
from jax.experimental.pallas import tpu as pltpu
from jax.sharding import PartitionSpec as P

D = 4096
QUERY_HEADS = 64
KEY_VALUE_HEADS = 4
HEAD_SIZE = 128
EXPERTS = 64
TOPK = 8
CAP = 2
CACHE_LENGTH = 256
SIDE = 4
BF16 = jnp.bfloat16
F32 = jnp.float32
MIB = 1 << 20
HERE = pl.BlockSpec(memory_space=pltpu.VMEM)
SCALARS = pl.BlockSpec(memory_space=pltpu.SMEM)
ANYWHERE = pl.BlockSpec(memory_space=pl.ANY)
DMA = pltpu.SemaphoreType.DMA


def swap(block, axis, k):
    return lax.ppermute(block, axis, [(i, i ^ k) for i in range(SIDE)])


def far(array):
    return pltpu.with_memory_space_constraint(array, pltpu.HBM)


def split3(value):
    high = value.astype(BF16)
    rest = value - high.astype(F32)
    middle = rest.astype(BF16)
    low = (rest - middle.astype(F32)).astype(BF16)
    return high, middle, low


def hosted(body, inputs, outputs, loads):
    n = len(loads)

    def kernel(*refs):
        sources = refs[inputs : inputs + n]
        targets = refs[inputs + n + outputs : inputs + n + outputs + n]
        ins, outs = refs[:inputs], refs[inputs + n : inputs + n + outputs]
        copies = []
        for i, (load, source, target) in enumerate(zip(loads, sources, targets)):
            _, first, count, other = load
            depth, width = target.shape
            rows = pl.ds(first * (depth // count), depth)
            if other is None:
                source = source.at[rows]
            else:
                chip = (lax.axis_index("hd") // 2) ^ other
                source = source.at[rows, pl.ds(pl.multiple_of(chip * width, width), width)]
            copies.append(pltpu.make_async_copy(source, target, refs[-1].at[i]))
        begin = lambda: [copy.start() for copy in copies]
        rest = refs[inputs + outputs + 2 * n : -1]
        if body is attention_kernel:
            body(*ins, *outs, *rest, begin)
        else:
            begin()

            @pl.when(lax.axis_index("ep") >= 0)
            def _():
                body(*ins, *outs, *rest)

        for copy in copies:
            copy.wait()

    return kernel


def kernel_call(
    body, name, args, specs, outs, scratch=(), loads=(), limit=4, cost=(0, 0, 0), aliases=None
):
    targets = [
        pltpu.VMEM((count * array.shape[1], array.shape[2] // (1 if other is None else 2)), BF16)
        for array, _, count, other in loads
    ]
    flops, bytes_accessed, transcendentals = cost
    bytes_accessed += sum(2 * math.prod(target.shape) for target in targets)
    results = pl.pallas_call(
        hosted(body, len(args), len(outs), loads) if loads or body is attention_kernel else body,
        out_shape=(*outs, *targets),
        in_specs=[*specs] + [ANYWHERE] * len(loads),
        out_specs=(HERE,) * (len(outs) + len(targets)),
        scratch_shapes=[*scratch] + ([DMA((max(1, len(loads)),))] if loads or body is attention_kernel else []),
        input_output_aliases=aliases or {},
        compiler_params=pltpu.CompilerParams(vmem_limit_bytes=limit * MIB),
        cost_estimate=pl.CostEstimate(
            flops=flops, bytes_accessed=bytes_accessed, transcendentals=transcendentals
        ),
        name=name,
    )(*args, *(far(array.reshape(-1, array.shape[2])) for array, *_ in loads))
    return results[: len(outs)], results[len(outs) :]


class Loads:
    def __init__(self, entry, leave):
        self.entry, self.leave = entry, leave
        self.near = {"entry": [], "leave": [], "away": [], "here": []}

    def call(self, body, name, args, specs, outs, pieces=(), **more):
        half = {"away": 1, "here": 0}
        loads = tuple(
            (self.entry if what == "entry" else self.leave, first, count, half.get(what))
            for what, first, count in pieces
        )
        results, arrays = kernel_call(body, name, args, specs, outs, loads=loads, **more)
        for (what, first, count), array in zip(pieces, arrays):
            self.near[what].append((first, count, array))
        return results

    def pieces(self, first, last, *kinds):
        held = sum((self.near[what] for what in kinds), [])
        chosen = [p for p in held if first <= p[0] and p[0] + p[1] <= last]
        assert sum(p[1] for p in chosen) == last - first
        return tuple(p[2] for p in sorted(chosen, key=lambda p: p[0]))


def shaped(shape, dtype=F32):
    return jax.ShapeDtypeStruct(shape, dtype)


def attention_kernel(
    lengths_far,
    queries_far,
    cache_far,
    ids_far,
    route_far,
    residual_far,
    weight_far,
    slot_far,
    out,
    weight,
    order,
    lengths,
    queries,
    cache,
    ids,
    route,
    residual,
    slot_of,
    staged,
    gathered,
    sems,
    begin,
):
    pairs = (
        (lengths_far, lengths),
        (queries_far, queries),
        (cache_far, cache),
        (ids_far, ids),
        (route_far, route),
        (residual_far, residual),
        (slot_far, slot_of),
        (weight_far, weight),
    )
    copies = [pltpu.make_async_copy(*pair, sems.at[i]) for i, pair in enumerate(pairs)]
    for copy in copies:
        copy.start()
    begin()
    rows = queries.shape[0]
    heads = queries.shape[1] // HEAD_SIZE
    everyone = rows * heads
    copies[1].wait()
    for h in range(heads):
        lanes = slice(h * HEAD_SIZE, (h + 1) * HEAD_SIZE)
        staged[pl.ds(h, rows, stride=heads), :] = queries[:, lanes].astype(F32)
    turned = staged[...].T.astype(BF16)
    copies[0].wait()
    slot = lax.broadcasted_iota(jnp.int32, (1, everyone), 1) // heads
    limit = jnp.zeros((1, everyone), jnp.int32)
    for s in range(rows):
        limit = jnp.where(slot == s, 2 * lengths[s], limit)
    place = lax.broadcasted_iota(jnp.int32, (2 * CACHE_LENGTH, everyone), 0)
    visible = jnp.logical_and(place % 2 == 0, place < limit)
    width = heads * HEAD_SIZE
    copies[3].wait()
    copies[4].wait()
    row = lax.broadcasted_iota(jnp.int32, (TOPK, 128), 0)
    lane = lax.broadcasted_iota(jnp.int32, (TOPK, 128), 1)
    total = jnp.zeros((rows, 128), F32)
    for j, part in enumerate((ids[...].astype(F32).astype(BF16), *split3(route[...]))):
        spread = (lane == row + j * TOPK).astype(F32).astype(BF16)
        total = total + jnp.dot(part, spread, preferred_element_type=F32)
    out[:, width : width + 128] = total.astype(BF16)
    copies[5].wait()
    out[:, width + 128 :] = residual[...]
    copies[6].wait()
    me = lax.axis_index("ep")
    row = lax.broadcasted_iota(jnp.int32, order.shape, 0)
    wanted = jnp.zeros(order.shape, jnp.int32)
    for r in range(order.shape[0]):
        held = slot_of[r]
        wanted = jnp.where(row == r, ((held // rows) ^ me) * rows + held % rows, wanted)
    column = lax.broadcasted_iota(jnp.int32, order.shape, 1)
    order[...] = (wanted == column).astype(F32).astype(BF16)
    copies[2].wait()
    scores = jnp.dot(cache[0], turned, preferred_element_type=F32)
    for s in range(1, rows):
        more = jnp.dot(cache[s], turned, preferred_element_type=F32)
        scores = jnp.where(slot == s, more, scores)
    scores = jnp.where(visible, scores * (1.0 / math.sqrt(HEAD_SIZE)), -1e30)
    raised = jnp.where(visible, jnp.exp(scores - jnp.max(scores, axis=0, keepdims=True)), 0.0)
    weights = raised / jnp.sum(raised, axis=0, keepdims=True)
    moved = pltpu.roll(weights, 1, 0).T.astype(BF16)
    for s in range(rows):
        span = slice(s * heads, (s + 1) * heads)
        gathered[span, :] = jnp.dot(moved[span], cache[s], preferred_element_type=F32)
    for h in range(heads):
        lanes = slice(h * HEAD_SIZE, (h + 1) * HEAD_SIZE)
        out[:, lanes] = gathered[pl.ds(h, rows, stride=heads), :].astype(BF16)
    copies[7].wait()


def attention(loads, pieces, lengths, queries, cache, ids, route, residual, weight, slot_of):
    rows, width = queries.shape
    staged = pltpu.VMEM((rows * width // HEAD_SIZE, HEAD_SIZE), F32)
    return loads.call(
        attention_kernel,
        "attention",
        tuple(map(far, (lengths, queries, cache, ids, route, residual, weight, slot_of))),
        [ANYWHERE] * 8,
        (
            shaped((rows, width + 128 + residual.shape[1]), BF16),
            pltpu.VMEM(weight.shape, BF16),
            shaped((slot_of.shape[0], slot_of.shape[0]), BF16),
        ),
        pieces,
        scratch=[
            pltpu.SMEM(lengths.shape, jnp.int32),
            pltpu.VMEM(queries.shape, BF16),
            pltpu.VMEM(cache.shape, BF16),
            pltpu.VMEM(ids.shape, jnp.int32),
            pltpu.VMEM(route.shape, F32),
            pltpu.VMEM(residual.shape, BF16),
            pltpu.SMEM(slot_of.shape, jnp.int32),
            staged,
            staged,
            DMA((8,)),
        ],
        cost=(140_000_000, 12_000_000, 65536),
    )


def fetch_kernel(after, mark):
    del after
    mark[...] = jnp.zeros_like(mark)


def fetch(loads, pieces, name, after):
    return loads.call(
        fetch_kernel, name, (after,), [ANYWHERE], (shaped((8, 128)),), pieces, limit=1
    )[0]


def projection_kernel(order, b0, b1, b2, b3, weight, unused, out, routing, kept):
    del unused
    blocks = (b0, b1, b2, b3)
    rows = b0.shape[0]
    width = weight.shape[0]
    me = lax.axis_index("ep")
    for k, block in enumerate(blocks):
        span = pl.ds(pl.multiple_of((me ^ k) * rows, rows), rows)
        routing[span, :] = block[:, width : width + 128].astype(F32)
        kept[span, :] = block[:, width + 128 :].astype(F32)
    held = jnp.concatenate([b[:, :width].astype(F32) for b in blocks], axis=0).astype(BF16)
    ordered = jnp.dot(order[...], held, preferred_element_type=F32).astype(BF16)
    own = (me == lax.axis_index("hd")).astype(F32)
    out[...] = jnp.dot(ordered, weight[...], preferred_element_type=F32) + own * kept[...]


def projection(loads, pieces, order, blocks, weight, unused):
    everyone = SIDE * blocks[0].shape[0]
    wide = (everyone, weight.shape[1])
    return loads.call(
        projection_kernel,
        "projection",
        (order, *blocks, weight, unused),
        [HERE] * 6 + [ANYWHERE],
        (shaped(wide), shaped((everyone, 128))),
        pieces,
        scratch=[pltpu.VMEM(wide, F32)],
        limit=6,
        cost=(140_000_000, 4_500_000, 0),
    )


def add_kernel(a, b, out):
    out[...] = a[...] + b[...]


def add(a, b):
    outs = (shaped(a.shape),)
    return kernel_call(add_kernel, "add", (a, b), [HERE] * 2, outs, cost=(a.size, a.size, 0))[0][0]


def stream_kernel(a, b, unused, stream, packed):
    del unused
    total = a[...] + b[...]
    stream[...] = total
    width = total.shape[1]
    packed[:, :width] = total.astype(BF16)
    squares = jnp.sum(total * total, axis=1, keepdims=True)
    lane = lax.broadcasted_iota(jnp.int32, (total.shape[0], 128), 1)
    parts = [part.astype(F32) for part in split3(jnp.broadcast_to(squares, lane.shape))]
    spread = jnp.where(lane == 0, parts[0], jnp.where(lane == 1, parts[1], parts[2]))
    packed[:, width:] = jnp.where(lane < 3, spread, 0.0).astype(BF16)


def streams(a, b, unused):
    rows, width = a.shape
    outs = (shaped(a.shape), shaped((rows, width + 128), BF16))
    return kernel_call(
        stream_kernel,
        "stream",
        (a, b, unused),
        [HERE, HERE, ANYWHERE],
        outs,
        cost=(a.size * 4, a.size * 4, 0),
    )[0]


def entry_own_kernel(hidden, packed, *refs):
    near, out = refs[:-1], refs[-1]
    width = packed.shape[1] - 128
    start = pl.multiple_of(lax.axis_index("ep") * width, width)
    turned = packed[:, :width].astype(F32).T.astype(BF16)
    at = 0
    for array in near:
        for first in range(0, array.shape[0], hidden):
            out[at : at + hidden, :] = jnp.dot(
                array[first : first + hidden, pl.ds(start, width)],
                turned,
                preferred_element_type=F32,
            )
            at += hidden


def entry_own(loads, pieces, packed, count):
    _, hidden, width = loads.leave.shape
    rows = packed.shape[0]
    near = loads.pieces(0, count, "entry")
    return loads.call(
        functools.partial(entry_own_kernel, hidden),
        "entry_own",
        (packed, *near),
        [HERE] * (1 + len(near)),
        (shaped((count * hidden, rows)),),
        pieces,
        cost=(2 * rows * count * hidden * width // 4, count * hidden * width // 2, 0),
    )[0]


def entry_kernel(base, first, n, hidden, *refs):
    packs, routing, before = refs[:SIDE], refs[SIDE], refs[SIDE + 1]
    near, rest = refs[SIDE + 2 : SIDE + 2 + n], refs[SIDE + 2 + n :]
    rows, width = packs[0].shape
    width = width - 128
    me = lax.axis_index("ep")
    if first:
        out, turned = rest
        for k, packed in enumerate(packs):
            turned[k * width : (k + 1) * width, :] = packed[:, :width].astype(F32).T.astype(BF16)
    else:
        turned, out = rest
    squares = jnp.zeros((rows, 128), F32)
    for packed in packs:
        squares = squares + packed[:, width:].astype(F32)
    mean = jnp.sum(squares.T, axis=0, keepdims=True) / (SIDE * width)
    scale = lax.rsqrt(mean + 1e-06)
    table = routing[...].T
    ids = table[0:TOPK, :]
    weight = table[TOPK : 2 * TOPK, :] + table[2 * TOPK : 3 * TOPK, :]
    weight = weight + table[3 * TOPK : 4 * TOPK, :]
    count = EXPERTS // SIDE
    number = 0
    pair = []
    for array in near:
        for start in range(0, array.shape[0], hidden):
            chosen = ids == (me * count + base + number).astype(F32)
            share = jnp.sum(jnp.where(chosen, weight, 0.0), axis=0, keepdims=True)
            at = (base + number) * hidden
            begun = at < before.shape[0]
            total = before[at : at + hidden, :] if begun else 0.0
            for k in range(1 if begun else 0, SIDE):
                columns = pl.ds(pl.multiple_of((me ^ k) * width, width), width)
                total = total + jnp.dot(
                    array[start : start + hidden, columns],
                    turned[k * width : (k + 1) * width, :],
                    preferred_element_type=F32,
                )
            total = total * scale
            active = (total / (1.0 + jnp.exp(-total))).astype(BF16).astype(F32) * share
            high = active.astype(BF16).astype(F32)
            pair.append(jnp.concatenate([high, active - high], axis=1))
            number += 1
            if len(pair) == 2:
                end = number * hidden
                both = jnp.concatenate(pair, axis=0)
                out[:, end - 2 * hidden : end] = both.T.astype(BF16)
                pair = []


def entries(loads, pieces, base, last, packs, routing, before, turned=None):
    _, hidden, width = loads.leave.shape
    count = last - base
    rows = packs[0].shape[0]
    near = loads.pieces(base, last, "entry")
    first = turned is None
    args = (*packs, routing, before, *near) + (() if first else (turned,))
    outs = (shaped((2 * rows, count * hidden), BF16),)
    if first:
        outs += (shaped((width, rows), BF16),)
    return loads.call(
        functools.partial(entry_kernel, base, first, len(near), hidden),
        f"entry{base}",
        args,
        [HERE] * len(args),
        outs,
        pieces,
        cost=(2 * rows * count * hidden * width, 2 * count * hidden * width, 0),
    )


def leave_kernel(other, n, m, step, *refs):
    scaled, near, out = refs[:m], refs[m : m + n], refs[m + n + 1]
    rows, half = out.shape
    chip = (lax.axis_index("hd") // 2) ^ other
    for c in range(0, half, step):
        total = jnp.zeros((2 * rows, step), F32)
        which, at = 0, 0
        for array in near:
            start = c if array.shape[1] == half else pl.multiple_of(chip * half + c, step)
            done = 0
            while done < array.shape[0]:
                depth = min(array.shape[0] - done, scaled[which].shape[1] - at)
                total = total + jnp.dot(
                    scaled[which][:, at : at + depth],
                    array[done : done + depth, pl.ds(start, step)],
                    preferred_element_type=F32,
                )
                done, at = done + depth, at + depth
                if at == scaled[which].shape[1]:
                    which, at = which + 1, 0
        out[:, c : c + step] = (total[:rows] + total[rows:]).astype(out.dtype)


def leaves(loads, pieces, name, other, dtype, scaled, unused):
    count, hidden, width = loads.leave.shape
    near = loads.pieces(0, count, "leave", "away" if other else "here")
    rows = scaled[0].shape[0] // 2
    return loads.call(
        functools.partial(leave_kernel, other, len(near), len(scaled), 1024),
        name,
        (*scaled, *near, unused),
        [HERE] * (len(scaled) + len(near)) + [ANYWHERE],
        (shaped((rows, width // 2), dtype),),
        pieces,
        cost=(2 * rows * count * hidden * width, count * hidden * width, 0),
        limit=6,
    )[0]


def halve_kernel(mine, received, keep, send):
    width = keep.shape[1]
    core = lax.axis_index("hd") % 2
    for out, which in ((send, 1 - core), (keep, core)):
        columns = pl.ds(pl.multiple_of(which * width, width), width)
        out[...] = mine[:, columns] + received[:, columns].astype(F32)


def halve(mine, received):
    rows, width = mine.shape
    outs = (shaped((rows, width // 2)),) * 2
    cost = (mine.size, mine.size * 6, 0)
    return kernel_call(halve_kernel, "halve", (mine, received), [HERE] * 2, outs, cost=cost)[0]


def share_kernel(own, received, stream, o0, o1, o2, o3):
    rows = o0.shape[0]
    me = lax.axis_index("ep")
    here = (me == lax.axis_index("hd")).astype(F32)
    for k, out in enumerate((o0, o1, o2, o3)):
        span = pl.ds(pl.multiple_of((me ^ k) * rows, rows), rows)
        out[...] = own[span, :] + received[span, :] + here * stream[span, :]


def share(own, received, stream):
    rows, width = own.shape
    outs = (shaped((rows // SIDE, width)),) * SIDE
    cost = (own.size * 3, own.size * 16, 0)
    args = (own, received, stream)
    return kernel_call(share_kernel, "share", args, [HERE] * 3, outs, cost=cost)[0]


PLAN = {
    "attention": [],
    "fetch0": [("entry", 0, 6)],
    "projection": [],
    "fetch1": [("entry", 6, 2), ("entry", 8, 5)],
    "own": [("leave", 0, 8)],
    "entry0": [("entry", 13, 3), ("leave", 8, 1)],
    "entry8": [("away", 9, 7)],
    "leave1": [("here", 9, 7)],
}


def square_body(
    residual,
    queries,
    key_value_cache,
    lengths,
    slot_of,
    out_weight,
    expert_ids,
    route_weight,
    in_weight,
    down_weight,
):
    rows = queries.shape[0]
    cache = key_value_cache.reshape(rows, 2 * CACHE_LENGTH, HEAD_SIZE)
    loads = Loads(jnp.swapaxes(in_weight, 1, 2), down_weight)
    plan = PLAN
    attended, weight, order = attention(
        loads,
        plan["attention"],
        lengths,
        queries,
        cache,
        expert_ids,
        route_weight,
        residual,
        out_weight,
        slot_of,
    )
    blocks = [attended] + [swap(attended, "ep", k) for k in (1, 2, 3)]
    mark = fetch(loads, plan["fetch0"], "fetch0", attended)
    partial_value, routing = projection(loads, plan["projection"], order, blocks, weight, mark)
    pair = add(partial_value, swap(partial_value, "hd", 1))
    far_pair = swap(pair, "hd", 2)
    mark = fetch(loads, plan["fetch1"], "fetch1", pair)
    stream, packed = streams(pair, far_pair, mark)
    packs = [packed] + [swap(packed, "ep", k) for k in (1, 2, 3)]
    before = entry_own(loads, plan["own"], packed, 13)
    scaled, turned = entries(loads, plan["entry0"], 0, 8, packs, routing, before)
    (more,) = entries(loads, plan["entry8"], 8, 16, packs, routing, before, turned)
    scaled = (scaled, more)
    theirs = leaves(loads, plan["leave1"], "leave1", 1, BF16, scaled, more)
    mine = leaves(loads, (), "leave0", 0, F32, scaled, theirs)
    keep, send = halve(mine, swap(theirs, "hd", 2))
    total, *others = share(keep, swap(send, "hd", 1), stream)
    for k in (3, 2, 1):
        total = total + swap(others[k - 1], "ep", k)
    return total.astype(BF16)


def expert_pass(block, in_weight, down_weight):
    local_count = in_weight.shape[0]
    senders = block.shape[0] // local_count
    slots = block.shape[1]
    width = block.shape[2]
    grouped = block.reshape(senders, local_count, slots, width)
    hidden = jnp.einsum("secd,edf->secf", grouped, in_weight, preferred_element_type=jnp.float32)
    hidden = jax.nn.silu(hidden).astype(jnp.bfloat16)
    output = jnp.einsum("secf,efd->secd", hidden, down_weight, preferred_element_type=jnp.float32)
    return output.reshape(senders * local_count, slots, width)


def body(
    residual,
    queries,
    key_value_cache,
    lengths,
    slot_of,
    out_weight,
    expert_ids,
    route_weight,
    in_weight,
    down_weight,
):
    rows_here = queries.shape[0]
    local_groups = key_value_cache.shape[3] // HEAD_SIZE
    heads_per_group = QUERY_HEADS // KEY_VALUE_HEADS
    query_head_rows = queries.reshape(rows_here, local_groups, heads_per_group, HEAD_SIZE)
    cached_key_rows = key_value_cache[:, :, 0].reshape(
        rows_here, CACHE_LENGTH, local_groups, HEAD_SIZE
    )
    cached_value_rows = key_value_cache[:, :, 1].reshape(
        rows_here, CACHE_LENGTH, local_groups, HEAD_SIZE
    )
    scores = jnp.einsum(
        "sagd,slad->sagl", query_head_rows, cached_key_rows, preferred_element_type=jnp.float32
    )
    scores = scores * (1.0 / math.sqrt(HEAD_SIZE))
    visible = (jnp.arange(CACHE_LENGTH)[None, :] < lengths[:, None])[:, None, None, :]
    scores = jnp.where(visible, scores, -1e30)
    highest = jnp.max(scores, axis=3, keepdims=True)
    raised = jnp.where(visible, jnp.exp(scores - highest), 0.0)
    weights = (raised / jnp.sum(raised, axis=3, keepdims=True)).astype(jnp.bfloat16)
    attended = jnp.einsum(
        "sagl,slad->sagd", weights, cached_value_rows, preferred_element_type=jnp.float32
    )
    attended = attended.astype(jnp.bfloat16).reshape(
        rows_here, local_groups * heads_per_group * HEAD_SIZE
    )
    partial_value = jnp.dot(
        lax.all_gather(attended, "ep", axis=0, tiled=True),
        out_weight,
        preferred_element_type=jnp.float32,
    )
    ordered = jnp.take(partial_value, slot_of, axis=0)
    moved = lax.all_to_all(ordered, "ep", split_axis=0, concat_axis=1, tiled=True)
    summed = lax.psum_scatter(moved, "hd", scatter_dimension=1, tiled=True)
    stream = residual.astype(jnp.float32) + summed
    squares = lax.psum(jnp.sum(stream * stream, axis=1), "hd")
    normed = (stream * lax.rsqrt(squares / D + 1e-06)[:, None]).astype(jnp.bfloat16)
    picked = expert_ids.reshape(-1)
    member = (picked[:, None] == jnp.arange(EXPERTS)[None, :]).astype(jnp.int32)
    earlier = jnp.cumsum(member, axis=0) - member
    position = jnp.sum(earlier * member, axis=1)
    target = picked * CAP + position
    placed = (target[:, None] == jnp.arange(EXPERTS * CAP)[None, :]).astype(jnp.float32)
    owner = (jnp.arange(picked.shape[0])[:, None] // TOPK == jnp.arange(rows_here)[None, :]).astype(
        jnp.float32
    )
    select_matrix = jnp.dot(placed.T, owner, precision=lax.Precision.HIGHEST).astype(jnp.bfloat16)
    mixing = jnp.dot(
        owner.T, placed * route_weight.reshape(-1)[:, None], precision=lax.Precision.HIGHEST
    )
    full_rows = lax.all_gather(normed, "hd", axis=1, tiled=True)
    outgoing = jnp.dot(select_matrix, full_rows, preferred_element_type=jnp.float32).astype(
        jnp.bfloat16
    )
    outgoing = outgoing.reshape(EXPERTS, CAP, full_rows.shape[1])
    results = expert_pass(
        lax.all_to_all(outgoing, "ep", split_axis=0, concat_axis=0, tiled=True),
        in_weight,
        down_weight,
    )
    share_width = residual.shape[1]
    shares = lax.psum_scatter(results.astype(jnp.bfloat16), "hd", scatter_dimension=2, tiled=True)
    returned = lax.all_to_all(shares, "ep", split_axis=0, concat_axis=0, tiled=True)
    flat_back = returned.reshape(EXPERTS * CAP, share_width).astype(jnp.float32)
    mixture = jnp.dot(mixing, flat_back, precision=lax.Precision.HIGHEST)
    return (stream + mixture).astype(jnp.bfloat16)


def solution(mesh):
    in_specs = (
        P(("groups", "ep"), "hd"),
        P(("groups", "ep"), "hd"),
        P(("groups", "ep"), None, None, "hd"),
        P(("groups", "ep")),
        P("groups"),
        P("hd", "ep"),
        P(("groups", "ep"), None),
        P(("groups", "ep"), None),
        P("ep", None, "hd"),
        P("ep", "hd", None),
    )
    out_specs = P(("groups", "ep"), "hd")
    chosen = square_body if mesh.shape["ep"] == mesh.shape["hd"] == SIDE else body
    return jax.shard_map(chosen, mesh=mesh, in_specs=in_specs, out_specs=out_specs, check_vma=False)
```

```python
import functools
import math

import jax
import jax.numpy as jnp
from jax import lax
from jax.experimental import pallas as pl
from jax.experimental.pallas import tpu as pltpu
from jax.sharding import PartitionSpec as P

D = 4096
QUERY_HEADS = 64
KEY_VALUE_HEADS = 4
HEAD_SIZE = 128
EXPERTS = 64
TOPK = 8
CAP = 2
CACHE_LENGTH = 256
SIDE = 4
BF16 = jnp.bfloat16
F32 = jnp.float32
MIB = 1 << 20
HERE = pl.BlockSpec(memory_space=pltpu.VMEM)
SCALARS = pl.BlockSpec(memory_space=pltpu.SMEM)
ANYWHERE = pl.BlockSpec(memory_space=pl.ANY)
DMA = pltpu.SemaphoreType.DMA


def swap(block, axis, k):
    return lax.ppermute(block, axis, [(i, i ^ k) for i in range(SIDE)])


def far(array):
    return pltpu.with_memory_space_constraint(array, pltpu.HBM)


def split3(value):
    high = value.astype(BF16)
    rest = value - high.astype(F32)
    middle = rest.astype(BF16)
    low = (rest - middle.astype(F32)).astype(BF16)
    return high, middle, low


def hosted(body, inputs, outputs, loads):
    n = len(loads)

    def kernel(*refs):
        sources = refs[inputs : inputs + n]
        targets = refs[inputs + n + outputs : inputs + n + outputs + n]
        ins, outs = refs[:inputs], refs[inputs + n : inputs + n + outputs]
        copies = []
        for i, (load, source, target) in enumerate(zip(loads, sources, targets)):
            _, first, count, other = load
            depth, width = target.shape
            rows = pl.ds(first * (depth // count), depth)
            if other is None:
                source = source.at[rows]
            else:
                chip = (lax.axis_index("hd") // 2) ^ other
                source = source.at[rows, pl.ds(pl.multiple_of(chip * width, width), width)]
            copies.append(pltpu.make_async_copy(source, target, refs[-1].at[i]))
        begin = lambda: [copy.start() for copy in copies]
        rest = refs[inputs + outputs + 2 * n : -1]
        if body is attention_kernel:
            body(*ins, *outs, *rest, begin)
        else:
            begin()

            @pl.when(lax.axis_index("ep") >= 0)
            def _():
                body(*ins, *outs, *rest)

        for copy in copies:
            copy.wait()

    return kernel


def kernel_call(
    body, name, args, specs, outs, scratch=(), loads=(), limit=4, cost=(0, 0, 0), aliases=None
):
    targets = [
        pltpu.VMEM((count * array.shape[1], array.shape[2] // (1 if other is None else 2)), BF16)
        for array, _, count, other in loads
    ]
    flops, bytes_accessed, transcendentals = cost
    bytes_accessed += sum(2 * math.prod(target.shape) for target in targets)
    results = pl.pallas_call(
        hosted(body, len(args), len(outs), loads) if loads or body is attention_kernel else body,
        out_shape=(*outs, *targets),
        in_specs=[*specs] + [ANYWHERE] * len(loads),
        out_specs=(HERE,) * (len(outs) + len(targets)),
        scratch_shapes=[*scratch] + ([DMA((max(1, len(loads)),))] if loads or body is attention_kernel else []),
        input_output_aliases=aliases or {},
        compiler_params=pltpu.CompilerParams(vmem_limit_bytes=limit * MIB),
        cost_estimate=pl.CostEstimate(
            flops=flops, bytes_accessed=bytes_accessed, transcendentals=transcendentals
        ),
        name=name,
    )(*args, *(far(array.reshape(-1, array.shape[2])) for array, *_ in loads))
    return results[: len(outs)], results[len(outs) :]


class Loads:
    def __init__(self, entry, leave):
        self.entry, self.leave = entry, leave
        self.near = {"entry": [], "leave": [], "away": [], "here": []}

    def call(self, body, name, args, specs, outs, pieces=(), **more):
        half = {"away": 1, "here": 0}
        loads = tuple(
            (self.entry if what == "entry" else self.leave, first, count, half.get(what))
            for what, first, count in pieces
        )
        results, arrays = kernel_call(body, name, args, specs, outs, loads=loads, **more)
        for (what, first, count), array in zip(pieces, arrays):
            self.near[what].append((first, count, array))
        return results

    def pieces(self, first, last, *kinds):
        held = sum((self.near[what] for what in kinds), [])
        chosen = [p for p in held if first <= p[0] and p[0] + p[1] <= last]
        assert sum(p[1] for p in chosen) == last - first
        return tuple(p[2] for p in sorted(chosen, key=lambda p: p[0]))


def shaped(shape, dtype=F32):
    return jax.ShapeDtypeStruct(shape, dtype)


def attention_kernel(
    lengths_far,
    queries_far,
    cache_far,
    ids_far,
    route_far,
    residual_far,
    weight_far,
    slot_far,
    out,
    weight,
    order,
    lengths,
    queries,
    cache,
    ids,
    route,
    residual,
    slot_of,
    staged,
    gathered,
    sems,
    begin,
):
    pairs = (
        (lengths_far, lengths),
        (queries_far, queries),
        (cache_far, cache),
        (ids_far, ids),
        (route_far, route),
        (residual_far, residual),
        (slot_far, slot_of),
        (weight_far, weight),
    )
    copies = [pltpu.make_async_copy(*pair, sems.at[i]) for i, pair in enumerate(pairs)]
    for copy in copies:
        copy.start()
    begin()
    rows = queries.shape[0]
    heads = queries.shape[1] // HEAD_SIZE
    everyone = rows * heads
    copies[1].wait()
    for h in range(heads):
        lanes = slice(h * HEAD_SIZE, (h + 1) * HEAD_SIZE)
        staged[pl.ds(h, rows, stride=heads), :] = queries[:, lanes].astype(F32)
    turned = staged[...].T.astype(BF16)
    copies[0].wait()
    slot = lax.broadcasted_iota(jnp.int32, (1, everyone), 1) // heads
    limit = jnp.zeros((1, everyone), jnp.int32)
    for s in range(rows):
        limit = jnp.where(slot == s, 2 * lengths[s], limit)
    place = lax.broadcasted_iota(jnp.int32, (2 * CACHE_LENGTH, everyone), 0)
    visible = jnp.logical_and(place % 2 == 0, place < limit)
    width = heads * HEAD_SIZE
    copies[3].wait()
    copies[4].wait()
    row = lax.broadcasted_iota(jnp.int32, (TOPK, 128), 0)
    lane = lax.broadcasted_iota(jnp.int32, (TOPK, 128), 1)
    total = jnp.zeros((rows, 128), F32)
    for j, part in enumerate((ids[...].astype(F32).astype(BF16), *split3(route[...]))):
        spread = (lane == row + j * TOPK).astype(F32).astype(BF16)
        total = total + jnp.dot(part, spread, preferred_element_type=F32)
    out[:, width : width + 128] = total.astype(BF16)
    copies[5].wait()
    out[:, width + 128 :] = residual[...]
    copies[6].wait()
    me = lax.axis_index("ep")
    row = lax.broadcasted_iota(jnp.int32, order.shape, 0)
    wanted = jnp.zeros(order.shape, jnp.int32)
    for r in range(order.shape[0]):
        held = slot_of[r]
        wanted = jnp.where(row == r, ((held // rows) ^ me) * rows + held % rows, wanted)
    column = lax.broadcasted_iota(jnp.int32, order.shape, 1)
    order[...] = (wanted == column).astype(F32).astype(BF16)
    copies[2].wait()
    scores = jnp.dot(cache[0], turned, preferred_element_type=F32)
    for s in range(1, rows):
        more = jnp.dot(cache[s], turned, preferred_element_type=F32)
        scores = jnp.where(slot == s, more, scores)
    scores = jnp.where(visible, scores * (1.0 / math.sqrt(HEAD_SIZE)), -1e30)
    raised = jnp.where(visible, jnp.exp(scores - jnp.max(scores, axis=0, keepdims=True)), 0.0)
    weights = raised / jnp.sum(raised, axis=0, keepdims=True)
    moved = pltpu.roll(weights, 1, 0).T.astype(BF16)
    for s in range(rows):
        span = slice(s * heads, (s + 1) * heads)
        gathered[span, :] = jnp.dot(moved[span], cache[s], preferred_element_type=F32)
    for h in range(heads):
        lanes = slice(h * HEAD_SIZE, (h + 1) * HEAD_SIZE)
        out[:, lanes] = gathered[pl.ds(h, rows, stride=heads), :].astype(BF16)
    copies[7].wait()


def attention(loads, pieces, lengths, queries, cache, ids, route, residual, weight, slot_of):
    rows, width = queries.shape
    staged = pltpu.VMEM((rows * width // HEAD_SIZE, HEAD_SIZE), F32)
    return loads.call(
        attention_kernel,
        "attention",
        tuple(map(far, (lengths, queries, cache, ids, route, residual, weight, slot_of))),
        [ANYWHERE] * 8,
        (
            shaped((rows, width + 128 + residual.shape[1]), BF16),
            pltpu.VMEM(weight.shape, BF16),
            shaped((slot_of.shape[0], slot_of.shape[0]), BF16),
        ),
        pieces,
        scratch=[
            pltpu.SMEM(lengths.shape, jnp.int32),
            pltpu.VMEM(queries.shape, BF16),
            pltpu.VMEM(cache.shape, BF16),
            pltpu.VMEM(ids.shape, jnp.int32),
            pltpu.VMEM(route.shape, F32),
            pltpu.VMEM(residual.shape, BF16),
            pltpu.SMEM(slot_of.shape, jnp.int32),
            staged,
            staged,
            DMA((8,)),
        ],
        cost=(140_000_000, 12_000_000, 65536),
    )


def fetch_kernel(after, mark):
    del after
    mark[...] = jnp.zeros_like(mark)


def fetch(loads, pieces, name, after):
    return loads.call(
        fetch_kernel, name, (after,), [ANYWHERE], (shaped((8, 128)),), pieces, limit=1
    )[0]


def projection_kernel(order, b0, b1, b2, b3, weight, unused, out, routing, kept):
    del unused
    blocks = (b0, b1, b2, b3)
    rows = b0.shape[0]
    width = weight.shape[0]
    me = lax.axis_index("ep")
    for k, block in enumerate(blocks):
        span = pl.ds(pl.multiple_of((me ^ k) * rows, rows), rows)
        routing[span, :] = block[:, width : width + 128].astype(F32)
        kept[span, :] = block[:, width + 128 :].astype(F32)
    held = jnp.concatenate([b[:, :width].astype(F32) for b in blocks], axis=0).astype(BF16)
    ordered = jnp.dot(order[...], held, preferred_element_type=F32).astype(BF16)
    own = (me == lax.axis_index("hd")).astype(F32)
    out[...] = jnp.dot(ordered, weight[...], preferred_element_type=F32) + own * kept[...]


def projection(loads, pieces, order, blocks, weight, unused):
    everyone = SIDE * blocks[0].shape[0]
    wide = (everyone, weight.shape[1])
    return loads.call(
        projection_kernel,
        "projection",
        (order, *blocks, weight, unused),
        [HERE] * 6 + [ANYWHERE],
        (shaped(wide), shaped((everyone, 128))),
        pieces,
        scratch=[pltpu.VMEM(wide, F32)],
        limit=6,
        cost=(140_000_000, 4_500_000, 0),
    )


def add_kernel(a, b, out):
    out[...] = a[...] + b[...]


def add(a, b):
    outs = (shaped(a.shape),)
    return kernel_call(add_kernel, "add", (a, b), [HERE] * 2, outs, cost=(a.size, a.size, 0))[0][0]


def stream_kernel(a, b, unused, stream, packed):
    del unused
    total = a[...] + b[...]
    stream[...] = total
    width = total.shape[1]
    packed[:, :width] = total.astype(BF16)
    squares = jnp.sum(total * total, axis=1, keepdims=True)
    lane = lax.broadcasted_iota(jnp.int32, (total.shape[0], 128), 1)
    parts = [part.astype(F32) for part in split3(jnp.broadcast_to(squares, lane.shape))]
    spread = jnp.where(lane == 0, parts[0], jnp.where(lane == 1, parts[1], parts[2]))
    packed[:, width:] = jnp.where(lane < 3, spread, 0.0).astype(BF16)


def streams(a, b, unused):
    rows, width = a.shape
    outs = (shaped(a.shape), shaped((rows, width + 128), BF16))
    return kernel_call(
        stream_kernel,
        "stream",
        (a, b, unused),
        [HERE, HERE, ANYWHERE],
        outs,
        cost=(a.size * 4, a.size * 4, 0),
    )[0]


def entry_own_kernel(hidden, packed, *refs):
    near, out = refs[:-1], refs[-1]
    width = packed.shape[1] - 128
    start = pl.multiple_of(lax.axis_index("ep") * width, width)
    turned = packed[:, :width].T
    at = 0
    for array in near:
        for first in range(0, array.shape[0], hidden):
            out[at : at + hidden, :] = jnp.dot(
                array[first : first + hidden, pl.ds(start, width)],
                turned,
                preferred_element_type=F32,
            )
            at += hidden


def entry_own(loads, pieces, packed, count):
    _, hidden, width = loads.leave.shape
    rows = packed.shape[0]
    near = loads.pieces(0, count, "entry")
    return loads.call(
        functools.partial(entry_own_kernel, hidden),
        "entry_own",
        (packed, *near),
        [HERE] * (1 + len(near)),
        (shaped((count * hidden, rows)),),
        pieces,
        cost=(2 * rows * count * hidden * width // 4, count * hidden * width // 2, 0),
    )[0]


def entry_kernel(base, first, n, hidden, *refs):
    packs, routing, before = refs[:SIDE], refs[SIDE], refs[SIDE + 1]
    near, rest = refs[SIDE + 2 : SIDE + 2 + n], refs[SIDE + 2 + n :]
    rows, width = packs[0].shape
    width = width - 128
    me = lax.axis_index("ep")
    if first:
        out, turned = rest
        for k, packed in enumerate(packs):
            turned[k * width : (k + 1) * width, :] = packed[:, :width].T
    else:
        turned, out = rest
    squares = jnp.zeros((rows, 128), F32)
    for packed in packs:
        squares = squares + packed[:, width:].astype(F32)
    mean = jnp.sum(squares.T, axis=0, keepdims=True) / (SIDE * width)
    scale = lax.rsqrt(mean + 1e-06)
    table = routing[...].T
    ids = table[0:TOPK, :]
    weight = table[TOPK : 2 * TOPK, :] + table[2 * TOPK : 3 * TOPK, :]
    weight = weight + table[3 * TOPK : 4 * TOPK, :]
    count = EXPERTS // SIDE
    number = 0
    pair = []
    for array in near:
        for start in range(0, array.shape[0], hidden):
            chosen = ids == (me * count + base + number).astype(F32)
            share = jnp.sum(jnp.where(chosen, weight, 0.0), axis=0, keepdims=True)
            at = (base + number) * hidden
            begun = at < before.shape[0]
            total = before[at : at + hidden, :] if begun else 0.0
            for k in range(1 if begun else 0, SIDE):
                columns = pl.ds(pl.multiple_of((me ^ k) * width, width), width)
                total = total + jnp.dot(
                    array[start : start + hidden, columns],
                    turned[k * width : (k + 1) * width, :],
                    preferred_element_type=F32,
                )
            total = total * scale
            active = (total / (1.0 + jnp.exp(-total))).astype(BF16).astype(F32) * share
            high = active.astype(BF16).astype(F32)
            pair.append(jnp.concatenate([high, active - high], axis=1))
            number += 1
            if len(pair) == 2:
                end = number * hidden
                both = jnp.concatenate(pair, axis=0)
                out[:, end - 2 * hidden : end] = both.astype(BF16).T
                pair = []


def entries(loads, pieces, base, last, packs, routing, before, turned=None):
    _, hidden, width = loads.leave.shape
    count = last - base
    rows = packs[0].shape[0]
    near = loads.pieces(base, last, "entry")
    first = turned is None
    args = (*packs, routing, before, *near) + (() if first else (turned,))
    outs = (shaped((2 * rows, count * hidden), BF16),)
    if first:
        outs += (shaped((width, rows), BF16),)
    return loads.call(
        functools.partial(entry_kernel, base, first, len(near), hidden),
        f"entry{base}",
        args,
        [HERE] * len(args),
        outs,
        pieces,
        cost=(2 * rows * count * hidden * width, 2 * count * hidden * width, 0),
    )


def leave_kernel(other, n, m, step, *refs):
    scaled, near, out = refs[:m], refs[m : m + n], refs[m + n + 1]
    rows, half = out.shape
    chip = (lax.axis_index("hd") // 2) ^ other
    for c in range(0, half, step):
        total = jnp.zeros((2 * rows, step), F32)
        which, at = 0, 0
        for array in near:
            start = c if array.shape[1] == half else pl.multiple_of(chip * half + c, step)
            done = 0
            while done < array.shape[0]:
                depth = min(array.shape[0] - done, scaled[which].shape[1] - at)
                total = total + jnp.dot(
                    scaled[which][:, at : at + depth],
                    array[done : done + depth, pl.ds(start, step)],
                    preferred_element_type=F32,
                )
                done, at = done + depth, at + depth
                if at == scaled[which].shape[1]:
                    which, at = which + 1, 0
        out[:, c : c + step] = (total[:rows] + total[rows:]).astype(out.dtype)


def leaves(loads, pieces, name, other, dtype, scaled, unused):
    count, hidden, width = loads.leave.shape
    near = loads.pieces(0, count, "leave", "away" if other else "here")
    rows = scaled[0].shape[0] // 2
    return loads.call(
        functools.partial(leave_kernel, other, len(near), len(scaled), 1024),
        name,
        (*scaled, *near, unused),
        [HERE] * (len(scaled) + len(near)) + [ANYWHERE],
        (shaped((rows, width // 2), dtype),),
        pieces,
        cost=(2 * rows * count * hidden * width, count * hidden * width, 0),
        limit=6,
    )[0]


def halve_kernel(mine, received, keep, send):
    width = keep.shape[1]
    core = lax.axis_index("hd") % 2
    for out, which in ((send, 1 - core), (keep, core)):
        columns = pl.ds(pl.multiple_of(which * width, width), width)
        out[...] = mine[:, columns] + received[:, columns].astype(F32)


def halve(mine, received):
    rows, width = mine.shape
    outs = (shaped((rows, width // 2)),) * 2
    cost = (mine.size, mine.size * 6, 0)
    return kernel_call(halve_kernel, "halve", (mine, received), [HERE] * 2, outs, cost=cost)[0]


def share_kernel(own, received, stream, o0, o1, o2, o3):
    rows = o0.shape[0]
    me = lax.axis_index("ep")
    here = (me == lax.axis_index("hd")).astype(F32)
    for k, out in enumerate((o0, o1, o2, o3)):
        span = pl.ds(pl.multiple_of((me ^ k) * rows, rows), rows)
        out[...] = own[span, :] + received[span, :] + here * stream[span, :]


def share(own, received, stream):
    rows, width = own.shape
    outs = (shaped((rows // SIDE, width)),) * SIDE
    cost = (own.size * 3, own.size * 16, 0)
    args = (own, received, stream)
    return kernel_call(share_kernel, "share", args, [HERE] * 3, outs, cost=cost)[0]


PLAN = {
    "attention": [],
    "fetch0": [("entry", 0, 6)],
    "projection": [],
    "fetch1": [("entry", 6, 2), ("entry", 8, 5)],
    "own": [("leave", 0, 8)],
    "entry0": [("entry", 13, 3), ("leave", 8, 1)],
    "entry8": [("leave", 9, 2), ("away", 11, 5)],
    "leave1": [("here", 11, 5)],
}


def square_body(
    residual,
    queries,
    key_value_cache,
    lengths,
    slot_of,
    out_weight,
    expert_ids,
    route_weight,
    in_weight,
    down_weight,
):
    rows = queries.shape[0]
    cache = key_value_cache.reshape(rows, 2 * CACHE_LENGTH, HEAD_SIZE)
    loads = Loads(jnp.swapaxes(in_weight, 1, 2), down_weight)
    plan = PLAN
    attended, weight, order = attention(
        loads,
        plan["attention"],
        lengths,
        queries,
        cache,
        expert_ids,
        route_weight,
        residual,
        out_weight,
        slot_of,
    )
    blocks = [attended] + [swap(attended, "ep", k) for k in (1, 2, 3)]
    mark = fetch(loads, plan["fetch0"], "fetch0", attended)
    partial_value, routing = projection(loads, plan["projection"], order, blocks, weight, mark)
    pair = add(partial_value, swap(partial_value, "hd", 1))
    far_pair = swap(pair, "hd", 2)
    mark = fetch(loads, plan["fetch1"], "fetch1", pair)
    stream, packed = streams(pair, far_pair, mark)
    packs = [packed] + [swap(packed, "ep", k) for k in (1, 2, 3)]
    before = entry_own(loads, plan["own"], packed, 13)
    scaled, turned = entries(loads, plan["entry0"], 0, 8, packs, routing, before)
    (more,) = entries(loads, plan["entry8"], 8, 16, packs, routing, before, turned)
    scaled = (scaled, more)
    theirs = leaves(loads, plan["leave1"], "leave1", 1, BF16, scaled, more)
    mine = leaves(loads, (), "leave0", 0, F32, scaled, theirs)
    keep, send = halve(mine, swap(theirs, "hd", 2))
    total, *others = share(keep, swap(send, "hd", 1), stream)
    for k in (3, 2, 1):
        total = total + swap(others[k - 1], "ep", k)
    return total.astype(BF16)


def expert_pass(block, in_weight, down_weight):
    local_count = in_weight.shape[0]
    senders = block.shape[0] // local_count
    slots = block.shape[1]
    width = block.shape[2]
    grouped = block.reshape(senders, local_count, slots, width)
    hidden = jnp.einsum("secd,edf->secf", grouped, in_weight, preferred_element_type=jnp.float32)
    hidden = jax.nn.silu(hidden).astype(jnp.bfloat16)
    output = jnp.einsum("secf,efd->secd", hidden, down_weight, preferred_element_type=jnp.float32)
    return output.reshape(senders * local_count, slots, width)


def body(
    residual,
    queries,
    key_value_cache,
    lengths,
    slot_of,
    out_weight,
    expert_ids,
    route_weight,
    in_weight,
    down_weight,
):
    rows_here = queries.shape[0]
    local_groups = key_value_cache.shape[3] // HEAD_SIZE
    heads_per_group = QUERY_HEADS // KEY_VALUE_HEADS
    query_head_rows = queries.reshape(rows_here, local_groups, heads_per_group, HEAD_SIZE)
    cached_key_rows = key_value_cache[:, :, 0].reshape(
        rows_here, CACHE_LENGTH, local_groups, HEAD_SIZE
    )
    cached_value_rows = key_value_cache[:, :, 1].reshape(
        rows_here, CACHE_LENGTH, local_groups, HEAD_SIZE
    )
    scores = jnp.einsum(
        "sagd,slad->sagl", query_head_rows, cached_key_rows, preferred_element_type=jnp.float32
    )
    scores = scores * (1.0 / math.sqrt(HEAD_SIZE))
    visible = (jnp.arange(CACHE_LENGTH)[None, :] < lengths[:, None])[:, None, None, :]
    scores = jnp.where(visible, scores, -1e30)
    highest = jnp.max(scores, axis=3, keepdims=True)
    raised = jnp.where(visible, jnp.exp(scores - highest), 0.0)
    weights = (raised / jnp.sum(raised, axis=3, keepdims=True)).astype(jnp.bfloat16)
    attended = jnp.einsum(
        "sagl,slad->sagd", weights, cached_value_rows, preferred_element_type=jnp.float32
    )
    attended = attended.astype(jnp.bfloat16).reshape(
        rows_here, local_groups * heads_per_group * HEAD_SIZE
    )
    partial_value = jnp.dot(
        lax.all_gather(attended, "ep", axis=0, tiled=True),
        out_weight,
        preferred_element_type=jnp.float32,
    )
    ordered = jnp.take(partial_value, slot_of, axis=0)
    moved = lax.all_to_all(ordered, "ep", split_axis=0, concat_axis=1, tiled=True)
    summed = lax.psum_scatter(moved, "hd", scatter_dimension=1, tiled=True)
    stream = residual.astype(jnp.float32) + summed
    squares = lax.psum(jnp.sum(stream * stream, axis=1), "hd")
    normed = (stream * lax.rsqrt(squares / D + 1e-06)[:, None]).astype(jnp.bfloat16)
    picked = expert_ids.reshape(-1)
    member = (picked[:, None] == jnp.arange(EXPERTS)[None, :]).astype(jnp.int32)
    earlier = jnp.cumsum(member, axis=0) - member
    position = jnp.sum(earlier * member, axis=1)
    target = picked * CAP + position
    placed = (target[:, None] == jnp.arange(EXPERTS * CAP)[None, :]).astype(jnp.float32)
    owner = (jnp.arange(picked.shape[0])[:, None] // TOPK == jnp.arange(rows_here)[None, :]).astype(
        jnp.float32
    )
    select_matrix = jnp.dot(placed.T, owner, precision=lax.Precision.HIGHEST).astype(jnp.bfloat16)
    mixing = jnp.dot(
        owner.T, placed * route_weight.reshape(-1)[:, None], precision=lax.Precision.HIGHEST
    )
    full_rows = lax.all_gather(normed, "hd", axis=1, tiled=True)
    outgoing = jnp.dot(select_matrix, full_rows, preferred_element_type=jnp.float32).astype(
        jnp.bfloat16
    )
    outgoing = outgoing.reshape(EXPERTS, CAP, full_rows.shape[1])
    results = expert_pass(
        lax.all_to_all(outgoing, "ep", split_axis=0, concat_axis=0, tiled=True),
        in_weight,
        down_weight,
    )
    share_width = residual.shape[1]
    shares = lax.psum_scatter(results.astype(jnp.bfloat16), "hd", scatter_dimension=2, tiled=True)
    returned = lax.all_to_all(shares, "ep", split_axis=0, concat_axis=0, tiled=True)
    flat_back = returned.reshape(EXPERTS * CAP, share_width).astype(jnp.float32)
    mixture = jnp.dot(mixing, flat_back, precision=lax.Precision.HIGHEST)
    return (stream + mixture).astype(jnp.bfloat16)


def solution(mesh):
    in_specs = (
        P(("groups", "ep"), "hd"),
        P(("groups", "ep"), "hd"),
        P(("groups", "ep"), None, None, "hd"),
        P(("groups", "ep")),
        P("groups"),
        P("hd", "ep"),
        P(("groups", "ep"), None),
        P(("groups", "ep"), None),
        P("ep", None, "hd"),
        P("ep", "hd", None),
    )
    out_specs = P(("groups", "ep"), "hd")
    chosen = square_body if mesh.shape["ep"] == mesh.shape["hd"] == SIDE else body
    return jax.shard_map(chosen, mesh=mesh, in_specs=in_specs, out_specs=out_specs, check_vma=False)
```

```python
import functools
import math

import jax
import jax.numpy as jnp
from jax import lax
from jax.experimental import pallas as pl
from jax.experimental.pallas import tpu as pltpu
from jax.sharding import PartitionSpec as P

D = 4096
QUERY_HEADS = 64
KEY_VALUE_HEADS = 4
HEAD_SIZE = 128
EXPERTS = 64
TOPK = 8
CAP = 2
CACHE_LENGTH = 256
SIDE = 4
BF16 = jnp.bfloat16
F32 = jnp.float32
MIB = 1 << 20
HERE = pl.BlockSpec(memory_space=pltpu.VMEM)
SCALARS = pl.BlockSpec(memory_space=pltpu.SMEM)
ANYWHERE = pl.BlockSpec(memory_space=pl.ANY)
DMA = pltpu.SemaphoreType.DMA


def swap(block, axis, k):
    return lax.ppermute(block, axis, [(i, i ^ k) for i in range(SIDE)])


def far(array):
    return pltpu.with_memory_space_constraint(array, pltpu.HBM)


def split3(value):
    high = value.astype(BF16)
    rest = value - high.astype(F32)
    middle = rest.astype(BF16)
    low = (rest - middle.astype(F32)).astype(BF16)
    return high, middle, low


def hosted(body, inputs, outputs, loads):
    n = len(loads)

    def kernel(*refs):
        sources = refs[inputs : inputs + n]
        targets = refs[inputs + n + outputs : inputs + n + outputs + n]
        ins, outs = refs[:inputs], refs[inputs + n : inputs + n + outputs]
        copies = []
        for i, (load, source, target) in enumerate(zip(loads, sources, targets)):
            _, first, count, other = load
            depth, width = target.shape
            rows = pl.ds(first * (depth // count), depth)
            if other is None:
                source = source.at[rows]
            else:
                chip = (lax.axis_index("hd") // 2) ^ other
                source = source.at[rows, pl.ds(pl.multiple_of(chip * width, width), width)]
            copies.append(pltpu.make_async_copy(source, target, refs[-1].at[i]))
        begin = lambda: [copy.start() for copy in copies]
        rest = refs[inputs + outputs + 2 * n : -1]
        if body is attention_kernel:
            body(*ins, *outs, *rest, begin)
        else:
            begin()

            @pl.when(lax.axis_index("ep") >= 0)
            def _():
                body(*ins, *outs, *rest)

        for copy in copies:
            copy.wait()

    return kernel


def kernel_call(
    body, name, args, specs, outs, scratch=(), loads=(), limit=4, cost=(0, 0, 0), aliases=None
):
    targets = [
        pltpu.VMEM((count * array.shape[1], array.shape[2] // (1 if other is None else 2)), BF16)
        for array, _, count, other in loads
    ]
    flops, bytes_accessed, transcendentals = cost
    bytes_accessed += sum(2 * math.prod(target.shape) for target in targets)
    results = pl.pallas_call(
        hosted(body, len(args), len(outs), loads) if loads or body is attention_kernel else body,
        out_shape=(*outs, *targets),
        in_specs=[*specs] + [ANYWHERE] * len(loads),
        out_specs=(HERE,) * (len(outs) + len(targets)),
        scratch_shapes=[*scratch] + ([DMA((max(1, len(loads)),))] if loads or body is attention_kernel else []),
        input_output_aliases=aliases or {},
        compiler_params=pltpu.CompilerParams(vmem_limit_bytes=limit * MIB),
        cost_estimate=pl.CostEstimate(
            flops=flops, bytes_accessed=bytes_accessed, transcendentals=transcendentals
        ),
        name=name,
    )(*args, *(far(array.reshape(-1, array.shape[2])) for array, *_ in loads))
    return results[: len(outs)], results[len(outs) :]


class Loads:
    def __init__(self, entry, leave):
        self.entry, self.leave = entry, leave
        self.near = {"entry": [], "leave": [], "away": [], "here": []}

    def call(self, body, name, args, specs, outs, pieces=(), **more):
        half = {"away": 1, "here": 0}
        loads = tuple(
            (self.entry if what == "entry" else self.leave, first, count, half.get(what))
            for what, first, count in pieces
        )
        results, arrays = kernel_call(body, name, args, specs, outs, loads=loads, **more)
        for (what, first, count), array in zip(pieces, arrays):
            self.near[what].append((first, count, array))
        return results

    def pieces(self, first, last, *kinds):
        held = sum((self.near[what] for what in kinds), [])
        chosen = [p for p in held if first <= p[0] and p[0] + p[1] <= last]
        assert sum(p[1] for p in chosen) == last - first
        return tuple(p[2] for p in sorted(chosen, key=lambda p: p[0]))


def shaped(shape, dtype=F32):
    return jax.ShapeDtypeStruct(shape, dtype)


def attention_kernel(
    lengths_far,
    queries_far,
    cache_far,
    ids_far,
    route_far,
    residual_far,
    weight_far,
    slot_far,
    out,
    weight,
    order,
    lengths,
    queries,
    cache,
    ids,
    route,
    residual,
    slot_of,
    staged,
    gathered,
    sems,
    begin,
):
    pairs = (
        (lengths_far, lengths),
        (queries_far, queries),
        (cache_far, cache),
        (ids_far, ids),
        (route_far, route),
        (residual_far, residual),
        (slot_far, slot_of),
        (weight_far, weight),
    )
    copies = [pltpu.make_async_copy(*pair, sems.at[i]) for i, pair in enumerate(pairs)]
    for copy in copies:
        copy.start()
    begin()
    rows = queries.shape[0]
    heads = queries.shape[1] // HEAD_SIZE
    everyone = rows * heads
    copies[1].wait()
    for h in range(heads):
        lanes = slice(h * HEAD_SIZE, (h + 1) * HEAD_SIZE)
        staged[pl.ds(h, rows, stride=heads), :] = queries[:, lanes].astype(F32)
    turned = staged[...].T.astype(BF16)
    copies[0].wait()
    slot = lax.broadcasted_iota(jnp.int32, (1, everyone), 1) // heads
    limit = jnp.zeros((1, everyone), jnp.int32)
    for s in range(rows):
        limit = jnp.where(slot == s, 2 * lengths[s], limit)
    place = lax.broadcasted_iota(jnp.int32, (2 * CACHE_LENGTH, everyone), 0)
    visible = jnp.logical_and(place % 2 == 0, place < limit)
    width = heads * HEAD_SIZE
    copies[3].wait()
    copies[4].wait()
    row = lax.broadcasted_iota(jnp.int32, (TOPK, 128), 0)
    lane = lax.broadcasted_iota(jnp.int32, (TOPK, 128), 1)
    total = jnp.zeros((rows, 128), F32)
    for j, part in enumerate((ids[...].astype(F32).astype(BF16), *split3(route[...]))):
        spread = (lane == row + j * TOPK).astype(F32).astype(BF16)
        total = total + jnp.dot(part, spread, preferred_element_type=F32)
    out[:, width : width + 128] = total.astype(BF16)
    copies[5].wait()
    out[:, width + 128 :] = residual[...]
    copies[6].wait()
    me = lax.axis_index("ep")
    row = lax.broadcasted_iota(jnp.int32, order.shape, 0)
    wanted = jnp.zeros(order.shape, jnp.int32)
    for r in range(order.shape[0]):
        held = slot_of[r]
        wanted = jnp.where(row == r, ((held // rows) ^ me) * rows + held % rows, wanted)
    column = lax.broadcasted_iota(jnp.int32, order.shape, 1)
    order[...] = (wanted == column).astype(F32).astype(BF16)
    copies[2].wait()
    scores = jnp.dot(cache[0], turned, preferred_element_type=F32)
    for s in range(1, rows):
        more = jnp.dot(cache[s], turned, preferred_element_type=F32)
        scores = jnp.where(slot == s, more, scores)
    scores = jnp.where(visible, scores * (1.0 / math.sqrt(HEAD_SIZE)), -1e30)
    raised = jnp.where(visible, jnp.exp(scores - jnp.max(scores, axis=0, keepdims=True)), 0.0)
    weights = raised / jnp.sum(raised, axis=0, keepdims=True)
    moved = pltpu.roll(weights, 1, 0).T.astype(BF16)
    for s in range(rows):
        span = slice(s * heads, (s + 1) * heads)
        gathered[span, :] = jnp.dot(moved[span], cache[s], preferred_element_type=F32)
    for h in range(heads):
        lanes = slice(h * HEAD_SIZE, (h + 1) * HEAD_SIZE)
        out[:, lanes] = gathered[pl.ds(h, rows, stride=heads), :].astype(BF16)
    copies[7].wait()


def attention(loads, pieces, lengths, queries, cache, ids, route, residual, weight, slot_of):
    rows, width = queries.shape
    staged = pltpu.VMEM((rows * width // HEAD_SIZE, HEAD_SIZE), F32)
    return loads.call(
        attention_kernel,
        "attention",
        tuple(map(far, (lengths, queries, cache, ids, route, residual, weight, slot_of))),
        [ANYWHERE] * 8,
        (
            shaped((rows, width + 128 + residual.shape[1]), BF16),
            pltpu.VMEM(weight.shape, BF16),
            shaped((slot_of.shape[0], slot_of.shape[0]), BF16),
        ),
        pieces,
        scratch=[
            pltpu.SMEM(lengths.shape, jnp.int32),
            pltpu.VMEM(queries.shape, BF16),
            pltpu.VMEM(cache.shape, BF16),
            pltpu.VMEM(ids.shape, jnp.int32),
            pltpu.VMEM(route.shape, F32),
            pltpu.VMEM(residual.shape, BF16),
            pltpu.SMEM(slot_of.shape, jnp.int32),
            staged,
            staged,
            DMA((8,)),
        ],
        cost=(140_000_000, 12_000_000, 65536),
    )


def fetch_kernel(after, mark):
    del after
    mark[...] = jnp.zeros_like(mark)


def fetch(loads, pieces, name, after):
    return loads.call(
        fetch_kernel, name, (after,), [ANYWHERE], (shaped((8, 128)),), pieces, limit=1
    )[0]


def projection_kernel(order, b0, b1, b2, b3, weight, unused, out, routing, kept):
    del unused
    blocks = (b0, b1, b2, b3)
    rows = b0.shape[0]
    width = weight.shape[0]
    me = lax.axis_index("ep")
    for k, block in enumerate(blocks):
        span = pl.ds(pl.multiple_of((me ^ k) * rows, rows), rows)
        routing[span, :] = block[:, width : width + 128].astype(F32)
        kept[span, :] = block[:, width + 128 :].astype(F32)
    held = jnp.concatenate([b[:, :width].astype(F32) for b in blocks], axis=0).astype(BF16)
    ordered = jnp.dot(order[...], held, preferred_element_type=F32).astype(BF16)
    own = (me == lax.axis_index("hd")).astype(F32)
    out[...] = jnp.dot(ordered, weight[...], preferred_element_type=F32) + own * kept[...]


def projection(loads, pieces, order, blocks, weight, unused):
    everyone = SIDE * blocks[0].shape[0]
    wide = (everyone, weight.shape[1])
    return loads.call(
        projection_kernel,
        "projection",
        (order, *blocks, weight, unused),
        [HERE] * 6 + [ANYWHERE],
        (shaped(wide), shaped((everyone, 128))),
        pieces,
        scratch=[pltpu.VMEM(wide, F32)],
        limit=6,
        cost=(140_000_000, 4_500_000, 0),
    )


def add_kernel(a, b, out):
    out[...] = a[...] + b[...]


def add(a, b):
    outs = (shaped(a.shape),)
    return kernel_call(add_kernel, "add", (a, b), [HERE] * 2, outs, cost=(a.size, a.size, 0))[0][0]


def stream_kernel(a, b, unused, stream, packed):
    del unused
    total = a[...] + b[...]
    stream[...] = total
    width = total.shape[1]
    packed[:, :width] = total.astype(BF16)
    squares = jnp.sum(total * total, axis=1, keepdims=True)
    lane = lax.broadcasted_iota(jnp.int32, (total.shape[0], 128), 1)
    parts = [part.astype(F32) for part in split3(jnp.broadcast_to(squares, lane.shape))]
    spread = jnp.where(lane == 0, parts[0], jnp.where(lane == 1, parts[1], parts[2]))
    packed[:, width:] = jnp.where(lane < 3, spread, 0.0).astype(BF16)


def streams(a, b, unused):
    rows, width = a.shape
    outs = (shaped(a.shape), shaped((rows, width + 128), BF16))
    return kernel_call(
        stream_kernel,
        "stream",
        (a, b, unused),
        [HERE, HERE, ANYWHERE],
        outs,
        cost=(a.size * 4, a.size * 4, 0),
    )[0]


def entry_own_kernel(hidden, packed, *refs):
    near, out = refs[:-1], refs[-1]
    width = packed.shape[1] - 128
    start = pl.multiple_of(lax.axis_index("ep") * width, width)
    turned = packed[:, :width].T
    at = 0
    for array in near:
        for first in range(0, array.shape[0], hidden):
            out[at : at + hidden, :] = jnp.dot(
                array[first : first + hidden, pl.ds(start, width)],
                turned,
                preferred_element_type=F32,
            )
            at += hidden


def entry_own(loads, pieces, packed, count):
    _, hidden, width = loads.leave.shape
    rows = packed.shape[0]
    near = loads.pieces(0, count, "entry")
    return loads.call(
        functools.partial(entry_own_kernel, hidden),
        "entry_own",
        (packed, *near),
        [HERE] * (1 + len(near)),
        (shaped((count * hidden, rows)),),
        pieces,
        cost=(2 * rows * count * hidden * width // 4, count * hidden * width // 2, 0),
    )[0]


def entry_kernel(base, first, n, hidden, *refs):
    packs, routing, before = refs[:SIDE], refs[SIDE], refs[SIDE + 1]
    near, rest = refs[SIDE + 2 : SIDE + 2 + n], refs[SIDE + 2 + n :]
    rows, width = packs[0].shape
    width = width - 128
    me = lax.axis_index("ep")
    if first:
        out, turned = rest
        for k, packed in enumerate(packs):
            turned[k * width : (k + 1) * width, :] = packed[:, :width].T
    else:
        turned, out = rest
    squares = jnp.zeros((rows, 128), F32)
    for packed in packs:
        squares = squares + packed[:, width:].astype(F32)
    mean = jnp.sum(squares.T, axis=0, keepdims=True) / (SIDE * width)
    scale = lax.rsqrt(mean + 1e-06)
    table = routing[...].T
    ids = table[0:TOPK, :]
    weight = table[TOPK : 2 * TOPK, :] + table[2 * TOPK : 3 * TOPK, :]
    weight = weight + table[3 * TOPK : 4 * TOPK, :]
    count = EXPERTS // SIDE
    number = 0
    pair = []
    for array in near:
        for start in range(0, array.shape[0], hidden):
            chosen = ids == (me * count + base + number).astype(F32)
            share = jnp.sum(jnp.where(chosen, weight, 0.0), axis=0, keepdims=True)
            at = (base + number) * hidden
            begun = at < before.shape[0]
            total = before[at : at + hidden, :] if begun else 0.0
            for k in range(1 if begun else 0, SIDE):
                columns = pl.ds(pl.multiple_of((me ^ k) * width, width), width)
                total = total + jnp.dot(
                    array[start : start + hidden, columns],
                    turned[k * width : (k + 1) * width, :],
                    preferred_element_type=F32,
                )
            total = total * scale
            active = (total / (1.0 + jnp.exp(-total))).astype(BF16).astype(F32) * share
            high = active.astype(BF16).astype(F32)
            pair.append(jnp.concatenate([high, active - high], axis=1))
            number += 1
            if len(pair) == 2:
                end = number * hidden
                both = jnp.concatenate(pair, axis=0)
                out[:, end - 2 * hidden : end] = both.astype(BF16).T
                pair = []


def entries(loads, pieces, base, last, packs, routing, before, turned=None):
    _, hidden, width = loads.leave.shape
    count = last - base
    rows = packs[0].shape[0]
    near = loads.pieces(base, last, "entry")
    first = turned is None
    args = (*packs, routing, before, *near) + (() if first else (turned,))
    outs = (shaped((2 * rows, count * hidden), BF16),)
    if first:
        outs += (shaped((width, rows), BF16),)
    return loads.call(
        functools.partial(entry_kernel, base, first, len(near), hidden),
        f"entry{base}",
        args,
        [HERE] * len(args),
        outs,
        pieces,
        cost=(2 * rows * count * hidden * width, 2 * count * hidden * width, 0),
    )


def leave_kernel(other, n, m, step, *refs):
    scaled, near, out = refs[:m], refs[m : m + n], refs[m + n + 1]
    rows, half = out.shape
    chip = (lax.axis_index("hd") // 2) ^ other
    for c in range(0, half, step):
        total = jnp.zeros((2 * rows, step), F32)
        which, at = 0, 0
        for array in near:
            start = c if array.shape[1] == half else pl.multiple_of(chip * half + c, step)
            done = 0
            while done < array.shape[0]:
                depth = min(array.shape[0] - done, scaled[which].shape[1] - at)
                total = total + jnp.dot(
                    scaled[which][:, at : at + depth],
                    array[done : done + depth, pl.ds(start, step)],
                    preferred_element_type=F32,
                )
                done, at = done + depth, at + depth
                if at == scaled[which].shape[1]:
                    which, at = which + 1, 0
        out[:, c : c + step] = (total[:rows] + total[rows:]).astype(out.dtype)


def leaves(loads, pieces, name, other, dtype, scaled, unused):
    count, hidden, width = loads.leave.shape
    near = loads.pieces(0, count, "leave", "away" if other else "here")
    rows = scaled[0].shape[0] // 2
    return loads.call(
        functools.partial(leave_kernel, other, len(near), len(scaled), 1024),
        name,
        (*scaled, *near, unused),
        [HERE] * (len(scaled) + len(near)) + [ANYWHERE],
        (shaped((rows, width // 2), dtype),),
        pieces,
        cost=(2 * rows * count * hidden * width, count * hidden * width, 0),
        limit=6,
    )[0]


def halve_kernel(mine, received, keep, send):
    width = keep.shape[1]
    core = lax.axis_index("hd") % 2
    for out, which in ((send, 1 - core), (keep, core)):
        columns = pl.ds(pl.multiple_of(which * width, width), width)
        out[...] = mine[:, columns] + received[:, columns].astype(F32)


def halve(mine, received):
    rows, width = mine.shape
    outs = (shaped((rows, width // 2)),) * 2
    cost = (mine.size, mine.size * 6, 0)
    return kernel_call(halve_kernel, "halve", (mine, received), [HERE] * 2, outs, cost=cost)[0]


def share_kernel(own, received, stream, o0, o1, o2, o3):
    rows = o0.shape[0]
    me = lax.axis_index("ep")
    here = (me == lax.axis_index("hd")).astype(F32)
    for k, out in enumerate((o0, o1, o2, o3)):
        span = pl.ds(pl.multiple_of((me ^ k) * rows, rows), rows)
        out[...] = own[span, :] + received[span, :] + here * stream[span, :]


def share(own, received, stream):
    rows, width = own.shape
    outs = (shaped((rows // SIDE, width)),) * SIDE
    cost = (own.size * 3, own.size * 16, 0)
    args = (own, received, stream)
    return kernel_call(share_kernel, "share", args, [HERE] * 3, outs, cost=cost)[0]


PLAN = {
    "attention": [],
    "fetch0": [("entry", 0, 6)],
    "projection": [],
    "fetch1": [("entry", 6, 2), ("entry", 8, 5)],
    "own": [("leave", 0, 8)],
    "entry0": [("entry", 13, 3), ("leave", 8, 1)],
    "entry8": [("leave", 9, 3), ("away", 12, 4)],
    "leave1": [("here", 12, 4)],
}


def square_body(
    residual,
    queries,
    key_value_cache,
    lengths,
    slot_of,
    out_weight,
    expert_ids,
    route_weight,
    in_weight,
    down_weight,
):
    rows = queries.shape[0]
    cache = key_value_cache.reshape(rows, 2 * CACHE_LENGTH, HEAD_SIZE)
    loads = Loads(jnp.swapaxes(in_weight, 1, 2), down_weight)
    plan = PLAN
    attended, weight, order = attention(
        loads,
        plan["attention"],
        lengths,
        queries,
        cache,
        expert_ids,
        route_weight,
        residual,
        out_weight,
        slot_of,
    )
    blocks = [attended] + [swap(attended, "ep", k) for k in (1, 2, 3)]
    mark = fetch(loads, plan["fetch0"], "fetch0", attended)
    partial_value, routing = projection(loads, plan["projection"], order, blocks, weight, mark)
    pair = add(partial_value, swap(partial_value, "hd", 1))
    far_pair = swap(pair, "hd", 2)
    mark = fetch(loads, plan["fetch1"], "fetch1", pair)
    stream, packed = streams(pair, far_pair, mark)
    packs = [packed] + [swap(packed, "ep", k) for k in (1, 2, 3)]
    before = entry_own(loads, plan["own"], packed, 13)
    scaled, turned = entries(loads, plan["entry0"], 0, 8, packs, routing, before)
    (more,) = entries(loads, plan["entry8"], 8, 16, packs, routing, before, turned)
    scaled = (scaled, more)
    theirs = leaves(loads, plan["leave1"], "leave1", 1, BF16, scaled, more)
    mine = leaves(loads, (), "leave0", 0, F32, scaled, theirs)
    keep, send = halve(mine, swap(theirs, "hd", 2))
    total, *others = share(keep, swap(send, "hd", 1), stream)
    for k in (3, 2, 1):
        total = total + swap(others[k - 1], "ep", k)
    return total.astype(BF16)


def expert_pass(block, in_weight, down_weight):
    local_count = in_weight.shape[0]
    senders = block.shape[0] // local_count
    slots = block.shape[1]
    width = block.shape[2]
    grouped = block.reshape(senders, local_count, slots, width)
    hidden = jnp.einsum("secd,edf->secf", grouped, in_weight, preferred_element_type=jnp.float32)
    hidden = jax.nn.silu(hidden).astype(jnp.bfloat16)
    output = jnp.einsum("secf,efd->secd", hidden, down_weight, preferred_element_type=jnp.float32)
    return output.reshape(senders * local_count, slots, width)


def body(
    residual,
    queries,
    key_value_cache,
    lengths,
    slot_of,
    out_weight,
    expert_ids,
    route_weight,
    in_weight,
    down_weight,
):
    rows_here = queries.shape[0]
    local_groups = key_value_cache.shape[3] // HEAD_SIZE
    heads_per_group = QUERY_HEADS // KEY_VALUE_HEADS
    query_head_rows = queries.reshape(rows_here, local_groups, heads_per_group, HEAD_SIZE)
    cached_key_rows = key_value_cache[:, :, 0].reshape(
        rows_here, CACHE_LENGTH, local_groups, HEAD_SIZE
    )
    cached_value_rows = key_value_cache[:, :, 1].reshape(
        rows_here, CACHE_LENGTH, local_groups, HEAD_SIZE
    )
    scores = jnp.einsum(
        "sagd,slad->sagl", query_head_rows, cached_key_rows, preferred_element_type=jnp.float32
    )
    scores = scores * (1.0 / math.sqrt(HEAD_SIZE))
    visible = (jnp.arange(CACHE_LENGTH)[None, :] < lengths[:, None])[:, None, None, :]
    scores = jnp.where(visible, scores, -1e30)
    highest = jnp.max(scores, axis=3, keepdims=True)
    raised = jnp.where(visible, jnp.exp(scores - highest), 0.0)
    weights = (raised / jnp.sum(raised, axis=3, keepdims=True)).astype(jnp.bfloat16)
    attended = jnp.einsum(
        "sagl,slad->sagd", weights, cached_value_rows, preferred_element_type=jnp.float32
    )
    attended = attended.astype(jnp.bfloat16).reshape(
        rows_here, local_groups * heads_per_group * HEAD_SIZE
    )
    partial_value = jnp.dot(
        lax.all_gather(attended, "ep", axis=0, tiled=True),
        out_weight,
        preferred_element_type=jnp.float32,
    )
    ordered = jnp.take(partial_value, slot_of, axis=0)
    moved = lax.all_to_all(ordered, "ep", split_axis=0, concat_axis=1, tiled=True)
    summed = lax.psum_scatter(moved, "hd", scatter_dimension=1, tiled=True)
    stream = residual.astype(jnp.float32) + summed
    squares = lax.psum(jnp.sum(stream * stream, axis=1), "hd")
    normed = (stream * lax.rsqrt(squares / D + 1e-06)[:, None]).astype(jnp.bfloat16)
    picked = expert_ids.reshape(-1)
    member = (picked[:, None] == jnp.arange(EXPERTS)[None, :]).astype(jnp.int32)
    earlier = jnp.cumsum(member, axis=0) - member
    position = jnp.sum(earlier * member, axis=1)
    target = picked * CAP + position
    placed = (target[:, None] == jnp.arange(EXPERTS * CAP)[None, :]).astype(jnp.float32)
    owner = (jnp.arange(picked.shape[0])[:, None] // TOPK == jnp.arange(rows_here)[None, :]).astype(
        jnp.float32
    )
    select_matrix = jnp.dot(placed.T, owner, precision=lax.Precision.HIGHEST).astype(jnp.bfloat16)
    mixing = jnp.dot(
        owner.T, placed * route_weight.reshape(-1)[:, None], precision=lax.Precision.HIGHEST
    )
    full_rows = lax.all_gather(normed, "hd", axis=1, tiled=True)
    outgoing = jnp.dot(select_matrix, full_rows, preferred_element_type=jnp.float32).astype(
        jnp.bfloat16
    )
    outgoing = outgoing.reshape(EXPERTS, CAP, full_rows.shape[1])
    results = expert_pass(
        lax.all_to_all(outgoing, "ep", split_axis=0, concat_axis=0, tiled=True),
        in_weight,
        down_weight,
    )
    share_width = residual.shape[1]
    shares = lax.psum_scatter(results.astype(jnp.bfloat16), "hd", scatter_dimension=2, tiled=True)
    returned = lax.all_to_all(shares, "ep", split_axis=0, concat_axis=0, tiled=True)
    flat_back = returned.reshape(EXPERTS * CAP, share_width).astype(jnp.float32)
    mixture = jnp.dot(mixing, flat_back, precision=lax.Precision.HIGHEST)
    return (stream + mixture).astype(jnp.bfloat16)


def solution(mesh):
    in_specs = (
        P(("groups", "ep"), "hd"),
        P(("groups", "ep"), "hd"),
        P(("groups", "ep"), None, None, "hd"),
        P(("groups", "ep")),
        P("groups"),
        P("hd", "ep"),
        P(("groups", "ep"), None),
        P(("groups", "ep"), None),
        P("ep", None, "hd"),
        P("ep", "hd", None),
    )
    out_specs = P(("groups", "ep"), "hd")
    chosen = square_body if mesh.shape["ep"] == mesh.shape["hd"] == SIDE else body
    return jax.shard_map(chosen, mesh=mesh, in_specs=in_specs, out_specs=out_specs, check_vma=False)
```
